32 devices in a mesh: tok: 16 (over z, y, x), hid: 2 (over core).
Axes of the slice: x: 2, y: 2, z: 4, core: 2. Of those that a mesh axis runs over, the one named last changes fastest.
Arguments:
- acts: bfloat16 [8192, 14336], P('tok', 'hid'), may hold values from -6 to 6
- dictionary: float32 [14336, 256], P('hid'), may hold values from -0.046875 to 0.046875
- codes: float32 [8192, 256], P('tok'), may hold values from 0.02 to 1, as said below
Outputs:
- codes_out: float32 [8192, 256], P('tok')
- dict_out: float32 [14336, 256], P('hid')
The draws below stay inside these ranges and needn't reach their ends.
Inputs may be any that keep to these rules, and one draw needn't show every extreme that they name: `codes`: every starting code is positive.
All inputs are finite; a program needn't handle non-finite values.
Results may differ from the reference program's by a relative error of at most 0.0043.
Values sent between devices are 32-bit elements; how exact they have to be, the bound alone decides.
No kernel may reach another device: no remote copies, remote signals or barrier semaphores. Data moves between devices by JAX's collectives and lax.ppermute only.
A program may use at most 128 MiB of HBM per device.

```python
import math
import jax
import jax.numpy as jnp
from jax import lax

HID = 14336
COMP = 256
TOKENS = 8192


def draw_codes(key, part):
    key = jax.random.fold_in(key, 7)
    value_key = jax.random.fold_in(key, 1)
    row_key = jax.random.fold_in(key, 2)
    low_key = jax.random.fold_in(key, 3)
    spread_codes = jnp.exp(jax.random.uniform(value_key, (TOKENS, COMP), jnp.float32, math.log(0.02), 0.0))
    faint_codes = jnp.exp(jax.random.uniform(low_key, (TOKENS, COMP), jnp.float32, math.log(0.02), math.log(0.025)))
    picked = jax.random.randint(row_key, (TOKENS, 1), 0, 8) == 0
    return jnp.clip(jnp.where(picked, faint_codes, spread_codes), 0.02, 1.0)


def level_of(rng, dims, cuts, least, top_value):
    gain, own = 1.0, jax.random.fold_in(rng, 6)
    for dim, shards_of in cuts:
        draws = jnp.exp(jax.random.uniform(jax.random.fold_in(own, dim), (shards_of,), jnp.float32, least / len(cuts), top_value / len(cuts)))
        gain = gain * jnp.repeat(draws, dims[dim] // shards_of).reshape([-1 if axis == dim else 1 for axis in range(len(dims))])
    return gain


def noise(rng, extent, scale, limit, split=(), kind=jnp.bfloat16):
    gain = level_of(rng, extent, split, -0.22, 0.18) if split else 1.0
    values = jax.random.normal(rng, extent, jnp.float32) * scale * gain
    return jnp.minimum(jnp.maximum(values, -limit), limit).astype(kind)


def setup_inputs(seed: int = 0) -> dict:
    keys = jax.random.split(jax.random.key(seed), 4)
    return {
        "acts": noise(keys[0], (TOKENS, HID), 1.0, 6.0, ((0, 16), (1, 2))),
        "dictionary": noise(keys[1], (HID, COMP), HID ** -0.5, 0.046875, ((0, 2),), jnp.float32),
        "codes": draw_codes(jax.random.fold_in(keys[3], 71), 0),
    }


floor_value = 0.05

def refine(codes, proj, gram):
    gram_pos = jnp.maximum(gram, 0.0)
    gram_neg = jnp.maximum(-gram, 0.0)
    numer = jnp.maximum(proj, 0.0) + jnp.dot(codes, gram_neg, precision=lax.Precision.HIGHEST)
    denom = jnp.maximum(jnp.maximum(-proj, 0.0) + jnp.dot(codes, gram_pos, precision=lax.Precision.HIGHEST), floor_value)
    return codes * jnp.sqrt(numer / denom)

def solve_rows(cross, gram):
    lower = jnp.linalg.cholesky(gram)
    return jax.scipy.linalg.cho_solve((lower, True), cross.T).T

def reference(acts, dictionary, codes):
    dict_low = dictionary.astype(jnp.bfloat16)
    proj = jnp.dot(acts.astype(jnp.float32), dict_low.astype(jnp.float32), preferred_element_type=jnp.float32)
    gram_dict = jnp.dot(dictionary.T, dictionary, precision=lax.Precision.HIGHEST)
    codes_mid = refine(codes, proj, gram_dict)
    codes_low = codes_mid.astype(jnp.bfloat16)
    cross = jnp.dot(acts.T.astype(jnp.float32), codes_low.astype(jnp.float32), preferred_element_type=jnp.float32)
    gram_codes = jnp.dot(codes_low.T.astype(jnp.float32), codes_low.astype(jnp.float32), preferred_element_type=jnp.float32)
    dict_out = solve_rows(cross, gram_codes)
    gram_new = jnp.dot(dict_out.T, dict_out, precision=lax.Precision.HIGHEST)
    proj_two = jnp.dot(acts.astype(jnp.float32), dict_out.astype(jnp.bfloat16).astype(jnp.float32), preferred_element_type=jnp.float32)
    codes_out = refine(codes_mid, proj_two, gram_new)
    return (codes_out, dict_out)
```

```python
import functools

import jax
import jax.numpy as jnp
from jax import lax
from jax.experimental import pallas as pl
from jax.experimental.pallas import tpu as pltpu
from jax.sharding import PartitionSpec as P

floor_value = 0.05
HIGHEST = lax.Precision.HIGHEST
f32, bf16 = jnp.float32, jnp.bfloat16
BOTH = ("tok", "hid")
OVER_ROWS = (((0,), (0,)), ((), ()))
OVER_COLS = (((1,), (1,)), ((), ()))


def dot(left, right, dims=(((1,), (0,)), ((), ())), precision=None):
    return lax.dot_general(left, right, dims, precision=precision, preferred_element_type=f32)


def refine(codes, proj, gram):
    gram_pos = jnp.maximum(gram, 0.0)
    gram_neg = jnp.maximum(-gram, 0.0)
    numer = jnp.maximum(proj, 0.0) + dot(codes, gram_neg, precision=HIGHEST)
    denom = jnp.maximum(jnp.maximum(-proj, 0.0) + dot(codes, gram_pos, precision=HIGHEST), floor_value)
    return codes * jnp.sqrt(numer / denom)


def project_kernel(acts_ref, dict_ref, out_ref, cross_ref):
    step = pl.program_id(0)
    tokens = acts_ref.shape[0]

    @pl.when(step == 0)
    def _():
        out_ref[...] = jnp.zeros_like(out_ref)
        cross_ref[...] = jnp.zeros_like(cross_ref)

    rows = dict_ref[...]
    high = rows.astype(bf16)
    low = (rows - high.astype(f32)).astype(bf16)
    out_ref[:tokens, :] += dot(acts_ref[...], high)
    turned = high.T
    out_ref[tokens:, :] += dot(turned, high)
    cross_ref[...] += dot(turned, low)

    @pl.when(step == pl.num_programs(0) - 1)
    def _():
        out_ref[tokens:, :] += cross_ref[...] + cross_ref[...].T


def project(acts, dictionary):
    tokens, hidden = acts.shape
    comp = dictionary.shape[1]
    tile = 1024 if hidden % 1024 == 0 else 512
    return pl.pallas_call(
        project_kernel,
        out_shape=jax.ShapeDtypeStruct((tokens + comp, comp), f32),
        grid=(hidden // tile,),
        in_specs=[
            pl.BlockSpec((tokens, tile), lambda i: (0, i)),
            pl.BlockSpec((tile, comp), lambda i: (i, 0)),
        ],
        out_specs=pl.BlockSpec((tokens + comp, comp), lambda i: (0, 0)),
        scratch_shapes=[pltpu.VMEM((comp, comp), f32)],
        compiler_params=pltpu.CompilerParams(vmem_limit_bytes=48 * 2**20),
        cost_estimate=pl.CostEstimate(
            flops=2 * hidden * comp * (tokens + 2 * comp), bytes_accessed=hidden * (2 * tokens + 4 * comp), transcendentals=0
        ),
    )(acts, dictionary)


def unit_inverse(block):
    n = block.shape[0]
    done = []
    rest = block
    for start in range(0, n, 8):
        shape = rest.shape
        row = lax.broadcasted_iota(jnp.int32, shape, 0)
        lane = lax.broadcasted_iota(jnp.int32, shape, 1)
        lane_row = lax.broadcasted_iota(jnp.int32, (1, n), 1)
        cols = [jnp.broadcast_to(rest[:, start + j : start + j + 1], shape) for j in range(8)]
        for j in range(8):
            inverse = 1.0 / cols[j][j : j + 1, :]
            below = jnp.where(row > j, cols[j], 0.0)
            scaled = jnp.where(lane_row == start + j, inverse, rest[j : j + 1, :] * inverse)
            rest = jnp.where((lane == start + j) & (row > j), 0.0, rest) - below * scaled
            for k in range(j + 1, 8):
                cols[k] = cols[k] - below * (cols[k][j : j + 1, :] * inverse)
        done.append(rest[:8, :])
        rest = rest[8:, :]
    full = jnp.concatenate(done, axis=0)
    row = lax.broadcasted_iota(jnp.int32, (n, n), 0)
    lane = lax.broadcasted_iota(jnp.int32, (n, n), 1)
    pivots = jnp.sum(jnp.where(row == lane, full, 0.0), axis=1, keepdims=True)
    unit = jnp.where(row > lane, full, jnp.where(row == lane, 1.0, 0.0))
    return unit * (1.0 / jnp.sqrt(pivots))


def factor_kernel(gram_ref, out_ref):
    half = gram_ref.shape[0] // 2
    upper = unit_inverse(gram_ref[:half, :half])
    side = dot(gram_ref[half:, :half], upper, OVER_COLS, HIGHEST)
    lower = unit_inverse(gram_ref[half:, half:] - dot(side, side, OVER_COLS, HIGHEST))
    out_ref[:half, :half] = upper
    out_ref[:half, half:] = jnp.zeros((half, half), f32)
    out_ref[half:, :half] = -dot(dot(lower, side, precision=HIGHEST), upper, precision=HIGHEST)
    out_ref[half:, half:] = lower


def factor_inverse(gram):
    return pl.pallas_call(
        factor_kernel,
        out_shape=jax.ShapeDtypeStruct(gram.shape, f32),
        compiler_params=pltpu.CompilerParams(vmem_limit_bytes=48 * 2**20),
        cost_estimate=pl.CostEstimate(flops=10**10, bytes_accessed=8 * gram.size, transcendentals=0),
    )(gram)


def solve_rows(cross, inverse):
    return dot(dot(cross, inverse, OVER_COLS, HIGHEST), inverse, precision=HIGHEST)


def plain(acts, dictionary, codes, split):
    tokens = acts.shape[0]
    sums = lax.psum(project(acts, dictionary), "hid")
    codes_mid = refine(codes, sums[:tokens], sums[tokens:])
    codes_low = codes_mid.astype(bf16)
    cross = dot(acts, codes_low, OVER_ROWS)
    gram_codes = lax.psum(dot(codes_low, codes_low, OVER_ROWS), "tok")
    if split:
        mine = solve_rows(lax.psum_scatter(cross, "tok", tiled=True), factor_inverse(gram_codes))
        dict_out = lax.all_gather(mine, "tok", tiled=True)
    else:
        dict_out = solve_rows(lax.psum(cross, "tok"), factor_inverse(gram_codes))
    gram_part = dot(dict_out, dict_out, OVER_ROWS, HIGHEST)
    proj_two, gram_new = lax.psum((dot(acts, dict_out.astype(bf16)), gram_part), "hid")
    return refine(codes_mid, proj_two, gram_new), dict_out


DEPTH = 4


def device(z, y, x, c):
    return (z * 4 + y * 2 + x) * 2 + c


def every():
    return [(z, y, x, c) for z in range(DEPTH) for y in range(2) for x in range(2) for c in range(2)]


def flip(which):
    pairs = []
    for z, y, x, c in every():
        along_x = (c == 0) == (which == "first")
        pairs.append((device(z, y, x, c), device(z, y, 1 - x, c) if along_x else device(z, 1 - y, x, c)))
    return pairs


def along(sources, step):
    return [(device(z, y, x, c), device(z + step, y, x, c)) for z, y, x, c in every() if z in sources]


def send(value, pairs):
    return lax.ppermute(value, BOTH, pairs)


def line_sum(get, z):
    right = left = None
    for s in range(1, DEPTH):
        out_r = get(jnp.minimum(DEPTH - s + z, DEPTH - 1), right)
        out_l = get(jnp.maximum(s - DEPTH + z, 0), left)
        right = send(out_r, along(range(0, s), 1))
        left = send(out_l, along(range(DEPTH - s, DEPTH), -1))
    return get(z, right) + left


def line_gather(own, z):
    rights, lefts = [own], [own]
    for s in range(1, DEPTH):
        rights.append(send(rights[-1], along(range(s - 1, DEPTH - 1), 1)))
        lefts.append(send(lefts[-1], along(range(1, DEPTH - s + 1), -1)))
    return [own] + [rights[s] + lefts[DEPTH - s] for s in range(1, DEPTH)]


def place(blocks, total):
    out = jnp.zeros((total, blocks[0][0].shape[1]), f32)
    for value, row in blocks:
        out = lax.dynamic_update_slice_in_dim(out, value, row, 0)
    return out


def meshed(acts, dictionary, codes):
    tokens, hidden = acts.shape
    tok, core = lax.axis_index("tok"), lax.axis_index("hid")
    z, y, x = tok // 4, (tok // 2) % 2, tok % 2
    p = jnp.where(core == 0, x, y)
    q = jnp.where(core == 0, y, x)
    first, second = flip("first"), flip("second")
    swap = [(0, 1), (1, 0)]

    sums = project(acts, dictionary)
    sums = sums + lax.ppermute(sums, "hid", swap)
    codes_mid = refine(codes, sums[:tokens], sums[tokens:])
    codes_low = codes_mid.astype(bf16)
    gram_codes = lax.psum(dot(codes_low, codes_low, OVER_ROWS), "tok")
    inverse = factor_inverse(gram_codes)

    wide = (hidden * 11 // 14) // 512 * 512
    narrow = hidden - wide
    quarter, stripe = wide // 4, narrow // 4

    def cross_of(row, rows, add=None):
        out = dot(lax.dynamic_slice_in_dim(acts, row, rows, 1), codes_low, OVER_ROWS)
        return out if add is None else out + add

    def quarter_row(a, b):
        return a * (2 * quarter) + b * quarter

    got_1 = send(cross_of(quarter_row(1 - p, 1 - q), quarter), first)
    narrow_mine = line_sum(lambda j, add: cross_of(wide + j * stripe, stripe, add), z)
    got_2 = send(cross_of(quarter_row(1 - p, q), quarter), first)
    got_3 = send(cross_of(quarter_row(p, 1 - q), quarter, got_1), second)
    wide_mine = cross_of(quarter_row(p, q), quarter, got_2) + got_3

    def half_of(value, which):
        rows = value.shape[0] // 2
        return lax.dynamic_slice_in_dim(value, which * rows, rows, 0)

    narrow_mine = half_of(narrow_mine, p) + send(half_of(narrow_mine, 1 - p), first)
    narrow_mine = half_of(narrow_mine, q) + send(half_of(narrow_mine, 1 - q), second)

    piece = quarter // DEPTH

    def wide_block(j, add):
        value = lax.dynamic_slice_in_dim(wide_mine, j * piece, piece, 0)
        return value if add is None else value + add

    wide_mine = line_sum(wide_block, z)

    narrow_mine = solve_rows(narrow_mine, inverse)
    wide_mine = solve_rows(wide_mine, inverse)
    gram_part = dot(narrow_mine, narrow_mine, OVER_ROWS, HIGHEST) + dot(wide_mine, wide_mine, OVER_ROWS, HIGHEST)
    gram_new = lax.psum(gram_part, BOTH)

    small = narrow // 16
    narrow_mine = place([(narrow_mine, q * small), (send(narrow_mine, second), (1 - q) * small)], 2 * small)
    narrow_mine = place([(narrow_mine, p * 2 * small), (send(narrow_mine, first), (1 - p) * 2 * small)], 4 * small)
    wide_all = line_gather(wide_mine, z)
    own = place([(value, (z - s) % DEPTH * piece) for s, value in enumerate(wide_all)], quarter)
    narrow_all = line_gather(narrow_mine, z)
    from_second = send(own, second)
    from_first = send(own, first)
    from_far = send(from_second, first)

    blocks = [(value, wide + (z - s) % DEPTH * stripe) for s, value in enumerate(narrow_all)]
    blocks += [
        (own, quarter_row(p, q)),
        (from_second, quarter_row(p, 1 - q)),
        (from_first, quarter_row(1 - p, q)),
        (from_far, quarter_row(1 - p, 1 - q)),
    ]
    dict_out = place(blocks, hidden)
    proj_two = None
    for value, row in blocks:
        part = dot(lax.dynamic_slice_in_dim(acts, row, value.shape[0], 1), value.astype(bf16))
        proj_two = part if proj_two is None else proj_two + part
    proj_two = proj_two + lax.ppermute(proj_two, "hid", swap)
    return refine(codes_mid, proj_two, gram_new), dict_out


def solution(mesh):
    tok, hid = mesh.shape["tok"], mesh.shape["hid"]

    def per_device(acts, dictionary, codes):
        if tok == 16 and hid == 2 and acts.shape[1] % 512 == 0:
            return meshed(acts, dictionary, codes)
        return plain(acts, dictionary, codes, acts.shape[1] % tok == 0)

    return jax.shard_map(
        per_device,
        mesh=mesh,
        in_specs=(P("tok", "hid"), P("hid", None), P("tok", None)),
        out_specs=(P("tok", None), P("hid", None)),
        check_vma=False,
    )
```

```python
import functools

import jax
import jax.numpy as jnp
from jax import lax
from jax.experimental import pallas as pl
from jax.experimental.pallas import tpu as pltpu
from jax.sharding import PartitionSpec as P

floor_value = 0.05
HIGHEST = lax.Precision.HIGHEST
f32, bf16 = jnp.float32, jnp.bfloat16
BOTH = ("tok", "hid")
OVER_ROWS = (((0,), (0,)), ((), ()))
OVER_COLS = (((1,), (1,)), ((), ()))


def dot(left, right, dims=(((1,), (0,)), ((), ())), precision=None):
    return lax.dot_general(left, right, dims, precision=precision, preferred_element_type=f32)


def refine(codes, proj, gram):
    gram_pos = jnp.maximum(gram, 0.0)
    gram_neg = jnp.maximum(-gram, 0.0)
    numer = jnp.maximum(proj, 0.0) + dot(codes, gram_neg, precision=HIGHEST)
    denom = jnp.maximum(jnp.maximum(-proj, 0.0) + dot(codes, gram_pos, precision=HIGHEST), floor_value)
    return codes * jnp.sqrt(numer / denom)


def project_kernel(acts_ref, dict_ref, out_ref, cross_ref):
    step = pl.program_id(0)
    tokens = acts_ref.shape[0]

    @pl.when(step == 0)
    def _():
        out_ref[...] = jnp.zeros_like(out_ref)
        cross_ref[...] = jnp.zeros_like(cross_ref)

    rows = dict_ref[...]
    high = rows.astype(bf16)
    low = (rows - high.astype(f32)).astype(bf16)
    out_ref[:tokens, :] += dot(acts_ref[...], high)
    turned = high.T
    out_ref[tokens:, :] += dot(turned, high)
    cross_ref[...] += dot(turned, low)

    @pl.when(step == pl.num_programs(0) - 1)
    def _():
        out_ref[tokens:, :] += cross_ref[...] + cross_ref[...].T


def project(acts, dictionary):
    tokens, hidden = acts.shape
    comp = dictionary.shape[1]
    tile = 1024 if hidden % 1024 == 0 else 512
    return pl.pallas_call(
        project_kernel,
        out_shape=jax.ShapeDtypeStruct((tokens + comp, comp), f32),
        grid=(hidden // tile,),
        in_specs=[
            pl.BlockSpec((tokens, tile), lambda i: (0, i)),
            pl.BlockSpec((tile, comp), lambda i: (i, 0)),
        ],
        out_specs=pl.BlockSpec((tokens + comp, comp), lambda i: (0, 0)),
        scratch_shapes=[pltpu.VMEM((comp, comp), f32)],
        compiler_params=pltpu.CompilerParams(vmem_limit_bytes=48 * 2**20),
        cost_estimate=pl.CostEstimate(
            flops=2 * hidden * comp * (tokens + 2 * comp), bytes_accessed=hidden * (2 * tokens + 4 * comp), transcendentals=0
        ),
    )(acts, dictionary)


def unit_inverse(block):
    n = block.shape[0]
    done = []
    rest = block
    for start in range(0, n, 8):
        shape = rest.shape
        row = lax.broadcasted_iota(jnp.int32, shape, 0)
        lane = lax.broadcasted_iota(jnp.int32, shape, 1)
        lane_row = lax.broadcasted_iota(jnp.int32, (1, n), 1)
        cols = [jnp.broadcast_to(rest[:, start + j : start + j + 1], shape) for j in range(8)]
        for j in range(8):
            inverse = 1.0 / cols[j][j : j + 1, :]
            below = jnp.where(row > j, cols[j], 0.0)
            scaled = jnp.where(lane_row == start + j, inverse, rest[j : j + 1, :] * inverse)
            rest = jnp.where((lane == start + j) & (row > j), 0.0, rest) - below * scaled
            for k in range(j + 1, 8):
                cols[k] = cols[k] - below * (cols[k][j : j + 1, :] * inverse)
        done.append(rest[:8, :])
        rest = rest[8:, :]
    full = jnp.concatenate(done, axis=0)
    row = lax.broadcasted_iota(jnp.int32, (n, n), 0)
    lane = lax.broadcasted_iota(jnp.int32, (n, n), 1)
    pivots = jnp.sum(jnp.where(row == lane, full, 0.0), axis=1, keepdims=True)
    unit = jnp.where(row > lane, full, jnp.where(row == lane, 1.0, 0.0))
    return unit * (1.0 / jnp.sqrt(pivots))


def factor_kernel(gram_ref, out_ref):
    half = gram_ref.shape[0] // 2
    upper = unit_inverse(gram_ref[:half, :half])
    side = dot(gram_ref[half:, :half], upper, OVER_COLS, HIGHEST)
    lower = unit_inverse(gram_ref[half:, half:] - dot(side, side, OVER_COLS, HIGHEST))
    out_ref[:half, :half] = upper
    out_ref[:half, half:] = jnp.zeros((half, half), f32)
    out_ref[half:, :half] = -dot(dot(lower, side, precision=HIGHEST), upper, precision=HIGHEST)
    out_ref[half:, half:] = lower


def factor_inverse(gram):
    return pl.pallas_call(
        factor_kernel,
        out_shape=jax.ShapeDtypeStruct(gram.shape, f32),
        compiler_params=pltpu.CompilerParams(vmem_limit_bytes=48 * 2**20),
        cost_estimate=pl.CostEstimate(flops=10**10, bytes_accessed=8 * gram.size, transcendentals=0),
    )(gram)


def solve_rows(cross, inverse):
    return dot(dot(cross, inverse, OVER_COLS, HIGHEST), inverse, precision=HIGHEST)


def plain(acts, dictionary, codes, split):
    tokens = acts.shape[0]
    sums = lax.psum(project(acts, dictionary), "hid")
    codes_mid = refine(codes, sums[:tokens], sums[tokens:])
    codes_low = codes_mid.astype(bf16)
    cross = dot(acts, codes_low, OVER_ROWS)
    gram_codes = lax.psum(dot(codes_low, codes_low, OVER_ROWS), "tok")
    if split:
        mine = solve_rows(lax.psum_scatter(cross, "tok", tiled=True), factor_inverse(gram_codes))
        dict_out = lax.all_gather(mine, "tok", tiled=True)
    else:
        dict_out = solve_rows(lax.psum(cross, "tok"), factor_inverse(gram_codes))
    gram_part = dot(dict_out, dict_out, OVER_ROWS, HIGHEST)
    proj_two, gram_new = lax.psum((dot(acts, dict_out.astype(bf16)), gram_part), "hid")
    return refine(codes_mid, proj_two, gram_new), dict_out


def update(codes, sums, tokens, precision=HIGHEST):
    proj, gram = sums[:tokens], sums[tokens:]
    numer = jnp.maximum(proj, 0.0) + dot(codes, jnp.maximum(-gram, 0.0), precision=precision)
    denom = jnp.maximum(-proj, 0.0) + dot(codes, jnp.maximum(gram, 0.0), precision=precision)
    return codes * jnp.sqrt(numer / jnp.maximum(denom, floor_value))


def first_kernel(core_ref, codes_ref, mine_ref, theirs_ref, mid_ref, low_ref, gram_ref):
    mid = update(codes_ref[...], mine_ref[...] + theirs_ref[...], codes_ref.shape[0])
    low = mid.astype(bf16)
    mid_ref[...] = mid
    low_ref[...] = low
    half = low.shape[1] // 2
    side = jnp.where(core_ref[0] == 0, mid[:, :half], mid[:, half:]).astype(bf16)
    gram_ref[...] = dot(side.T, low)


def first_update(core, codes, mine, theirs):
    tokens, comp = codes.shape
    whole = pl.BlockSpec(memory_space=pltpu.VMEM)
    return pl.pallas_call(
        first_kernel,
        out_shape=[
            jax.ShapeDtypeStruct((tokens, comp), f32),
            jax.ShapeDtypeStruct((tokens, comp), bf16),
            jax.ShapeDtypeStruct((comp // 2, comp), f32),
        ],
        in_specs=[pl.BlockSpec(memory_space=pltpu.SMEM), whole, whole, whole],
        out_specs=[whole, whole, whole],
        compiler_params=pltpu.CompilerParams(vmem_limit_bytes=48 * 2**20),
    )(core, codes, mine, theirs)


def second_kernel(codes_ref, mine_ref, theirs_ref, out_ref):
    out_ref[...] = update(codes_ref[...], mine_ref[...] + theirs_ref[...], codes_ref.shape[0])


def second_update(codes, mine, theirs):
    return pl.pallas_call(
        second_kernel,
        out_shape=jax.ShapeDtypeStruct(codes.shape, f32),
        compiler_params=pltpu.CompilerParams(vmem_limit_bytes=48 * 2**20),
    )(codes, mine, theirs)


def rows_kernel(mine_ref, theirs_ref, inverse_ref, out_ref):
    inverse = inverse_ref[...]
    out_ref[...] = dot(dot(mine_ref[...] + theirs_ref[...], inverse, OVER_COLS, HIGHEST), inverse, precision=HIGHEST)


def solve_sum(mine, theirs, inverse):
    return pl.pallas_call(
        rows_kernel,
        out_shape=jax.ShapeDtypeStruct(mine.shape, f32),
        compiler_params=pltpu.CompilerParams(vmem_limit_bytes=48 * 2**20),
    )(mine, theirs, inverse)


def absorb_kernel(count, fresh, *refs):
    row_ref, acts_ref = refs[:2]
    values = refs[2 : 2 + count]
    refs = refs[2 + count :]
    if not fresh:
        sums_ref, refs = refs[0], refs[2:]
    out_ref, dict_ref = refs[:2]
    buffers, in_sem, out_sem = refs[2 : 2 + count], refs[2 + count], refs[3 + count]
    tokens = acts_ref.shape[0]
    ins, outs = [], []
    for k, value in enumerate(values):
        row = pl.multiple_of(row_ref[k], 128)
        rows = value.shape[0]
        ins.append(pltpu.make_async_copy(acts_ref.at[:, pl.ds(row, rows)], buffers[k], in_sem.at[k]))
        outs.append(pltpu.make_async_copy(value, dict_ref.at[pl.ds(row, rows), :], out_sem.at[k]))
        ins[k].start()
        outs[k].start()
    proj, gram = (0.0, 0.0) if fresh else (sums_ref[:tokens, :], sums_ref[tokens:, :])
    for k, value in enumerate(values):
        block = value[...]
        high = block.astype(bf16)
        low = (block - high.astype(f32)).astype(bf16)
        turned = high.T
        cross = dot(turned, low)
        gram = gram + (dot(turned, high) + (cross + cross.T))
        ins[k].wait()
        proj = proj + dot(buffers[k][...], high)
    out_ref[:tokens, :] = proj
    out_ref[tokens:, :] = gram
    for copy in outs:
        copy.wait()


def absorb(state, acts, blocks):
    tokens, hidden = acts.shape
    comp = blocks[0][0].shape[1]
    count = len(blocks)
    values = [value for value, _ in blocks]
    rows = jnp.stack([row for _, row in blocks]).astype(jnp.int32)
    whole, anywhere = pl.BlockSpec(memory_space=pltpu.VMEM), pl.BlockSpec(memory_space=pl.ANY)
    held = [] if state is None else list(state)
    total = sum(value.shape[0] for value in values)
    return pl.pallas_call(
        functools.partial(absorb_kernel, count, state is None),
        out_shape=[jax.ShapeDtypeStruct((tokens + comp, comp), f32), jax.ShapeDtypeStruct((hidden, comp), f32)],
        in_specs=[pl.BlockSpec(memory_space=pltpu.SMEM), anywhere] + [whole] * count + ([whole, anywhere] if held else []),
        out_specs=[whole, anywhere],
        scratch_shapes=[pltpu.VMEM((tokens, value.shape[0]), bf16) for value in values]
        + [pltpu.SemaphoreType.DMA((count,)), pltpu.SemaphoreType.DMA((count,))],
        input_output_aliases={2 + count: 0, 3 + count: 1} if held else {},
        compiler_params=pltpu.CompilerParams(vmem_limit_bytes=48 * 2**20),
        cost_estimate=pl.CostEstimate(
            flops=2 * total * comp * (tokens + 2 * comp), bytes_accessed=total * (2 * tokens + 8 * comp), transcendentals=0
        ),
    )(rows, acts, *values, *held)


def flips(bits):
    return [(t * 2 + c, (t ^ bits[c]) * 2 + c) for t in range(16) for c in range(2)]


X, Y, ZL, ZH = 1, 2, 4, 8
ALONG = {"first": (X, Y), "second": (Y, X), "near": (ZL, ZL), "far": (ZH, ZH), "x": (X, X), "y": (Y, Y)}


def swap(value, along):
    return lax.ppermute(value, BOTH, flips(ALONG[along]))


def meshed(acts, dictionary, codes):
    tokens, hidden = acts.shape
    tok, core = lax.axis_index("tok"), lax.axis_index("hid")

    def other_core(value):
        return lax.ppermute(value, "hid", [(0, 1), (1, 0)])

    def bit(along):
        on_0, on_1 = ALONG[along]
        return jnp.where(core == 0, tok & on_0, tok & on_1) // jnp.where(core == 0, on_0, on_1)

    sums = project(acts, dictionary)
    codes_mid, codes_low, gram = first_update(jnp.reshape(core, (1,)).astype(jnp.int32), codes, sums, other_core(sums))
    for along in ("x", "y", "near", "far"):
        gram = gram + swap(gram, along)
    other = other_core(gram)
    inverse = factor_inverse(jnp.where(core == 0, jnp.concatenate([gram, other]), jnp.concatenate([other, gram])))

    def cross_of(row, rows):
        return dot(lax.dynamic_slice_in_dim(acts, row, rows, 1), codes_low, OVER_ROWS)

    def part_of(value, which, parts=2):
        rows = value.shape[0] // parts
        return lax.dynamic_slice_in_dim(value, which * rows, rows, 0)

    def joined(mine, theirs, which):
        return jnp.where(which == 0, jnp.concatenate([mine, theirs]), jnp.concatenate([theirs, mine]))

    unit = hidden // 7
    parts = [
        (0, 3 * unit, ("first", "second", "near", "far")),
        (3 * unit, 2 * unit, ("first", "second", "near", "far")),
        (5 * unit, 2 * unit, ("near", "first", "second", "far")),
    ]

    solved = []
    for start, rows, order in parts:
        a, b, c, d = (bit(along) for along in order)
        quarter = rows // 4
        got = swap(cross_of(start + (1 - a) * 2 * quarter, 2 * quarter), order[0])
        out = cross_of(start + a * 2 * quarter + (1 - b) * quarter, quarter) + part_of(got, 1 - b)
        held = cross_of(start + a * 2 * quarter + b * quarter, quarter) + part_of(got, b)
        held = held + swap(out, order[1])
        held = part_of(held, c) + swap(part_of(held, 1 - c), order[2])
        solved.append(solve_sum(part_of(held, d), swap(part_of(held, 1 - d), order[3]), inverse))

    state = None
    for (start, rows, order), mine in zip(parts, solved):
        a, b, c, d = (bit(along) for along in order)
        quarter = rows // 4
        mine = joined(mine, swap(mine, order[3]), d)
        mine = joined(mine, swap(mine, order[2]), c)
        theirs = swap(mine, order[1])
        here, there = start + a * 2 * quarter, start + (1 - a) * 2 * quarter
        state = absorb(state, acts, [(mine, here + b * quarter), (theirs, here + (1 - b) * quarter)])
        far = [(swap(mine, order[0]), there + b * quarter), (swap(theirs, order[0]), there + (1 - b) * quarter)]
        state = absorb(state, acts, far)
    sums, dict_out = state
    return second_update(codes_mid, sums, other_core(sums)), dict_out


def solution(mesh):
    tok, hid = mesh.shape["tok"], mesh.shape["hid"]

    def per_device(acts, dictionary, codes):
        if tok == 16 and hid == 2 and acts.shape[1] % (7 * 1024) == 0:
            return meshed(acts, dictionary, codes)
        return plain(acts, dictionary, codes, acts.shape[1] % tok == 0)

    return jax.shard_map(
        per_device,
        mesh=mesh,
        in_specs=(P("tok", "hid"), P("hid", None), P("tok", None)),
        out_specs=(P("tok", None), P("hid", None)),
        check_vma=False,
    )
```

```python
import functools

import jax
import jax.numpy as jnp
import numpy as np
from jax import lax
from jax.experimental import pallas as pl
from jax.experimental.pallas import tpu as pltpu
from jax.sharding import PartitionSpec as P

floor_value = 0.05
HIGHEST = lax.Precision.HIGHEST
f32, bf16 = jnp.float32, jnp.bfloat16
BOTH = ("tok", "hid")
OVER_ROWS = (((0,), (0,)), ((), ()))
OVER_COLS = (((1,), (1,)), ((), ()))
LIMIT = pltpu.CompilerParams(vmem_limit_bytes=48 * 2**20)


def dot(left, right, dims=(((1,), (0,)), ((), ())), precision=None):
    return lax.dot_general(left, right, dims, precision=precision, preferred_element_type=f32)


def refine(codes, proj, gram):
    gram_pos = jnp.maximum(gram, 0.0)
    gram_neg = jnp.maximum(-gram, 0.0)
    numer = jnp.maximum(proj, 0.0) + dot(codes, gram_neg, precision=HIGHEST)
    denom = jnp.maximum(jnp.maximum(-proj, 0.0) + dot(codes, gram_pos, precision=HIGHEST), floor_value)
    return codes * jnp.sqrt(numer / denom)


def project_kernel(acts_ref, dict_ref, out_ref, cross_ref):
    step = pl.program_id(0)
    tokens = acts_ref.shape[0]

    @pl.when(step == 0)
    def _():
        out_ref[...] = jnp.zeros_like(out_ref)
        cross_ref[...] = jnp.zeros_like(cross_ref)

    rows = dict_ref[...]
    high = rows.astype(bf16)
    low = (rows - high.astype(f32)).astype(bf16)
    out_ref[:tokens, :] += dot(acts_ref[...], high)
    turned = high.T
    out_ref[tokens:, :] += dot(turned, high)
    cross_ref[...] += dot(turned, low)

    @pl.when(step == pl.num_programs(0) - 1)
    def _():
        out_ref[tokens:, :] += cross_ref[...] + cross_ref[...].T


def project(acts, dictionary):
    tokens, hidden = acts.shape
    comp = dictionary.shape[1]
    tile = 1024 if hidden % 1024 == 0 else 512
    return pl.pallas_call(
        project_kernel,
        out_shape=jax.ShapeDtypeStruct((tokens + comp, comp), f32),
        grid=(hidden // tile,),
        in_specs=[
            pl.BlockSpec((tokens, tile), lambda i: (0, i)),
            pl.BlockSpec((tile, comp), lambda i: (i, 0)),
        ],
        out_specs=pl.BlockSpec((tokens + comp, comp), lambda i: (0, 0)),
        scratch_shapes=[pltpu.VMEM((comp, comp), f32)],
        compiler_params=LIMIT,
        cost_estimate=pl.CostEstimate(
            flops=2 * hidden * comp * (tokens + 2 * comp), bytes_accessed=hidden * (2 * tokens + 4 * comp), transcendentals=0
        ),
    )(acts, dictionary)


def unit_inverse(block):
    n = block.shape[0]
    done = []
    rest = block
    for start in range(0, n, 8):
        shape = rest.shape
        row = lax.broadcasted_iota(jnp.int32, shape, 0)
        lane = lax.broadcasted_iota(jnp.int32, shape, 1)
        lane_row = lax.broadcasted_iota(jnp.int32, (1, n), 1)
        cols = [jnp.broadcast_to(rest[:, start + j : start + j + 1], shape) for j in range(8)]
        for j in range(8):
            inverse = 1.0 / cols[j][j : j + 1, :]
            below = jnp.where(row > j, cols[j], 0.0)
            scaled = jnp.where(lane_row == start + j, inverse, rest[j : j + 1, :] * inverse)
            rest = jnp.where((lane == start + j) & (row > j), 0.0, rest) - below * scaled
            for k in range(j + 1, 8):
                cols[k] = cols[k] - below * (cols[k][j : j + 1, :] * inverse)
        done.append(rest[:8, :])
        rest = rest[8:, :]
    full = jnp.concatenate(done, axis=0)
    row = lax.broadcasted_iota(jnp.int32, (n, n), 0)
    lane = lax.broadcasted_iota(jnp.int32, (n, n), 1)
    pivots = jnp.sum(jnp.where(row == lane, full, 0.0), axis=1, keepdims=True)
    unit = jnp.where(row > lane, full, jnp.where(row == lane, 1.0, 0.0))
    return unit * (1.0 / jnp.sqrt(pivots))


def factor(gram_ref, out_ref):
    half = gram_ref.shape[0] // 2
    upper = unit_inverse(gram_ref[:half, :half])
    side = dot(gram_ref[half:, :half], upper, OVER_COLS, HIGHEST)
    lower = unit_inverse(gram_ref[half:, half:] - dot(side, side, OVER_COLS, HIGHEST))
    out_ref[:half, :half] = upper
    out_ref[:half, half:] = jnp.zeros((half, half), f32)
    out_ref[half:, :half] = -dot(dot(lower, side, precision=HIGHEST), upper, precision=HIGHEST)
    out_ref[half:, half:] = lower


def halves_kernel(table_ref, mine_ref, theirs_ref, *refs):
    half = mine_ref.shape[0]
    out_ref, gram_ref = refs[-2:]
    gram_ref[pl.ds(pl.multiple_of(table_ref[0] * half, half), half), :] = mine_ref[...]
    gram_ref[pl.ds(pl.multiple_of((1 - table_ref[0]) * half, half), half), :] = theirs_ref[...]
    factor(gram_ref, out_ref)


def factor_inverse(table, mine, theirs, after=()):
    comp = mine.shape[1]
    return pl.pallas_call(
        halves_kernel,
        out_shape=jax.ShapeDtypeStruct((comp, comp), f32),
        in_specs=[pl.BlockSpec(memory_space=pltpu.SMEM)]
        + [pl.BlockSpec(memory_space=pltpu.VMEM)] * 2
        + [pl.BlockSpec(memory_space=pl.ANY)] * len(after),
        scratch_shapes=[pltpu.VMEM((comp, comp), f32)],
        compiler_params=LIMIT,
        cost_estimate=pl.CostEstimate(flops=10**10, bytes_accessed=8 * comp * comp, transcendentals=0),
    )(table, mine, theirs, *after)


def solve_rows(cross, inverse):
    return dot(dot(cross, inverse, OVER_COLS, HIGHEST), inverse, precision=HIGHEST)


def plain(acts, dictionary, codes, split):
    tokens = acts.shape[0]
    sums = lax.psum(project(acts, dictionary), "hid")
    codes_mid = refine(codes, sums[:tokens], sums[tokens:])
    codes_low = codes_mid.astype(bf16)
    cross = dot(acts, codes_low, OVER_ROWS)
    gram_codes = lax.psum(dot(codes_low, codes_low, OVER_ROWS), "tok")
    half = gram_codes.shape[0] // 2
    if split:
        mine = solve_rows(lax.psum_scatter(cross, "tok", tiled=True), factor_inverse(jnp.zeros((1,), jnp.int32), gram_codes[:half], gram_codes[half:]))
        dict_out = lax.all_gather(mine, "tok", tiled=True)
    else:
        dict_out = solve_rows(lax.psum(cross, "tok"), factor_inverse(jnp.zeros((1,), jnp.int32), gram_codes[:half], gram_codes[half:]))
    gram_part = dot(dict_out, dict_out, OVER_ROWS, HIGHEST)
    proj_two, gram_new = lax.psum((dot(acts, dict_out.astype(bf16)), gram_part), "hid")
    return refine(codes_mid, proj_two, gram_new), dict_out


def update(codes, sums, tokens, precision=HIGHEST):
    proj, gram = sums[:tokens], sums[tokens:]
    numer = jnp.maximum(proj, 0.0) + dot(codes, jnp.maximum(-gram, 0.0), precision=precision)
    denom = jnp.maximum(-proj, 0.0) + dot(codes, jnp.maximum(gram, 0.0), precision=precision)
    return codes * jnp.sqrt(numer / jnp.maximum(denom, floor_value))


def first_kernel(core_ref, codes_ref, mine_ref, theirs_ref, mid_ref, low_ref, gram_ref):
    mid = update(codes_ref[...], mine_ref[...] + theirs_ref[...], codes_ref.shape[0])
    low = mid.astype(bf16)
    mid_ref[...] = mid
    low_ref[...] = low
    half = low.shape[1] // 2
    side = jnp.where(core_ref[0] == 0, mid[:, :half], mid[:, half:]).astype(bf16)
    gram_ref[...] = dot(side.T, low)


def first_update(core, codes, mine, theirs):
    tokens, comp = codes.shape
    whole = pl.BlockSpec(memory_space=pltpu.VMEM)
    return pl.pallas_call(
        first_kernel,
        out_shape=[
            jax.ShapeDtypeStruct((tokens, comp), f32),
            jax.ShapeDtypeStruct((tokens, comp), bf16),
            jax.ShapeDtypeStruct((comp // 2, comp), f32),
        ],
        in_specs=[pl.BlockSpec(memory_space=pltpu.SMEM), whole, whole, whole],
        out_specs=[whole, whole, whole],
        compiler_params=LIMIT,
    )(core, codes, mine, theirs)


def second_kernel(codes_ref, mine_ref, theirs_ref, out_ref):
    out_ref[...] = update(codes_ref[...], mine_ref[...] + theirs_ref[...], codes_ref.shape[0])


def second_update(codes, mine, theirs):
    return pl.pallas_call(
        second_kernel,
        out_shape=jax.ShapeDtypeStruct(codes.shape, f32),
        compiler_params=LIMIT,
    )(codes, mine, theirs)


WHOLE = pl.BlockSpec(memory_space=pltpu.VMEM)
SCALARS = pl.BlockSpec(memory_space=pltpu.SMEM)
ANYWHERE = pl.BlockSpec(memory_space=pl.ANY)
TILE = 256


def call(kernel, out_shapes, table, values, after):
    return pl.pallas_call(
        kernel,
        out_shape=out_shapes,
        in_specs=[SCALARS] + [WHOLE] * len(values) + [ANYWHERE] * len(after),
        out_specs=[WHOLE] * len(out_shapes),
        compiler_params=LIMIT,
    )(table, *values, *after)


def shape(rows, comp):
    return jax.ShapeDtypeStruct((rows, comp), f32)


def first_fold_kernel(at, table_ref, mine_ref, theirs_ref, gram_ref, *refs):
    whole = mine_ref.shape[0]
    rows = whole // 2
    keep = pl.ds(pl.multiple_of(table_ref[at] * rows, rows), rows)
    give = pl.ds(pl.multiple_of((1 - table_ref[at]) * rows, rows), rows)
    gram = gram_ref[...] + theirs_ref[whole:, :]
    refs[-2][:rows, :] = mine_ref[give, :] + theirs_ref[give, :]
    refs[-2][rows:, :] = gram
    refs[-1][:rows, :] = mine_ref[keep, :] + theirs_ref[keep, :]
    refs[-1][rows:, :] = gram


def first_fold(table, at, mine, theirs, gram):
    half = shape(mine.shape[0] // 2 + gram.shape[0], mine.shape[1])
    return call(functools.partial(first_fold_kernel, at), [half, half], table, [mine, theirs, gram], [])


def mixed_fold_kernel(at, extra, table_ref, mine_ref, theirs_ref, *refs):
    whole = mine_ref.shape[0] - extra
    rows = whole // 2
    keep = pl.ds(pl.multiple_of(table_ref[at] * rows, 8), rows)
    give = pl.ds(pl.multiple_of((1 - table_ref[at]) * rows, 8), rows)
    gram = mine_ref[whole:, :] + theirs_ref[whole:, :]
    refs[-2][:rows, :] = mine_ref[give, :] + theirs_ref[give, :]
    refs[-2][rows:, :] = gram
    refs[-1][:rows, :] = mine_ref[keep, :] + theirs_ref[keep, :]
    refs[-1][rows:, :] = gram


def mixed_fold(table, at, extra, mine, theirs, after):
    half = shape((mine.shape[0] - extra) // 2 + extra, mine.shape[1])
    return call(functools.partial(mixed_fold_kernel, at, extra), [half, half], table, [mine, theirs], after)


def part_kernel(rows, table_ref, mine_ref, theirs_ref, *refs):
    refs[-2][...] = mine_ref[:rows, :] + theirs_ref[:rows, :]
    refs[-1][...] = mine_ref[rows:, :] + theirs_ref[rows:, :]


def part(table, rows, mine, theirs, after):
    shapes = [shape(rows, mine.shape[1]), shape(mine.shape[0] - rows, mine.shape[1])]
    return call(functools.partial(part_kernel, rows), shapes, table, [mine, theirs], after)


def rows_kernel(table_ref, inverse_ref, mine_ref, *refs):
    inverse = inverse_ref[...]
    cross = mine_ref[...] + refs[0][...] if len(refs) > 1 else mine_ref[...]
    refs[-1][...] = dot(dot(cross, inverse, OVER_COLS, HIGHEST), inverse, precision=HIGHEST)


def solve_sum(table, inverse, parts):
    return call(rows_kernel, [shape(*parts[0].shape)], table, [inverse, *parts], [])[0]


def absorb_kernel(ats, fresh, table_ref, acts_ref, *refs):
    count = len(ats)
    values, refs = refs[:count], refs[count:]
    if not fresh:
        sums_ref, refs = refs[0], refs[2:]
    out_ref, dict_ref = refs[:2]
    buffers, in_sem, out_sem = refs[2 : 2 + count], refs[2 + count], refs[3 + count]
    tokens = acts_ref.shape[0]
    ins, outs = [], []
    for k, value in enumerate(values):
        row = pl.multiple_of(table_ref[ats[k]] * TILE, TILE)
        rows = value.shape[0]
        ins.append(pltpu.make_async_copy(acts_ref.at[:, pl.ds(row, rows)], buffers[k], in_sem.at[k]))
        outs.append(pltpu.make_async_copy(value, dict_ref.at[pl.ds(row, rows), :], out_sem.at[k]))
        ins[k].start()
        outs[k].start()
    proj, gram = (0.0, 0.0) if fresh else (sums_ref[:tokens, :], sums_ref[tokens:, :])
    for k, value in enumerate(values):
        high = value[...].astype(bf16)
        gram = gram + dot(high.T, high)
        ins[k].wait()
        proj = proj + dot(buffers[k][...], high)
    out_ref[:tokens, :] = proj
    out_ref[tokens:, :] = gram
    for copy in outs:
        copy.wait()


def absorb(table, state, acts, blocks):
    tokens, hidden = acts.shape
    comp = blocks[0][0].shape[1]
    count = len(blocks)
    values = [value for value, _ in blocks]
    held = [] if state is None else list(state)
    total = sum(value.shape[0] for value in values)
    return pl.pallas_call(
        functools.partial(absorb_kernel, [at for _, at in blocks], state is None),
        out_shape=[shape(tokens + comp, comp), shape(hidden, comp)],
        in_specs=[SCALARS, ANYWHERE] + [WHOLE] * count + ([WHOLE, ANYWHERE] if held else []),
        out_specs=[WHOLE, ANYWHERE],
        scratch_shapes=[pltpu.VMEM((tokens, value.shape[0]), bf16) for value in values]
        + [pltpu.SemaphoreType.DMA((count,)), pltpu.SemaphoreType.DMA((count,))],
        input_output_aliases={2 + count: 0, 3 + count: 1} if held else {},
        compiler_params=LIMIT,
        cost_estimate=pl.CostEstimate(
            flops=2 * total * comp * (tokens + comp), bytes_accessed=total * (2 * tokens + 8 * comp), transcendentals=0
        ),
    )(table, acts, *values, *held)


def flips(bits):
    return [(t * 2 + c, (t ^ bits[c]) * 2 + c) for t in range(16) for c in range(2)]


X, Y, ZL, ZH = 1, 2, 4, 8
ALONG = {"first": (X, Y), "second": (Y, X), "near": (ZL, ZL), "far": (ZH, ZH)}
ORDERS = {
    "A": ("first", "second", "near", "far"),
    "B": ("first", "second", "near", "far"),
    "N": ("near", "first", "second", "far"),
}
SHARES = {"A": 2, "B": 3, "N": 2}
FIELDS = ("c", "d", "mine", "theirs", "far_mine", "far_theirs")


def swap(value, along):
    return lax.ppermute(value, BOTH, flips(ALONG[along]))


def layout(hidden):
    unit = hidden // sum(SHARES.values())
    rows = {name: share * unit for name, share in SHARES.items()}
    table = np.zeros((32, 1 + len(FIELDS) * len(rows)), np.int32)
    where = {"core": 0}
    start, column = 0, 1
    for name, order in ORDERS.items():
        half, quarter = rows[name] // 2 // TILE, rows[name] // 4 // TILE
        for t in range(16):
            for core in range(2):
                a, b, c, d = (int(t & ALONG[along][core] != 0) for along in order)
                here, there = start + a * half, start + (1 - a) * half
                table[t * 2 + core, 0] = core
                table[t * 2 + core, column : column + len(FIELDS)] = (
                    c, d,
                    here + b * quarter, here + (1 - b) * quarter, there + b * quarter, there + (1 - b) * quarter,
                )
        for k, field in enumerate(FIELDS):
            where[name, field] = column + k
        start, column = start + 2 * half, column + len(FIELDS)
    return rows, table, where


def meshed(acts, dictionary, codes):
    hidden = acts.shape[1]
    tok, core = lax.axis_index("tok"), lax.axis_index("hid")
    rows, places, where = layout(hidden)
    table = lax.dynamic_slice_in_dim(jnp.asarray(places), tok * 2 + core, 1, 0).reshape(-1)

    def other_core(value):
        return lax.ppermute(value, "hid", [(0, 1), (1, 0)])

    sums = project(acts, dictionary)
    codes_mid, low, gram = first_update(table, codes, sums, other_core(sums))

    def bit(along):
        on_0, on_1 = ALONG[along]
        return jnp.where(core == 0, (tok & on_0) // on_0, (tok & on_1) // on_1)

    bits = {along: bit(along) for along in ALONG}
    starts, start = {}, 0
    for name in ORDERS:
        starts[name], start = start, start + rows[name]

    def cross_of(row, count):
        return dot(lax.dynamic_slice_in_dim(acts, row, count, 1), low, OVER_ROWS)

    def give_1(name):
        half = rows[name] // 2
        return cross_of(starts[name] + (1 - bits[ORDERS[name][0]]) * half, half)

    def stage_2(name, got, keep):
        half, quarter = rows[name] // 2, rows[name] // 4
        a, b = (bits[along] for along in ORDERS[name][:2])
        which = b if keep else 1 - b
        out = cross_of(starts[name] + a * half + which * quarter, quarter)
        return out + lax.dynamic_slice_in_dim(got, which * quarter, quarter, 0)

    def part_of(value, which):
        half = value.shape[0] // 2
        return lax.dynamic_slice_in_dim(value, which * half, half, 0)

    def joined(one, other, which):
        return jnp.where(which == 0, jnp.concatenate([one, other]), jnp.concatenate([other, one]))

    extra = gram.shape[0]
    got = {
        "A": swap(jnp.concatenate([give_1("A"), gram]), ORDERS["A"][0]),
        "N": swap(give_1("N"), ORDERS["N"][0]),
        "B": swap(give_1("B"), ORDERS["B"][0]),
    }
    gram = gram + got["A"][rows["A"] // 2 :]
    held = {}
    for name in ("A", "N", "B"):
        give = stage_2(name, got[name], False)
        if name == "A":
            give = jnp.concatenate([give, gram])
        held[name] = stage_2(name, got[name], True), swap(give, ORDERS[name][1])
    for name, (keep, arrived) in held.items():
        along = ORDERS[name][2]
        if name == "A":
            give, keep = first_fold(table, where[name, "c"], keep, arrived, gram)
            held[name] = keep, swap(give, along)
        else:
            keep = keep + arrived
            held[name] = part_of(keep, bits[along]), swap(part_of(keep, 1 - bits[along]), along)
    for name, (keep, arrived) in held.items():
        along = ORDERS[name][3]
        if name == "A":
            give, keep = mixed_fold(table, where[name, "d"], extra, keep, arrived, [])
            held[name] = keep, swap(give, along)
        else:
            keep = keep + arrived
            held[name] = part_of(keep, bits[along]), swap(part_of(keep, 1 - bits[along]), along)

    a_mine, gram = part(table, rows["A"] // 16, *held["A"], [])
    inverse = factor_inverse(table, gram, other_core(gram), [held["N"][0], held["B"][0]])
    held["A"] = (a_mine,)
    mine = {name: solve_sum(table, inverse, held[name]) for name in held}

    for k in (3, 2):
        for name in mine:
            along = ORDERS[name][k]
            mine[name] = joined(mine[name], swap(mine[name], along), bits[along])
    near, far = [], []
    for name in mine:
        theirs = swap(mine[name], ORDERS[name][1])
        near += [(mine[name], where[name, "mine"]), (theirs, where[name, "theirs"])]
        far += [(swap(value, ORDERS[name][0]), where[name, field]) for value, field in ((mine[name], "far_mine"), (theirs, "far_theirs"))]
    sums, dict_out = absorb(table, absorb(table, None, acts, near), acts, far)
    return second_update(codes_mid, sums, other_core(sums)), dict_out


def solution(mesh):
    tok, hid = mesh.shape["tok"], mesh.shape["hid"]

    def per_device(acts, dictionary, codes):
        if tok == 16 and hid == 2 and acts.shape[1] % (7 * 1024) == 0:
            return meshed(acts, dictionary, codes)
        return plain(acts, dictionary, codes, acts.shape[1] % tok == 0)

    return jax.shard_map(
        per_device,
        mesh=mesh,
        in_specs=(P("tok", "hid"), P("hid", None), P("tok", None)),
        out_specs=(P("tok", None), P("hid", None)),
        check_vma=False,
    )
```

```python
import functools

import jax
import jax.numpy as jnp
import numpy as np
from jax import lax
from jax.experimental import pallas as pl
from jax.experimental.pallas import tpu as pltpu
from jax.sharding import PartitionSpec as P

floor_value = 0.05
HIGHEST = lax.Precision.HIGHEST
f32, bf16 = jnp.float32, jnp.bfloat16
BOTH = ("tok", "hid")
OVER_ROWS = (((0,), (0,)), ((), ()))
OVER_COLS = (((1,), (1,)), ((), ()))
LIMIT = pltpu.CompilerParams(vmem_limit_bytes=48 * 2**20)


def dot(left, right, dims=(((1,), (0,)), ((), ())), precision=None):
    return lax.dot_general(left, right, dims, precision=precision, preferred_element_type=f32)


def refine(codes, proj, gram):
    gram_pos = jnp.maximum(gram, 0.0)
    gram_neg = jnp.maximum(-gram, 0.0)
    numer = jnp.maximum(proj, 0.0) + dot(codes, gram_neg, precision=HIGHEST)
    denom = jnp.maximum(jnp.maximum(-proj, 0.0) + dot(codes, gram_pos, precision=HIGHEST), floor_value)
    return codes * jnp.sqrt(numer / denom)


def project_kernel(acts_ref, dict_ref, out_ref, cross_ref):
    step = pl.program_id(0)
    tokens = acts_ref.shape[0]

    @pl.when(step == 0)
    def _():
        out_ref[...] = jnp.zeros_like(out_ref)
        cross_ref[...] = jnp.zeros_like(cross_ref)

    rows = dict_ref[...]
    high = rows.astype(bf16)
    low = (rows - high.astype(f32)).astype(bf16)
    out_ref[:tokens, :] += dot(acts_ref[...], high)
    turned = high.T
    out_ref[tokens:, :] += dot(turned, high)
    cross_ref[...] += dot(turned, low)

    @pl.when(step == pl.num_programs(0) - 1)
    def _():
        out_ref[tokens:, :] += cross_ref[...] + cross_ref[...].T


def project(acts, dictionary):
    tokens, hidden = acts.shape
    comp = dictionary.shape[1]
    tile = 1024 if hidden % 1024 == 0 else 512
    return pl.pallas_call(
        project_kernel,
        out_shape=jax.ShapeDtypeStruct((tokens + comp, comp), f32),
        grid=(hidden // tile,),
        in_specs=[
            pl.BlockSpec((tokens, tile), lambda i: (0, i)),
            pl.BlockSpec((tile, comp), lambda i: (i, 0)),
        ],
        out_specs=pl.BlockSpec((tokens + comp, comp), lambda i: (0, 0)),
        scratch_shapes=[pltpu.VMEM((comp, comp), f32)],
        compiler_params=LIMIT,
        cost_estimate=pl.CostEstimate(
            flops=2 * hidden * comp * (tokens + 2 * comp), bytes_accessed=hidden * (2 * tokens + 4 * comp), transcendentals=0
        ),
    )(acts, dictionary)


def unit_inverse(block):
    n = block.shape[0]
    done = []
    rest = block
    for start in range(0, n, 8):
        shape = rest.shape
        row = lax.broadcasted_iota(jnp.int32, shape, 0)
        lane = lax.broadcasted_iota(jnp.int32, shape, 1)
        lane_row = lax.broadcasted_iota(jnp.int32, (1, n), 1)
        cols = [jnp.broadcast_to(rest[:, start + j : start + j + 1], shape) for j in range(8)]
        for j in range(8):
            inverse = 1.0 / cols[j][j : j + 1, :]
            below = jnp.where(row > j, cols[j], 0.0)
            scaled = jnp.where(lane_row == start + j, inverse, rest[j : j + 1, :] * inverse)
            rest = jnp.where((lane == start + j) & (row > j), 0.0, rest) - below * scaled
            for k in range(j + 1, 8):
                cols[k] = cols[k] - below * (cols[k][j : j + 1, :] * inverse)
        done.append(rest[:8, :])
        rest = rest[8:, :]
    full = jnp.concatenate(done, axis=0)
    row = lax.broadcasted_iota(jnp.int32, (n, n), 0)
    lane = lax.broadcasted_iota(jnp.int32, (n, n), 1)
    pivots = jnp.sum(jnp.where(row == lane, full, 0.0), axis=1, keepdims=True)
    unit = jnp.where(row > lane, full, jnp.where(row == lane, 1.0, 0.0))
    return unit * (1.0 / jnp.sqrt(pivots))


def factor(gram_ref, out_ref):
    half = gram_ref.shape[0] // 2
    upper = unit_inverse(gram_ref[:half, :half])
    side = dot(gram_ref[half:, :half], upper, OVER_COLS, HIGHEST)
    lower = unit_inverse(gram_ref[half:, half:] - dot(side, side, OVER_COLS, HIGHEST))
    out_ref[:half, :half] = upper
    out_ref[:half, half:] = jnp.zeros((half, half), f32)
    out_ref[half:, :half] = -dot(dot(lower, side, precision=HIGHEST), upper, precision=HIGHEST)
    out_ref[half:, half:] = lower


def halves_kernel(table_ref, mine_ref, theirs_ref, *refs):
    half = mine_ref.shape[0]
    out_ref, gram_ref = refs[-2:]
    gram_ref[pl.ds(pl.multiple_of(table_ref[0] * half, half), half), :] = mine_ref[...]
    gram_ref[pl.ds(pl.multiple_of((1 - table_ref[0]) * half, half), half), :] = theirs_ref[...]
    factor(gram_ref, out_ref)


def factor_inverse(table, mine, theirs, after=()):
    comp = mine.shape[1]
    return pl.pallas_call(
        halves_kernel,
        out_shape=jax.ShapeDtypeStruct((comp, comp), f32),
        in_specs=[pl.BlockSpec(memory_space=pltpu.SMEM)]
        + [pl.BlockSpec(memory_space=pltpu.VMEM)] * 2
        + [pl.BlockSpec(memory_space=pl.ANY)] * len(after),
        scratch_shapes=[pltpu.VMEM((comp, comp), f32)],
        compiler_params=LIMIT,
        cost_estimate=pl.CostEstimate(flops=10**10, bytes_accessed=8 * comp * comp, transcendentals=0),
    )(table, mine, theirs, *after)


def solve_rows(cross, inverse):
    return dot(dot(cross, inverse, OVER_COLS, HIGHEST), inverse, precision=HIGHEST)


def plain(acts, dictionary, codes, split):
    tokens = acts.shape[0]
    sums = lax.psum(project(acts, dictionary), "hid")
    codes_mid = refine(codes, sums[:tokens], sums[tokens:])
    codes_low = codes_mid.astype(bf16)
    cross = dot(acts, codes_low, OVER_ROWS)
    gram_codes = lax.psum(dot(codes_low, codes_low, OVER_ROWS), "tok")
    half = gram_codes.shape[0] // 2
    if split:
        mine = solve_rows(lax.psum_scatter(cross, "tok", tiled=True), factor_inverse(jnp.zeros((1,), jnp.int32), gram_codes[:half], gram_codes[half:]))
        dict_out = lax.all_gather(mine, "tok", tiled=True)
    else:
        dict_out = solve_rows(lax.psum(cross, "tok"), factor_inverse(jnp.zeros((1,), jnp.int32), gram_codes[:half], gram_codes[half:]))
    gram_part = dot(dict_out, dict_out, OVER_ROWS, HIGHEST)
    proj_two, gram_new = lax.psum((dot(acts, dict_out.astype(bf16)), gram_part), "hid")
    return refine(codes_mid, proj_two, gram_new), dict_out


def update(codes, sums, tokens, precision=HIGHEST):
    proj, gram = sums[:tokens], sums[tokens:]
    numer = jnp.maximum(proj, 0.0) + dot(codes, jnp.maximum(-gram, 0.0), precision=precision)
    denom = jnp.maximum(-proj, 0.0) + dot(codes, jnp.maximum(gram, 0.0), precision=precision)
    return codes * jnp.sqrt(numer / jnp.maximum(denom, floor_value))


def first_kernel(core_ref, codes_ref, mine_ref, theirs_ref, mid_ref, low_ref, gram_ref):
    mid = update(codes_ref[...], mine_ref[...] + theirs_ref[...], codes_ref.shape[0])
    low = mid.astype(bf16)
    mid_ref[...] = mid
    low_ref[...] = low
    half = low.shape[1] // 2
    side = jnp.where(core_ref[0] == 0, mid[:, :half], mid[:, half:]).astype(bf16)
    gram_ref[...] = dot(side.T, low)


def first_update(core, codes, mine, theirs):
    tokens, comp = codes.shape
    whole = pl.BlockSpec(memory_space=pltpu.VMEM)
    return pl.pallas_call(
        first_kernel,
        out_shape=[
            jax.ShapeDtypeStruct((tokens, comp), f32),
            jax.ShapeDtypeStruct((tokens, comp), bf16),
            jax.ShapeDtypeStruct((comp // 2, comp), f32),
        ],
        in_specs=[pl.BlockSpec(memory_space=pltpu.SMEM), whole, whole, whole],
        out_specs=[whole, whole, whole],
        compiler_params=LIMIT,
    )(core, codes, mine, theirs)


def second_kernel(codes_ref, mine_ref, theirs_ref, out_ref):
    out_ref[...] = update(codes_ref[...], mine_ref[...] + theirs_ref[...], codes_ref.shape[0])


def second_update(codes, mine, theirs):
    return pl.pallas_call(
        second_kernel,
        out_shape=jax.ShapeDtypeStruct(codes.shape, f32),
        compiler_params=LIMIT,
    )(codes, mine, theirs)


WHOLE = pl.BlockSpec(memory_space=pltpu.VMEM)
SCALARS = pl.BlockSpec(memory_space=pltpu.SMEM)
ANYWHERE = pl.BlockSpec(memory_space=pl.ANY)
TILE = 128


def call(kernel, out_shapes, table, values, after):
    return pl.pallas_call(
        kernel,
        out_shape=out_shapes,
        in_specs=[SCALARS] + [WHOLE] * len(values) + [ANYWHERE] * len(after),
        out_specs=[WHOLE] * len(out_shapes),
        compiler_params=LIMIT,
    )(table, *values, *after)


def shape(rows, comp):
    return jax.ShapeDtypeStruct((rows, comp), f32)


def first_fold_kernel(at, table_ref, mine_ref, theirs_ref, gram_ref, *refs):
    whole = mine_ref.shape[0]
    rows = whole // 2
    keep = pl.ds(pl.multiple_of(table_ref[at] * rows, rows), rows)
    give = pl.ds(pl.multiple_of((1 - table_ref[at]) * rows, rows), rows)
    gram = gram_ref[...] + theirs_ref[whole:, :]
    refs[-2][:rows, :] = mine_ref[give, :] + theirs_ref[give, :]
    refs[-2][rows:, :] = gram
    refs[-1][:rows, :] = mine_ref[keep, :] + theirs_ref[keep, :]
    refs[-1][rows:, :] = gram


def first_fold(table, at, mine, theirs, gram):
    half = shape(mine.shape[0] // 2 + gram.shape[0], mine.shape[1])
    return call(functools.partial(first_fold_kernel, at), [half, half], table, [mine, theirs, gram], [])


def split_fold_kernel(at, table_ref, mine_ref, theirs_ref, give_ref, keep_ref, gram_ref):
    rows = give_ref.shape[0]
    keep = pl.ds(pl.multiple_of(table_ref[at] * rows, rows), rows)
    give = pl.ds(pl.multiple_of((1 - table_ref[at]) * rows, rows), rows)
    give_ref[...] = mine_ref[give, :] + theirs_ref[give, :]
    keep_ref[...] = mine_ref[keep, :] + theirs_ref[keep, :]
    gram_ref[...] = mine_ref[2 * rows :, :] + theirs_ref[2 * rows :, :]


def split_fold(table, at, extra, mine, theirs):
    comp = mine.shape[1]
    half = shape((mine.shape[0] - extra) // 2, comp)
    return call(functools.partial(split_fold_kernel, at), [half, half, shape(extra, comp)], table, [mine, theirs], [])


def rows_kernel(table_ref, inverse_ref, mine_ref, *refs):
    inverse = inverse_ref[...]
    cross = mine_ref[...] + refs[0][...]
    refs[-1][...] = dot(dot(cross, inverse, OVER_COLS, HIGHEST), inverse, precision=HIGHEST)


def solve_sum(table, inverse, parts, after):
    return call(rows_kernel, [shape(*parts[0].shape)], table, [inverse, *parts], after)[0]


def absorb_kernel(ats, fresh, table_ref, acts_ref, *refs):
    count = len(ats)
    values, refs = refs[:count], refs[count:]
    if not fresh:
        sums_ref, refs = refs[0], refs[2:]
    out_ref, dict_ref = refs[:2]
    buffers, in_sem, out_sem = refs[2 : 2 + count], refs[2 + count], refs[3 + count]
    tokens = acts_ref.shape[0]
    ins, outs = [], []
    for k, value in enumerate(values):
        row = pl.multiple_of(table_ref[ats[k]] * TILE, TILE)
        rows = value.shape[0]
        ins.append(pltpu.make_async_copy(acts_ref.at[:, pl.ds(row, rows)], buffers[k], in_sem.at[k]))
        outs.append(pltpu.make_async_copy(value, dict_ref.at[pl.ds(row, rows), :], out_sem.at[k]))
        ins[k].start()
        outs[k].start()
    proj, gram = (0.0, 0.0) if fresh else (sums_ref[:tokens, :], sums_ref[tokens:, :])
    for k, value in enumerate(values):
        high = value[...].astype(bf16)
        gram = gram + dot(high.T, high)
        ins[k].wait()
        proj = proj + dot(buffers[k][...], high)
    out_ref[:tokens, :] = proj
    out_ref[tokens:, :] = gram
    for copy in outs:
        copy.wait()


def absorb(table, state, acts, blocks):
    tokens, hidden = acts.shape
    comp = blocks[0][0].shape[1]
    count = len(blocks)
    values = [value for value, _ in blocks]
    held = [] if state is None else list(state)
    total = sum(value.shape[0] for value in values)
    return pl.pallas_call(
        functools.partial(absorb_kernel, [at for _, at in blocks], state is None),
        out_shape=[shape(tokens + comp, comp), shape(hidden, comp)],
        in_specs=[SCALARS, ANYWHERE] + [WHOLE] * count + ([WHOLE, ANYWHERE] if held else []),
        out_specs=[WHOLE, ANYWHERE],
        scratch_shapes=[pltpu.VMEM((tokens, value.shape[0]), bf16) for value in values]
        + [pltpu.SemaphoreType.DMA((count,)), pltpu.SemaphoreType.DMA((count,))],
        input_output_aliases={2 + count: 0, 3 + count: 1} if held else {},
        compiler_params=LIMIT,
        cost_estimate=pl.CostEstimate(
            flops=2 * total * comp * (tokens + comp), bytes_accessed=total * (2 * tokens + 8 * comp), transcendentals=0
        ),
    )(table, acts, *values, *held)


def flips(bits):
    return [(t * 2 + c, (t ^ bits[c]) * 2 + c) for t in range(16) for c in range(2)]


X, Y, ZL, ZH = 1, 2, 4, 8
ALONG = {"first": (X, Y), "second": (Y, X), "near": (ZL, ZL), "far": (ZH, ZH)}
ORDERS = {
    "A": ("first", "second", "near", "far"),
    "B": ("first", "near", "second", "far"),
    "N": ("near", "first", "second", "far"),
}
SHARES = {"A": 4, "B": 5, "N": 5}
FIELDS = ("c", "d", "mine", "theirs", "far_mine", "far_theirs")


def swap(value, along):
    return lax.ppermute(value, BOTH, flips(ALONG[along]))


def layout(hidden):
    unit = hidden // sum(SHARES.values())
    rows = {name: share * unit for name, share in SHARES.items()}
    table = np.zeros((32, 1 + len(FIELDS) * len(rows)), np.int32)
    where = {"core": 0}
    start, column = 0, 1
    for name, order in ORDERS.items():
        half, quarter = rows[name] // 2 // TILE, rows[name] // 4 // TILE
        for t in range(16):
            for core in range(2):
                a, b, c, d = (int(t & ALONG[along][core] != 0) for along in order)
                here, there = start + a * half, start + (1 - a) * half
                table[t * 2 + core, 0] = core
                table[t * 2 + core, column : column + len(FIELDS)] = (
                    c, d,
                    here + b * quarter, here + (1 - b) * quarter, there + b * quarter, there + (1 - b) * quarter,
                )
        for k, field in enumerate(FIELDS):
            where[name, field] = column + k
        start, column = start + 2 * half, column + len(FIELDS)
    return rows, table, where


def meshed(acts, dictionary, codes):
    hidden = acts.shape[1]
    tok, core = lax.axis_index("tok"), lax.axis_index("hid")
    rows, places, where = layout(hidden)
    table = lax.dynamic_slice_in_dim(jnp.asarray(places), tok * 2 + core, 1, 0).reshape(-1)

    def other_core(value):
        return lax.ppermute(value, "hid", [(0, 1), (1, 0)])

    sums = project(acts, dictionary)
    codes_mid, low, gram = first_update(table, codes, sums, other_core(sums))

    def bit(along):
        on_0, on_1 = ALONG[along]
        return jnp.where(core == 0, (tok & on_0) // on_0, (tok & on_1) // on_1)

    bits = {along: bit(along) for along in ALONG}
    starts, start = {}, 0
    for name in ORDERS:
        starts[name], start = start, start + rows[name]

    def cross_of(row, count):
        return dot(lax.dynamic_slice_in_dim(acts, row, count, 1), low, OVER_ROWS)

    def give_1(name):
        half = rows[name] // 2
        return cross_of(starts[name] + (1 - bits[ORDERS[name][0]]) * half, half)

    def stage_2(name, got, keep):
        half, quarter = rows[name] // 2, rows[name] // 4
        a, b = (bits[along] for along in ORDERS[name][:2])
        which = b if keep else 1 - b
        out = cross_of(starts[name] + a * half + which * quarter, quarter)
        return out + lax.dynamic_slice_in_dim(got, which * quarter, quarter, 0)

    def part_of(value, which):
        half = value.shape[0] // 2
        return lax.dynamic_slice_in_dim(value, which * half, half, 0)

    def joined(one, other, which):
        return jnp.where(which == 0, jnp.concatenate([one, other]), jnp.concatenate([other, one]))

    gram = gram + swap(gram, "far")
    held = {}
    for name, order in ORDERS.items():
        got = swap(give_1(name), order[0])
        give = stage_2(name, got, False)
        if name == "A":
            give = jnp.concatenate([give, gram])
        held[name] = stage_2(name, got, True), swap(give, order[1])
    for name, (keep, arrived) in held.items():
        along = ORDERS[name][2]
        if name == "A":
            give, keep = first_fold(table, where[name, "c"], keep, arrived, gram)
            held[name] = keep, swap(give, along)
        else:
            keep = keep + arrived
            held[name] = part_of(keep, bits[along]), swap(part_of(keep, 1 - bits[along]), along)
    for name, (keep, arrived) in held.items():
        along = ORDERS[name][3]
        if name == "A":
            give, keep, gram = split_fold(table, where[name, "d"], gram.shape[0], keep, arrived)
            gram = gram + swap(gram, "first")
            held[name] = keep, swap(give, along)
        else:
            keep = keep + arrived
            held[name] = part_of(keep, bits[along]), swap(part_of(keep, 1 - bits[along]), along)

    inverse = factor_inverse(table, gram, other_core(gram))
    mine = {}
    for name in held:
        mine[name] = solve_sum(table, inverse, held[name], list(mine.values()))

    for k in (3, 2):
        for name in mine:
            along = ORDERS[name][k]
            mine[name] = joined(mine[name], swap(mine[name], along), bits[along])
    near, far, last = [], [], []
    for name in mine:
        theirs = swap(mine[name], ORDERS[name][1])
        near += [(mine[name], where[name, "mine"]), (theirs, where[name, "theirs"])]
        far += [(swap(mine[name], ORDERS[name][0]), where[name, "far_mine"])]
        last += [(swap(theirs, ORDERS[name][0]), where[name, "far_theirs"])]
    state = None
    for blocks in (near, far, last):
        state = absorb(table, state, acts, blocks)
    sums, dict_out = state
    return second_update(codes_mid, sums, other_core(sums)), dict_out


def solution(mesh):
    tok, hid = mesh.shape["tok"], mesh.shape["hid"]

    def per_device(acts, dictionary, codes):
        if tok == 16 and hid == 2 and acts.shape[1] % (14 * 512) == 0:
            return meshed(acts, dictionary, codes)
        return plain(acts, dictionary, codes, acts.shape[1] % tok == 0)

    return jax.shard_map(
        per_device,
        mesh=mesh,
        in_specs=(P("tok", "hid"), P("hid", None), P("tok", None)),
        out_specs=(P("tok", None), P("hid", None)),
        check_vma=False,
    )
```

```python
import functools

import jax
import jax.numpy as jnp
import numpy as np
from jax import lax
from jax.experimental import pallas as pl
from jax.experimental.pallas import tpu as pltpu
from jax.sharding import PartitionSpec as P

floor_value = 0.05
HIGHEST = lax.Precision.HIGHEST
f32, bf16 = jnp.float32, jnp.bfloat16
BOTH = ("tok", "hid")
OVER_ROWS = (((0,), (0,)), ((), ()))
OVER_COLS = (((1,), (1,)), ((), ()))
LIMIT = pltpu.CompilerParams(vmem_limit_bytes=48 * 2**20)


def dot(left, right, dims=(((1,), (0,)), ((), ())), precision=None):
    return lax.dot_general(left, right, dims, precision=precision, preferred_element_type=f32)


def refine(codes, proj, gram):
    gram_pos = jnp.maximum(gram, 0.0)
    gram_neg = jnp.maximum(-gram, 0.0)
    numer = jnp.maximum(proj, 0.0) + dot(codes, gram_neg, precision=HIGHEST)
    denom = jnp.maximum(jnp.maximum(-proj, 0.0) + dot(codes, gram_pos, precision=HIGHEST), floor_value)
    return codes * jnp.sqrt(numer / denom)


def project_kernel(acts_ref, dict_ref, out_ref, cross_ref):
    step = pl.program_id(0)
    tokens = acts_ref.shape[0]

    @pl.when(step == 0)
    def _():
        out_ref[...] = jnp.zeros_like(out_ref)
        cross_ref[...] = jnp.zeros_like(cross_ref)

    rows = dict_ref[...]
    high = rows.astype(bf16)
    low = (rows - high.astype(f32)).astype(bf16)
    out_ref[:tokens, :] += dot(acts_ref[...], high)
    turned = high.T
    out_ref[tokens:, :] += dot(turned, high)
    cross_ref[...] += dot(turned, low)

    @pl.when(step == pl.num_programs(0) - 1)
    def _():
        out_ref[tokens:, :] += cross_ref[...] + cross_ref[...].T


def project(acts, dictionary):
    tokens, hidden = acts.shape
    comp = dictionary.shape[1]
    tile = 1024 if hidden % 1024 == 0 else 512
    return pl.pallas_call(
        project_kernel,
        out_shape=jax.ShapeDtypeStruct((tokens + comp, comp), f32),
        grid=(hidden // tile,),
        in_specs=[
            pl.BlockSpec((tokens, tile), lambda i: (0, i)),
            pl.BlockSpec((tile, comp), lambda i: (i, 0)),
        ],
        out_specs=pl.BlockSpec((tokens + comp, comp), lambda i: (0, 0)),
        scratch_shapes=[pltpu.VMEM((comp, comp), f32)],
        compiler_params=LIMIT,
        cost_estimate=pl.CostEstimate(
            flops=2 * hidden * comp * (tokens + 2 * comp), bytes_accessed=hidden * (2 * tokens + 4 * comp), transcendentals=0
        ),
    )(acts, dictionary)


def unit_inverse(block):
    n = block.shape[0]
    done = []
    rest = block
    for start in range(0, n, 8):
        shape = rest.shape
        row = lax.broadcasted_iota(jnp.int32, shape, 0)
        lane = lax.broadcasted_iota(jnp.int32, shape, 1)
        lane_row = lax.broadcasted_iota(jnp.int32, (1, n), 1)
        cols = [jnp.broadcast_to(rest[:, start + j : start + j + 1], shape) for j in range(8)]
        for j in range(8):
            inverse = 1.0 / cols[j][j : j + 1, :]
            below = jnp.where(row > j, cols[j], 0.0)
            scaled = jnp.where(lane_row == start + j, inverse, rest[j : j + 1, :] * inverse)
            rest = jnp.where((lane == start + j) & (row > j), 0.0, rest) - below * scaled
            for k in range(j + 1, 8):
                cols[k] = cols[k] - below * (cols[k][j : j + 1, :] * inverse)
        done.append(rest[:8, :])
        rest = rest[8:, :]
    full = jnp.concatenate(done, axis=0)
    row = lax.broadcasted_iota(jnp.int32, (n, n), 0)
    lane = lax.broadcasted_iota(jnp.int32, (n, n), 1)
    pivots = jnp.sum(jnp.where(row == lane, full, 0.0), axis=1, keepdims=True)
    unit = jnp.where(row > lane, full, jnp.where(row == lane, 1.0, 0.0))
    return unit * (1.0 / jnp.sqrt(pivots))


def factor(gram_ref, out_ref):
    half = gram_ref.shape[0] // 2
    upper = unit_inverse(gram_ref[:half, :half])
    side = dot(gram_ref[half:, :half], upper, OVER_COLS, HIGHEST)
    lower = unit_inverse(gram_ref[half:, half:] - dot(side, side, OVER_COLS, HIGHEST))
    out_ref[:half, :half] = upper
    out_ref[:half, half:] = jnp.zeros((half, half), f32)
    out_ref[half:, :half] = -dot(dot(lower, side, precision=HIGHEST), upper, precision=HIGHEST)
    out_ref[half:, half:] = lower


def halves_kernel(table_ref, mine_ref, theirs_ref, *refs):
    half = mine_ref.shape[0]
    out_ref, gram_ref = refs[-2:]
    gram_ref[pl.ds(pl.multiple_of(table_ref[0] * half, half), half), :] = mine_ref[...]
    gram_ref[pl.ds(pl.multiple_of((1 - table_ref[0]) * half, half), half), :] = theirs_ref[...]
    factor(gram_ref, out_ref)


def factor_inverse(table, mine, theirs, after=()):
    comp = mine.shape[1]
    return pl.pallas_call(
        halves_kernel,
        out_shape=jax.ShapeDtypeStruct((comp, comp), f32),
        in_specs=[pl.BlockSpec(memory_space=pltpu.SMEM)]
        + [pl.BlockSpec(memory_space=pltpu.VMEM)] * 2
        + [pl.BlockSpec(memory_space=pl.ANY)] * len(after),
        scratch_shapes=[pltpu.VMEM((comp, comp), f32)],
        compiler_params=LIMIT,
        cost_estimate=pl.CostEstimate(flops=10**10, bytes_accessed=8 * comp * comp, transcendentals=0),
    )(table, mine, theirs, *after)


def solve_rows(cross, inverse):
    return dot(dot(cross, inverse, OVER_COLS, HIGHEST), inverse, precision=HIGHEST)


def plain(acts, dictionary, codes, split):
    tokens = acts.shape[0]
    sums = lax.psum(project(acts, dictionary), "hid")
    codes_mid = refine(codes, sums[:tokens], sums[tokens:])
    codes_low = codes_mid.astype(bf16)
    cross = dot(acts, codes_low, OVER_ROWS)
    gram_codes = lax.psum(dot(codes_low, codes_low, OVER_ROWS), "tok")
    half = gram_codes.shape[0] // 2
    if split:
        mine = solve_rows(lax.psum_scatter(cross, "tok", tiled=True), factor_inverse(jnp.zeros((1,), jnp.int32), gram_codes[:half], gram_codes[half:]))
        dict_out = lax.all_gather(mine, "tok", tiled=True)
    else:
        dict_out = solve_rows(lax.psum(cross, "tok"), factor_inverse(jnp.zeros((1,), jnp.int32), gram_codes[:half], gram_codes[half:]))
    gram_part = dot(dict_out, dict_out, OVER_ROWS, HIGHEST)
    proj_two, gram_new = lax.psum((dot(acts, dict_out.astype(bf16)), gram_part), "hid")
    return refine(codes_mid, proj_two, gram_new), dict_out


def update(codes, sums, tokens, precision=HIGHEST):
    proj, gram = sums[:tokens], sums[tokens:]
    numer = jnp.maximum(proj, 0.0) + dot(codes, jnp.maximum(-gram, 0.0), precision=precision)
    denom = jnp.maximum(-proj, 0.0) + dot(codes, jnp.maximum(gram, 0.0), precision=precision)
    return codes * jnp.sqrt(numer / jnp.maximum(denom, floor_value))


def first_kernel(core_ref, codes_ref, mine_ref, theirs_ref, mid_ref, low_ref, gram_ref):
    mid = update(codes_ref[...], mine_ref[...] + theirs_ref[...], codes_ref.shape[0])
    low = mid.astype(bf16)
    mid_ref[...] = mid
    low_ref[...] = low
    half = low.shape[1] // 2
    side = jnp.where(core_ref[0] == 0, mid[:, :half], mid[:, half:]).astype(bf16)
    gram_ref[...] = dot(side.T, low)


def first_update(core, codes, mine, theirs):
    tokens, comp = codes.shape
    whole = pl.BlockSpec(memory_space=pltpu.VMEM)
    return pl.pallas_call(
        first_kernel,
        out_shape=[
            jax.ShapeDtypeStruct((tokens, comp), f32),
            jax.ShapeDtypeStruct((tokens, comp), bf16),
            jax.ShapeDtypeStruct((comp // 2, comp), f32),
        ],
        in_specs=[pl.BlockSpec(memory_space=pltpu.SMEM), whole, whole, whole],
        out_specs=[whole, whole, whole],
        compiler_params=LIMIT,
    )(core, codes, mine, theirs)


def second_kernel(codes_ref, mine_ref, theirs_ref, out_ref):
    out_ref[...] = update(codes_ref[...], mine_ref[...] + theirs_ref[...], codes_ref.shape[0])


def second_update(codes, mine, theirs):
    return pl.pallas_call(
        second_kernel,
        out_shape=jax.ShapeDtypeStruct(codes.shape, f32),
        compiler_params=LIMIT,
    )(codes, mine, theirs)


WHOLE = pl.BlockSpec(memory_space=pltpu.VMEM)
SCALARS = pl.BlockSpec(memory_space=pltpu.SMEM)
ANYWHERE = pl.BlockSpec(memory_space=pl.ANY)
TILE = 128


def call(kernel, out_shapes, table, values, after):
    return pl.pallas_call(
        kernel,
        out_shape=out_shapes,
        in_specs=[SCALARS] + [WHOLE] * len(values) + [ANYWHERE] * len(after),
        out_specs=[WHOLE] * len(out_shapes),
        compiler_params=LIMIT,
    )(table, *values, *after)


def shape(rows, comp):
    return jax.ShapeDtypeStruct((rows, comp), f32)


def relay_kernel(table_ref, mine_ref, theirs_ref, low_ref, out_ref, low_out_ref):
    out_ref[...] = mine_ref[...] + theirs_ref[...]
    low_out_ref[...] = low_ref[...]


def relay(table, mine, theirs, low):
    shapes = [shape(*mine.shape), jax.ShapeDtypeStruct(low.shape, low.dtype)]
    return call(relay_kernel, shapes, table, [mine, theirs, low], [])


def fold_kernel(at, table_ref, mine_ref, theirs_ref, *refs):
    rows = mine_ref.shape[0] // 2
    keep = pl.ds(pl.multiple_of(table_ref[at] * rows, rows), rows)
    give = pl.ds(pl.multiple_of((1 - table_ref[at]) * rows, rows), rows)
    refs[-2][...] = mine_ref[give, :] + theirs_ref[give, :]
    refs[-1][...] = mine_ref[keep, :] + theirs_ref[keep, :]


def fold(table, at, mine, theirs, after):
    half = shape(mine.shape[0] // 2, mine.shape[1])
    return call(functools.partial(fold_kernel, at), [half, half], table, [mine, theirs], after)


def join_kernel(at, table_ref, mine_ref, theirs_ref, *refs):
    rows = mine_ref.shape[0]
    refs[-1][pl.ds(pl.multiple_of(table_ref[at] * rows, rows), rows), :] = mine_ref[...]
    refs[-1][pl.ds(pl.multiple_of((1 - table_ref[at]) * rows, rows), rows), :] = theirs_ref[...]


def join(table, at, mine, theirs, after):
    return call(functools.partial(join_kernel, at), [shape(2 * mine.shape[0], mine.shape[1])], table, [mine, theirs], after)[0]


def take_kernel(at, count, table_ref, mine_ref, theirs_ref, *refs):
    which = 1 - table_ref[at]
    refs[-1][:count, :] = mine_ref[...] + theirs_ref[pl.ds(pl.multiple_of(which * count, count), count), :]
    if refs[-1].shape[0] > count:
        refs[-1][count:, :] = refs[0][...]


def take(table, at, mine, theirs, tail, after):
    count = mine.shape[0]
    rows = count + sum(value.shape[0] for value in tail)
    return call(functools.partial(take_kernel, at, count), [shape(rows, mine.shape[1])], table, [mine, theirs, *tail], after)[0]


def first_fold_kernel(at, table_ref, mine_ref, theirs_ref, gram_ref, *refs):
    whole = mine_ref.shape[0]
    rows = whole // 2
    keep = pl.ds(pl.multiple_of(table_ref[at] * rows, rows), rows)
    give = pl.ds(pl.multiple_of((1 - table_ref[at]) * rows, rows), rows)
    gram = gram_ref[...] + theirs_ref[whole:, :]
    refs[-2][:rows, :] = mine_ref[give, :] + theirs_ref[give, :]
    refs[-2][rows:, :] = gram
    refs[-1][:rows, :] = mine_ref[keep, :] + theirs_ref[keep, :]
    refs[-1][rows:, :] = gram


def first_fold(table, at, mine, theirs, gram):
    half = shape(mine.shape[0] // 2 + gram.shape[0], mine.shape[1])
    return call(functools.partial(first_fold_kernel, at), [half, half], table, [mine, theirs, gram], [])


def split_fold_kernel(at, table_ref, mine_ref, theirs_ref, give_ref, keep_ref, gram_ref):
    rows = give_ref.shape[0]
    keep = pl.ds(pl.multiple_of(table_ref[at] * rows, rows), rows)
    give = pl.ds(pl.multiple_of((1 - table_ref[at]) * rows, rows), rows)
    give_ref[...] = mine_ref[give, :] + theirs_ref[give, :]
    keep_ref[...] = mine_ref[keep, :] + theirs_ref[keep, :]
    gram_ref[...] = mine_ref[2 * rows :, :] + theirs_ref[2 * rows :, :]


def split_fold(table, at, extra, mine, theirs):
    comp = mine.shape[1]
    half = shape((mine.shape[0] - extra) // 2, comp)
    return call(functools.partial(split_fold_kernel, at), [half, half, shape(extra, comp)], table, [mine, theirs], [])


def rows_kernel(table_ref, inverse_ref, mine_ref, *refs):
    inverse = inverse_ref[...]
    cross = mine_ref[...] + refs[0][...]
    refs[-1][...] = dot(dot(cross, inverse, OVER_COLS, HIGHEST), inverse, precision=HIGHEST)


def solve_sum(table, inverse, parts, after):
    return call(rows_kernel, [shape(*parts[0].shape)], table, [inverse, *parts], after)[0]


def absorb_kernel(ats, fresh, table_ref, acts_ref, *refs):
    count = len(ats)
    values, refs = refs[:count], refs[count:]
    if not fresh:
        sums_ref, refs = refs[0], refs[2:]
    out_ref, dict_ref = refs[:2]
    buffers, in_sem, out_sem = refs[2 : 2 + count], refs[2 + count], refs[3 + count]
    tokens = acts_ref.shape[0]
    ins, outs = [], []
    for k, value in enumerate(values):
        row = pl.multiple_of(table_ref[ats[k]] * TILE, TILE)
        rows = value.shape[0]
        ins.append(pltpu.make_async_copy(acts_ref.at[:, pl.ds(row, rows)], buffers[k], in_sem.at[k]))
        outs.append(pltpu.make_async_copy(value, dict_ref.at[pl.ds(row, rows), :], out_sem.at[k]))
        ins[k].start()
        outs[k].start()
    proj, gram = (0.0, 0.0) if fresh else (sums_ref[:tokens, :], sums_ref[tokens:, :])
    for k, value in enumerate(values):
        high = value[...].astype(bf16)
        gram = gram + dot(high.T, high)
        ins[k].wait()
        proj = proj + dot(buffers[k][...], high)
    out_ref[:tokens, :] = proj
    out_ref[tokens:, :] = gram
    for copy in outs:
        copy.wait()


def absorb(table, state, acts, blocks):
    tokens, hidden = acts.shape
    comp = blocks[0][0].shape[1]
    count = len(blocks)
    values = [value for value, _ in blocks]
    held = [] if state is None else list(state)
    total = sum(value.shape[0] for value in values)
    return pl.pallas_call(
        functools.partial(absorb_kernel, [at for _, at in blocks], state is None),
        out_shape=[shape(tokens + comp, comp), shape(hidden, comp)],
        in_specs=[SCALARS, ANYWHERE] + [WHOLE] * count + ([WHOLE, ANYWHERE] if held else []),
        out_specs=[WHOLE, ANYWHERE],
        scratch_shapes=[pltpu.VMEM((tokens, value.shape[0]), bf16) for value in values]
        + [pltpu.SemaphoreType.DMA((count,)), pltpu.SemaphoreType.DMA((count,))],
        input_output_aliases={2 + count: 0, 3 + count: 1} if held else {},
        compiler_params=LIMIT,
        cost_estimate=pl.CostEstimate(
            flops=2 * total * comp * (tokens + comp), bytes_accessed=total * (2 * tokens + 8 * comp), transcendentals=0
        ),
    )(table, acts, *values, *held)


def flips(bits):
    return [(t * 2 + c, (t ^ bits[c]) * 2 + c) for t in range(16) for c in range(2)]


X, Y, ZL, ZH = 1, 2, 4, 8
ALONG = {"first": (X, Y), "second": (Y, X), "near": (ZL, ZL), "far": (ZH, ZH)}
ORDERS = {
    "A": ("first", "second", "near", "far"),
    "B": ("first", "near", "second", "far"),
    "N": ("near", "first", "second", "far"),
}
SHARES = {"A": 5, "B": 5, "N": 4}
FIELDS = ("b", "c", "d", "mine", "theirs", "far_mine", "far_theirs")


def swap(value, along):
    return lax.ppermute(value, BOTH, flips(ALONG[along]))


def layout(hidden):
    unit = hidden // sum(SHARES.values())
    rows = {name: share * unit for name, share in SHARES.items()}
    table = np.zeros((32, 1 + len(FIELDS) * len(rows)), np.int32)
    where = {"core": 0}
    start, column = 0, 1
    for name, order in ORDERS.items():
        half, quarter = rows[name] // 2 // TILE, rows[name] // 4 // TILE
        for t in range(16):
            for core in range(2):
                a, b, c, d = (int(t & ALONG[along][core] != 0) for along in order)
                here, there = start + a * half, start + (1 - a) * half
                table[t * 2 + core, 0] = core
                table[t * 2 + core, column : column + len(FIELDS)] = (
                    b, c, d,
                    here + b * quarter, here + (1 - b) * quarter, there + b * quarter, there + (1 - b) * quarter,
                )
        for k, field in enumerate(FIELDS):
            where[name, field] = column + k
        start, column = start + 2 * half, column + len(FIELDS)
    return rows, table, where


def meshed(acts, dictionary, codes):
    hidden = acts.shape[1]
    tok, core = lax.axis_index("tok"), lax.axis_index("hid")
    rows, places, where = layout(hidden)
    table = lax.dynamic_slice_in_dim(jnp.asarray(places), tok * 2 + core, 1, 0).reshape(-1)

    def other_core(value):
        return lax.ppermute(value, "hid", [(0, 1), (1, 0)])

    sums = project(acts, dictionary)
    codes_mid, low, gram = first_update(table, codes, sums, other_core(sums))

    def bit(along):
        on_0, on_1 = ALONG[along]
        return jnp.where(core == 0, (tok & on_0) // on_0, (tok & on_1) // on_1)

    bits = {along: bit(along) for along in ALONG}
    starts, start = {}, 0
    for name in ORDERS:
        starts[name], start = start, start + rows[name]

    def cross_of(row, count, low):
        return dot(lax.dynamic_slice_in_dim(acts, row, count, 1), low, OVER_ROWS)

    def give_1(name, low):
        half = rows[name] // 2
        return cross_of(starts[name] + (1 - bits[ORDERS[name][0]]) * half, half, low)

    def own_2(name, keep):
        half, quarter = rows[name] // 2, rows[name] // 4
        a, b = (bits[along] for along in ORDERS[name][:2])
        return cross_of(starts[name] + a * half + (b if keep else 1 - b) * quarter, quarter, low)

    gram, low_later = relay(table, gram, swap(gram, "far"), low)
    got, keeps, held, last = {}, {}, {}, []
    for name, order in ORDERS.items():
        got[name] = swap(give_1(name, low if name == "A" else low_later), order[0])
    for name, order in ORDERS.items():
        give = take(table, where[name, "b"], own_2(name, False), got[name], [gram] if name == "A" else [], last)
        held[name], last = swap(give, order[1]), [give]
        quarter = rows[name] // 4
        keeps[name] = own_2(name, True) + lax.dynamic_slice_in_dim(got[name], bits[order[1]] * quarter, quarter, 0)
    last = []
    for name, order in ORDERS.items():
        if name == "A":
            give, keep = first_fold(table, where[name, "c"], keeps[name], held[name], gram)
        else:
            give, keep = fold(table, where[name, "c"], keeps[name], held[name], last)
        keeps[name], held[name], last = keep, swap(give, order[2]), [keep]
    last = []
    for name, order in ORDERS.items():
        if name == "A":
            give, keep, gram = split_fold(table, where[name, "d"], gram.shape[0], keeps[name], held[name])
            gram = gram + swap(gram, "first")
        else:
            give, keep = fold(table, where[name, "d"], keeps[name], held[name], last)
        held[name], last = (keep, swap(give, order[3])), [keep]

    inverse = factor_inverse(table, gram, other_core(gram), last)
    mine = {}
    for name in held:
        mine[name] = solve_sum(table, inverse, held[name], list(mine.values()))

    for k, field in ((3, "d"), (2, "c")):
        last = []
        for name, order in ORDERS.items():
            mine[name] = join(table, where[name, field], mine[name], swap(mine[name], order[k]), last)
            last = [mine[name]]
    near, far, last = [], [], []
    for name in mine:
        theirs = swap(mine[name], ORDERS[name][1])
        near += [(mine[name], where[name, "mine"]), (theirs, where[name, "theirs"])]
        far += [(swap(mine[name], ORDERS[name][0]), where[name, "far_mine"])]
        last += [(swap(theirs, ORDERS[name][0]), where[name, "far_theirs"])]
    state = None
    for blocks in (near, far, last[:2], last[2:]):
        state = absorb(table, state, acts, blocks)
    sums, dict_out = state
    return second_update(codes_mid, sums, other_core(sums)), dict_out


def solution(mesh):
    tok, hid = mesh.shape["tok"], mesh.shape["hid"]

    def per_device(acts, dictionary, codes):
        if tok == 16 and hid == 2 and acts.shape[1] % (14 * 512) == 0:
            return meshed(acts, dictionary, codes)
        return plain(acts, dictionary, codes, acts.shape[1] % tok == 0)

    return jax.shard_map(
        per_device,
        mesh=mesh,
        in_specs=(P("tok", "hid"), P("hid", None), P("tok", None)),
        out_specs=(P("tok", None), P("hid", None)),
        check_vma=False,
    )
```

```python
import functools

import jax
import jax.numpy as jnp
import numpy as np
from jax import lax
from jax.experimental import pallas as pl
from jax.experimental.pallas import tpu as pltpu
from jax.sharding import PartitionSpec as P

floor_value = 0.05
HIGHEST = lax.Precision.HIGHEST
f32, bf16 = jnp.float32, jnp.bfloat16
BOTH = ("tok", "hid")
OVER_ROWS = (((0,), (0,)), ((), ()))
OVER_COLS = (((1,), (1,)), ((), ()))
LIMIT = pltpu.CompilerParams(vmem_limit_bytes=48 * 2**20)


def dot(left, right, dims=(((1,), (0,)), ((), ())), precision=None):
    return lax.dot_general(left, right, dims, precision=precision, preferred_element_type=f32)


def refine(codes, proj, gram):
    gram_pos = jnp.maximum(gram, 0.0)
    gram_neg = jnp.maximum(-gram, 0.0)
    numer = jnp.maximum(proj, 0.0) + dot(codes, gram_neg, precision=HIGHEST)
    denom = jnp.maximum(jnp.maximum(-proj, 0.0) + dot(codes, gram_pos, precision=HIGHEST), floor_value)
    return codes * jnp.sqrt(numer / denom)


def project_kernel(acts_ref, dict_ref, out_ref, cross_ref):
    step = pl.program_id(0)
    tokens = acts_ref.shape[0]

    @pl.when(step == 0)
    def _():
        out_ref[...] = jnp.zeros_like(out_ref)
        cross_ref[...] = jnp.zeros_like(cross_ref)

    rows = dict_ref[...]
    high = rows.astype(bf16)
    low = (rows - high.astype(f32)).astype(bf16)
    out_ref[:tokens, :] += dot(acts_ref[...], high)
    turned = high.T
    out_ref[tokens:, :] += dot(turned, high)
    cross_ref[...] += dot(turned, low)

    @pl.when(step == pl.num_programs(0) - 1)
    def _():
        out_ref[tokens:, :] += cross_ref[...] + cross_ref[...].T


def project(acts, dictionary):
    tokens, hidden = acts.shape
    comp = dictionary.shape[1]
    tile = 1024 if hidden % 1024 == 0 else 512
    return pl.pallas_call(
        project_kernel,
        out_shape=jax.ShapeDtypeStruct((tokens + comp, comp), f32),
        grid=(hidden // tile,),
        in_specs=[
            pl.BlockSpec((tokens, tile), lambda i: (0, i)),
            pl.BlockSpec((tile, comp), lambda i: (i, 0)),
        ],
        out_specs=pl.BlockSpec((tokens + comp, comp), lambda i: (0, 0)),
        scratch_shapes=[pltpu.VMEM((comp, comp), f32)],
        compiler_params=LIMIT,
        cost_estimate=pl.CostEstimate(
            flops=2 * hidden * comp * (tokens + 2 * comp), bytes_accessed=hidden * (2 * tokens + 4 * comp), transcendentals=0
        ),
    )(acts, dictionary)


def unit_inverse(block):
    n = block.shape[0]
    done = []
    rest = block
    for start in range(0, n, 8):
        shape = rest.shape
        row = lax.broadcasted_iota(jnp.int32, shape, 0)
        lane = lax.broadcasted_iota(jnp.int32, shape, 1)
        lane_row = lax.broadcasted_iota(jnp.int32, (1, n), 1)
        cols = [jnp.broadcast_to(rest[:, start + j : start + j + 1], shape) for j in range(8)]
        for j in range(8):
            inverse = 1.0 / cols[j][j : j + 1, :]
            below = jnp.where(row > j, cols[j], 0.0)
            scaled = jnp.where(lane_row == start + j, inverse, rest[j : j + 1, :] * inverse)
            rest = jnp.where((lane == start + j) & (row > j), 0.0, rest) - below * scaled
            for k in range(j + 1, 8):
                cols[k] = cols[k] - below * (cols[k][j : j + 1, :] * inverse)
        done.append(rest[:8, :])
        rest = rest[8:, :]
    full = jnp.concatenate(done, axis=0)
    row = lax.broadcasted_iota(jnp.int32, (n, n), 0)
    lane = lax.broadcasted_iota(jnp.int32, (n, n), 1)
    pivots = jnp.sum(jnp.where(row == lane, full, 0.0), axis=1, keepdims=True)
    unit = jnp.where(row > lane, full, jnp.where(row == lane, 1.0, 0.0))
    return unit * (1.0 / jnp.sqrt(pivots))


def factor(gram_ref, out_ref):
    half = gram_ref.shape[0] // 2
    upper = unit_inverse(gram_ref[:half, :half])
    side = dot(gram_ref[half:, :half], upper, OVER_COLS, HIGHEST)
    lower = unit_inverse(gram_ref[half:, half:] - dot(side, side, OVER_COLS, HIGHEST))
    out_ref[:half, :half] = upper
    out_ref[:half, half:] = jnp.zeros((half, half), f32)
    out_ref[half:, :half] = -dot(dot(lower, side, precision=HIGHEST), upper, precision=HIGHEST)
    out_ref[half:, half:] = lower


def halves_kernel(table_ref, mine_ref, theirs_ref, *refs):
    half = mine_ref.shape[0]
    out_ref, gram_ref = refs[-2:]
    gram_ref[pl.ds(pl.multiple_of(table_ref[0] * half, half), half), :] = mine_ref[...]
    gram_ref[pl.ds(pl.multiple_of((1 - table_ref[0]) * half, half), half), :] = theirs_ref[...]
    factor(gram_ref, out_ref)


def factor_inverse(table, mine, theirs, after=()):
    comp = mine.shape[1]
    return pl.pallas_call(
        halves_kernel,
        out_shape=jax.ShapeDtypeStruct((comp, comp), f32),
        in_specs=[pl.BlockSpec(memory_space=pltpu.SMEM)]
        + [pl.BlockSpec(memory_space=pltpu.VMEM)] * 2
        + [pl.BlockSpec(memory_space=pl.ANY)] * len(after),
        scratch_shapes=[pltpu.VMEM((comp, comp), f32)],
        compiler_params=LIMIT,
        cost_estimate=pl.CostEstimate(flops=10**10, bytes_accessed=8 * comp * comp, transcendentals=0),
    )(table, mine, theirs, *after)


def solve_rows(cross, inverse):
    return dot(dot(cross, inverse, OVER_COLS, HIGHEST), inverse, precision=HIGHEST)


def plain(acts, dictionary, codes, split):
    tokens = acts.shape[0]
    sums = lax.psum(project(acts, dictionary), "hid")
    codes_mid = refine(codes, sums[:tokens], sums[tokens:])
    codes_low = codes_mid.astype(bf16)
    cross = dot(acts, codes_low, OVER_ROWS)
    gram_codes = lax.psum(dot(codes_low, codes_low, OVER_ROWS), "tok")
    half = gram_codes.shape[0] // 2
    if split:
        mine = solve_rows(lax.psum_scatter(cross, "tok", tiled=True), factor_inverse(jnp.zeros((1,), jnp.int32), gram_codes[:half], gram_codes[half:]))
        dict_out = lax.all_gather(mine, "tok", tiled=True)
    else:
        dict_out = solve_rows(lax.psum(cross, "tok"), factor_inverse(jnp.zeros((1,), jnp.int32), gram_codes[:half], gram_codes[half:]))
    gram_part = dot(dict_out, dict_out, OVER_ROWS, HIGHEST)
    proj_two, gram_new = lax.psum((dot(acts, dict_out.astype(bf16)), gram_part), "hid")
    return refine(codes_mid, proj_two, gram_new), dict_out


def update(codes, sums, tokens, precision=HIGHEST):
    proj, gram = sums[:tokens], sums[tokens:]
    numer = jnp.maximum(proj, 0.0) + dot(codes, jnp.maximum(-gram, 0.0), precision=precision)
    denom = jnp.maximum(-proj, 0.0) + dot(codes, jnp.maximum(gram, 0.0), precision=precision)
    return codes * jnp.sqrt(numer / jnp.maximum(denom, floor_value))


def first_kernel(core_ref, codes_ref, mine_ref, theirs_ref, mid_ref, low_ref, gram_ref):
    mid = update(codes_ref[...], mine_ref[...] + theirs_ref[...], codes_ref.shape[0])
    low = mid.astype(bf16)
    mid_ref[...] = mid
    low_ref[...] = low
    half = low.shape[1] // 2
    side = jnp.where(core_ref[0] == 0, mid[:, :half], mid[:, half:]).astype(bf16)
    gram_ref[...] = dot(side.T, low)


def first_update(core, codes, mine, theirs):
    tokens, comp = codes.shape
    whole = pl.BlockSpec(memory_space=pltpu.VMEM)
    return pl.pallas_call(
        first_kernel,
        out_shape=[
            jax.ShapeDtypeStruct((tokens, comp), f32),
            jax.ShapeDtypeStruct((tokens, comp), bf16),
            jax.ShapeDtypeStruct((comp // 2, comp), f32),
        ],
        in_specs=[pl.BlockSpec(memory_space=pltpu.SMEM), whole, whole, whole],
        out_specs=[whole, whole, whole],
        compiler_params=LIMIT,
    )(core, codes, mine, theirs)


def second_kernel(codes_ref, mine_ref, theirs_ref, out_ref):
    out_ref[...] = update(codes_ref[...], mine_ref[...] + theirs_ref[...], codes_ref.shape[0])


def second_update(codes, mine, theirs):
    return pl.pallas_call(
        second_kernel,
        out_shape=jax.ShapeDtypeStruct(codes.shape, f32),
        compiler_params=LIMIT,
    )(codes, mine, theirs)


WHOLE = pl.BlockSpec(memory_space=pltpu.VMEM)
SCALARS = pl.BlockSpec(memory_space=pltpu.SMEM)
ANYWHERE = pl.BlockSpec(memory_space=pl.ANY)
TILE = 128


def call(kernel, out_shapes, table, values, after):
    return pl.pallas_call(
        kernel,
        out_shape=out_shapes,
        in_specs=[SCALARS] + [WHOLE] * len(values) + [ANYWHERE] * len(after),
        out_specs=[WHOLE] * len(out_shapes),
        compiler_params=LIMIT,
    )(table, *values, *after)


def shape(rows, comp):
    return jax.ShapeDtypeStruct((rows, comp), f32)


def relay_kernel(table_ref, mine_ref, theirs_ref, low_ref, out_ref, low_out_ref):
    out_ref[...] = mine_ref[...] + theirs_ref[...]
    low_out_ref[...] = low_ref[...]


def relay(table, mine, theirs, low):
    shapes = [shape(*mine.shape), jax.ShapeDtypeStruct(low.shape, low.dtype)]
    return call(relay_kernel, shapes, table, [mine, theirs, low], [])


def several(kernel, table, groups, outs, after):
    counts = [len(group) for group in groups]
    gives = [len(shapes) for shapes in outs]

    def body(table_ref, *refs):
        ins, results = refs[: sum(counts)], refs[len(refs) - sum(gives) :]
        for k, (count, give) in enumerate(zip(counts, gives)):
            kernel(k, table_ref, ins[:count], results[:give])
            ins, results = ins[count:], results[give:]

    flat = call(body, [one for shapes in outs for one in shapes], table, [value for group in groups for value in group], after)
    results = []
    for give in gives:
        results.append(flat[:give])
        flat = flat[give:]
    return results


def fold(table, ats, pairs, after):
    def kernel(k, table_ref, ins, results):
        rows = ins[0].shape[0] // 2
        keep = pl.ds(pl.multiple_of(table_ref[ats[k]] * rows, rows), rows)
        give = pl.ds(pl.multiple_of((1 - table_ref[ats[k]]) * rows, rows), rows)
        results[0][...] = ins[0][give, :] + ins[1][give, :]
        results[1][...] = ins[0][keep, :] + ins[1][keep, :]

    return several(kernel, table, pairs, [[shape(mine.shape[0] // 2, mine.shape[1])] * 2 for mine, _ in pairs], after)


def join(table, ats, pairs, after):
    def kernel(k, table_ref, ins, results):
        rows = ins[0].shape[0]
        results[0][pl.ds(pl.multiple_of(table_ref[ats[k]] * rows, rows), rows), :] = ins[0][...]
        results[0][pl.ds(pl.multiple_of((1 - table_ref[ats[k]]) * rows, rows), rows), :] = ins[1][...]

    return several(kernel, table, pairs, [[shape(2 * mine.shape[0], mine.shape[1])] for mine, _ in pairs], after)


def take(table, ats, groups, after):
    def kernel(k, table_ref, ins, results):
        count = ins[0].shape[0]
        give = pl.ds(pl.multiple_of((1 - table_ref[ats[k]]) * count, count), count)
        results[0][:count, :] = ins[0][...] + ins[1][give, :]
        if len(ins) > 2:
            results[0][count:, :] = ins[2][...]

    rows = [group[0].shape[0] + sum(value.shape[0] for value in group[2:]) for group in groups]
    return several(kernel, table, groups, [[shape(count, groups[0][0].shape[1])] for count in rows], after)


def solve(table, inverse, pairs, after):
    def kernel(k, table_ref, ins, results):
        factor_inv = ins[2][...]
        results[0][...] = dot(dot(ins[0][...] + ins[1][...], factor_inv, OVER_COLS, HIGHEST), factor_inv, precision=HIGHEST)

    groups = [(mine, theirs, inverse) for mine, theirs in pairs]
    return several(kernel, table, groups, [[shape(*mine.shape)] for mine, _ in pairs], after)


def first_fold_kernel(at, table_ref, mine_ref, theirs_ref, gram_ref, *refs):
    whole = mine_ref.shape[0]
    rows = whole // 2
    keep = pl.ds(pl.multiple_of(table_ref[at] * rows, rows), rows)
    give = pl.ds(pl.multiple_of((1 - table_ref[at]) * rows, rows), rows)
    gram = gram_ref[...] + theirs_ref[whole:, :]
    refs[-2][:rows, :] = mine_ref[give, :] + theirs_ref[give, :]
    refs[-2][rows:, :] = gram
    refs[-1][:rows, :] = mine_ref[keep, :] + theirs_ref[keep, :]
    refs[-1][rows:, :] = gram


def first_fold(table, at, mine, theirs, gram, after):
    half = shape(mine.shape[0] // 2 + gram.shape[0], mine.shape[1])
    return call(functools.partial(first_fold_kernel, at), [half, half], table, [mine, theirs, gram], after)


def split_fold_kernel(at, table_ref, mine_ref, theirs_ref, *refs):
    give_ref, keep_ref, gram_ref = refs[-3:]
    rows = give_ref.shape[0]
    keep = pl.ds(pl.multiple_of(table_ref[at] * rows, rows), rows)
    give = pl.ds(pl.multiple_of((1 - table_ref[at]) * rows, rows), rows)
    give_ref[...] = mine_ref[give, :] + theirs_ref[give, :]
    keep_ref[...] = mine_ref[keep, :] + theirs_ref[keep, :]
    gram_ref[...] = mine_ref[2 * rows :, :] + theirs_ref[2 * rows :, :]


def split_fold(table, at, extra, mine, theirs, after):
    comp = mine.shape[1]
    half = shape((mine.shape[0] - extra) // 2, comp)
    return call(functools.partial(split_fold_kernel, at), [half, half, shape(extra, comp)], table, [mine, theirs], after)


def absorb_kernel(ats, fresh, table_ref, acts_ref, *refs):
    count = len(ats)
    values, refs = refs[:count], refs[count:]
    if not fresh:
        sums_ref, refs = refs[0], refs[2:]
    out_ref, dict_ref = refs[:2]
    buffers, in_sem, out_sem = refs[2 : 2 + count], refs[2 + count], refs[3 + count]
    tokens = acts_ref.shape[0]
    ins, outs = [], []
    for k, value in enumerate(values):
        row = pl.multiple_of(table_ref[ats[k]] * TILE, TILE)
        rows = value.shape[0]
        ins.append(pltpu.make_async_copy(acts_ref.at[:, pl.ds(row, rows)], buffers[k], in_sem.at[k]))
        outs.append(pltpu.make_async_copy(value, dict_ref.at[pl.ds(row, rows), :], out_sem.at[k]))
        ins[k].start()
        outs[k].start()
    proj, gram = (0.0, 0.0) if fresh else (sums_ref[:tokens, :], sums_ref[tokens:, :])
    for k, value in enumerate(values):
        high = value[...].astype(bf16)
        gram = gram + dot(high.T, high)
        ins[k].wait()
        proj = proj + dot(buffers[k][...], high)
    out_ref[:tokens, :] = proj
    out_ref[tokens:, :] = gram
    for copy in outs:
        copy.wait()


def absorb(table, state, acts, blocks):
    tokens, hidden = acts.shape
    comp = blocks[0][0].shape[1]
    count = len(blocks)
    values = [value for value, _ in blocks]
    held = [] if state is None else list(state)
    total = sum(value.shape[0] for value in values)
    return pl.pallas_call(
        functools.partial(absorb_kernel, [at for _, at in blocks], state is None),
        out_shape=[shape(tokens + comp, comp), shape(hidden, comp)],
        in_specs=[SCALARS, ANYWHERE] + [WHOLE] * count + ([WHOLE, ANYWHERE] if held else []),
        out_specs=[WHOLE, ANYWHERE],
        scratch_shapes=[pltpu.VMEM((tokens, value.shape[0]), bf16) for value in values]
        + [pltpu.SemaphoreType.DMA((count,)), pltpu.SemaphoreType.DMA((count,))],
        input_output_aliases={2 + count: 0, 3 + count: 1} if held else {},
        compiler_params=LIMIT,
        cost_estimate=pl.CostEstimate(
            flops=2 * total * comp * (tokens + comp), bytes_accessed=total * (2 * tokens + 8 * comp), transcendentals=0
        ),
    )(table, acts, *values, *held)


def flips(bits):
    return [(t * 2 + c, (t ^ bits[c]) * 2 + c) for t in range(16) for c in range(2)]


X, Y, ZL, ZH = 1, 2, 4, 8
ALONG = {"first": (X, Y), "second": (Y, X), "near": (ZL, ZL), "far": (ZH, ZH)}
ORDERS = {
    "A": ("first", "second", "near", "far"),
    "B": ("first", "near", "second", "far"),
    "N": ("near", "first", "second", "far"),
}
TURNS = (("A",), ("B", "N"))
SHARES = {"A": 5, "B": 5, "N": 4}
FIELDS = ("b", "c", "d", "mine", "theirs", "far_mine", "far_theirs")


def swap(value, along):
    return lax.ppermute(value, BOTH, flips(ALONG[along]))


def layout(hidden):
    unit = hidden // sum(SHARES.values())
    rows = {name: share * unit for name, share in SHARES.items()}
    table = np.zeros((32, 1 + len(FIELDS) * len(rows)), np.int32)
    where = {"core": 0}
    start, column = 0, 1
    for name, order in ORDERS.items():
        half, quarter = rows[name] // 2 // TILE, rows[name] // 4 // TILE
        for t in range(16):
            for core in range(2):
                a, b, c, d = (int(t & ALONG[along][core] != 0) for along in order)
                here, there = start + a * half, start + (1 - a) * half
                table[t * 2 + core, 0] = core
                table[t * 2 + core, column : column + len(FIELDS)] = (
                    b, c, d,
                    here + b * quarter, here + (1 - b) * quarter, there + b * quarter, there + (1 - b) * quarter,
                )
        for k, field in enumerate(FIELDS):
            where[name, field] = column + k
        start, column = start + 2 * half, column + len(FIELDS)
    return rows, table, where


def meshed(acts, dictionary, codes):
    hidden = acts.shape[1]
    tok, core = lax.axis_index("tok"), lax.axis_index("hid")
    rows, places, where = layout(hidden)
    table = lax.dynamic_slice_in_dim(jnp.asarray(places), tok * 2 + core, 1, 0).reshape(-1)

    def other_core(value):
        return lax.ppermute(value, "hid", [(0, 1), (1, 0)])

    sums = project(acts, dictionary)
    codes_mid, low, gram = first_update(table, codes, sums, other_core(sums))

    def bit(along):
        on_0, on_1 = ALONG[along]
        return jnp.where(core == 0, (tok & on_0) // on_0, (tok & on_1) // on_1)

    bits = {along: bit(along) for along in ALONG}
    starts, start = {}, 0
    for name in ORDERS:
        starts[name], start = start, start + rows[name]

    def cross_of(row, count, low):
        return dot(lax.dynamic_slice_in_dim(acts, row, count, 1), low, OVER_ROWS)

    def give_1(name, low):
        half = rows[name] // 2
        return cross_of(starts[name] + (1 - bits[ORDERS[name][0]]) * half, half, low)

    def own_2(name, keep):
        half, quarter = rows[name] // 2, rows[name] // 4
        a, b = (bits[along] for along in ORDERS[name][:2])
        return cross_of(starts[name] + a * half + (b if keep else 1 - b) * quarter, quarter, low)

    gram, low_later = relay(table, gram, swap(gram, "far"), low)
    got, keeps, held = {}, {}, {}
    for name, order in ORDERS.items():
        got[name] = swap(give_1(name, low if name == "A" else low_later), order[0])
    last = []
    for names in TURNS:
        groups = [[own_2(name, False), got[name]] + ([gram] if name == "A" else []) for name in names]
        gives = take(table, [where[name, "b"] for name in names], groups, last)
        for name, (give,) in zip(names, gives):
            held[name], last = swap(give, ORDERS[name][1]), [give]
            quarter = rows[name] // 4
            kept = lax.dynamic_slice_in_dim(got[name], bits[ORDERS[name][1]] * quarter, quarter, 0)
            keeps[name] = own_2(name, True) + kept
    for k, field in ((2, "c"), (3, "d")):
        for names in TURNS:
            if "A" in names and k == 2:
                parts = [first_fold(table, where["A", "c"], keeps["A"], held["A"], gram, last)]
            elif "A" in names:
                give, keep, gram = split_fold(table, where["A", "d"], gram.shape[0], keeps["A"], held["A"], last)
                gram = gram + swap(gram, "first")
                parts = [(give, keep)]
            else:
                parts = fold(table, [where[name, field] for name in names], [(keeps[name], held[name]) for name in names], last)
            for name, (give, keep) in zip(names, parts):
                keeps[name], held[name], last = keep, swap(give, ORDERS[name][k]), [keep]

    inverse = factor_inverse(table, gram, other_core(gram), last)
    mine, last = {}, []
    for names in TURNS:
        parts = solve(table, inverse, [(keeps[name], held[name]) for name in names], last)
        for name, (value,) in zip(names, parts):
            mine[name], last = value, [value]

    for k, field in ((3, "d"), (2, "c")):
        for names in TURNS:
            pairs = [(mine[name], swap(mine[name], ORDERS[name][k])) for name in names]
            parts = join(table, [where[name, field] for name in names], pairs, last)
            for name, (value,) in zip(names, parts):
                mine[name], last = value, [value]
    near, far, last = [], [], []
    for name in mine:
        theirs = swap(mine[name], ORDERS[name][1])
        near += [(mine[name], where[name, "mine"]), (theirs, where[name, "theirs"])]
        far += [(swap(mine[name], ORDERS[name][0]), where[name, "far_mine"])]
        last += [(swap(theirs, ORDERS[name][0]), where[name, "far_theirs"])]
    state = None
    for blocks in (near, far, last[2:], last[:2]):
        state = absorb(table, state, acts, blocks)
    sums, dict_out = state
    return second_update(codes_mid, sums, other_core(sums)), dict_out


def solution(mesh):
    tok, hid = mesh.shape["tok"], mesh.shape["hid"]

    def per_device(acts, dictionary, codes):
        if tok == 16 and hid == 2 and acts.shape[1] % (14 * 512) == 0:
            return meshed(acts, dictionary, codes)
        return plain(acts, dictionary, codes, acts.shape[1] % tok == 0)

    return jax.shard_map(
        per_device,
        mesh=mesh,
        in_specs=(P("tok", "hid"), P("hid", None), P("tok", None)),
        out_specs=(P("tok", None), P("hid", None)),
        check_vma=False,
    )
```

```python
import functools

import jax
import jax.numpy as jnp
import numpy as np
from jax import lax
from jax.experimental import pallas as pl
from jax.experimental.pallas import tpu as pltpu
from jax.sharding import PartitionSpec as P

floor_value = 0.05
HIGHEST = lax.Precision.HIGHEST
f32, bf16 = jnp.float32, jnp.bfloat16
BOTH = ("tok", "hid")
OVER_ROWS = (((0,), (0,)), ((), ()))
OVER_COLS = (((1,), (1,)), ((), ()))
LIMIT = pltpu.CompilerParams(vmem_limit_bytes=48 * 2**20)


def dot(left, right, dims=(((1,), (0,)), ((), ())), precision=None):
    return lax.dot_general(left, right, dims, precision=precision, preferred_element_type=f32)


def refine(codes, proj, gram):
    gram_pos = jnp.maximum(gram, 0.0)
    gram_neg = jnp.maximum(-gram, 0.0)
    numer = jnp.maximum(proj, 0.0) + dot(codes, gram_neg, precision=HIGHEST)
    denom = jnp.maximum(jnp.maximum(-proj, 0.0) + dot(codes, gram_pos, precision=HIGHEST), floor_value)
    return codes * jnp.sqrt(numer / denom)


def project_kernel(acts_ref, dict_ref, out_ref, cross_ref):
    step = pl.program_id(0)
    tokens = acts_ref.shape[0]

    @pl.when(step == 0)
    def _():
        out_ref[...] = jnp.zeros_like(out_ref)
        cross_ref[...] = jnp.zeros_like(cross_ref)

    rows = dict_ref[...]
    high = rows.astype(bf16)
    low = (rows - high.astype(f32)).astype(bf16)
    out_ref[:tokens, :] += dot(acts_ref[...], high)
    turned = high.T
    out_ref[tokens:, :] += dot(turned, high)
    cross_ref[...] += dot(turned, low)

    @pl.when(step == pl.num_programs(0) - 1)
    def _():
        out_ref[tokens:, :] += cross_ref[...] + cross_ref[...].T


def project(acts, dictionary):
    tokens, hidden = acts.shape
    comp = dictionary.shape[1]
    tile = 1024 if hidden % 1024 == 0 else 512
    return pl.pallas_call(
        project_kernel,
        out_shape=jax.ShapeDtypeStruct((tokens + comp, comp), f32),
        grid=(hidden // tile,),
        in_specs=[
            pl.BlockSpec((tokens, tile), lambda i: (0, i)),
            pl.BlockSpec((tile, comp), lambda i: (i, 0)),
        ],
        out_specs=pl.BlockSpec((tokens + comp, comp), lambda i: (0, 0)),
        scratch_shapes=[pltpu.VMEM((comp, comp), f32)],
        compiler_params=LIMIT,
        cost_estimate=pl.CostEstimate(
            flops=2 * hidden * comp * (tokens + 2 * comp), bytes_accessed=hidden * (2 * tokens + 4 * comp), transcendentals=0
        ),
    )(acts, dictionary)


def unit_inverse(block):
    n = block.shape[0]
    done = []
    rest = block
    for start in range(0, n, 8):
        shape = rest.shape
        row = lax.broadcasted_iota(jnp.int32, shape, 0)
        lane = lax.broadcasted_iota(jnp.int32, shape, 1)
        lane_row = lax.broadcasted_iota(jnp.int32, (1, n), 1)
        cols = [jnp.broadcast_to(rest[:, start + j : start + j + 1], shape) for j in range(8)]
        for j in range(8):
            inverse = 1.0 / cols[j][j : j + 1, :]
            below = jnp.where(row > j, cols[j], 0.0)
            scaled = jnp.where(lane_row == start + j, inverse, rest[j : j + 1, :] * inverse)
            rest = jnp.where((lane == start + j) & (row > j), 0.0, rest) - below * scaled
            for k in range(j + 1, 8):
                cols[k] = cols[k] - below * (cols[k][j : j + 1, :] * inverse)
        done.append(rest[:8, :])
        rest = rest[8:, :]
    full = jnp.concatenate(done, axis=0)
    row = lax.broadcasted_iota(jnp.int32, (n, n), 0)
    lane = lax.broadcasted_iota(jnp.int32, (n, n), 1)
    pivots = jnp.sum(jnp.where(row == lane, full, 0.0), axis=1, keepdims=True)
    unit = jnp.where(row > lane, full, jnp.where(row == lane, 1.0, 0.0))
    return unit * (1.0 / jnp.sqrt(pivots))


def factor(gram_ref, out_ref):
    half = gram_ref.shape[0] // 2
    upper = unit_inverse(gram_ref[:half, :half])
    side = dot(gram_ref[half:, :half], upper, OVER_COLS, HIGHEST)
    lower = unit_inverse(gram_ref[half:, half:] - dot(side, side, OVER_COLS, HIGHEST))
    out_ref[:half, :half] = upper
    out_ref[:half, half:] = jnp.zeros((half, half), f32)
    out_ref[half:, :half] = -dot(dot(lower, side, precision=HIGHEST), upper, precision=HIGHEST)
    out_ref[half:, half:] = lower


def halves_kernel(table_ref, mine_ref, theirs_ref, *refs):
    half = mine_ref.shape[0]
    out_ref, gram_ref = refs[-2:]
    gram_ref[pl.ds(pl.multiple_of(table_ref[0] * half, half), half), :] = mine_ref[...]
    gram_ref[pl.ds(pl.multiple_of((1 - table_ref[0]) * half, half), half), :] = theirs_ref[...]
    factor(gram_ref, out_ref)


def factor_inverse(table, mine, theirs, after=()):
    comp = mine.shape[1]
    return pl.pallas_call(
        halves_kernel,
        out_shape=jax.ShapeDtypeStruct((comp, comp), f32),
        in_specs=[pl.BlockSpec(memory_space=pltpu.SMEM)]
        + [pl.BlockSpec(memory_space=pltpu.VMEM)] * 2
        + [pl.BlockSpec(memory_space=pl.ANY)] * len(after),
        scratch_shapes=[pltpu.VMEM((comp, comp), f32)],
        compiler_params=LIMIT,
        cost_estimate=pl.CostEstimate(flops=10**10, bytes_accessed=8 * comp * comp, transcendentals=0),
    )(table, mine, theirs, *after)


def solve_rows(cross, inverse):
    return dot(dot(cross, inverse, OVER_COLS, HIGHEST), inverse, precision=HIGHEST)


def plain(acts, dictionary, codes, split):
    tokens = acts.shape[0]
    sums = lax.psum(project(acts, dictionary), "hid")
    codes_mid = refine(codes, sums[:tokens], sums[tokens:])
    codes_low = codes_mid.astype(bf16)
    cross = dot(acts, codes_low, OVER_ROWS)
    gram_codes = lax.psum(dot(codes_low, codes_low, OVER_ROWS), "tok")
    half = gram_codes.shape[0] // 2
    if split:
        mine = solve_rows(lax.psum_scatter(cross, "tok", tiled=True), factor_inverse(jnp.zeros((1,), jnp.int32), gram_codes[:half], gram_codes[half:]))
        dict_out = lax.all_gather(mine, "tok", tiled=True)
    else:
        dict_out = solve_rows(lax.psum(cross, "tok"), factor_inverse(jnp.zeros((1,), jnp.int32), gram_codes[:half], gram_codes[half:]))
    gram_part = dot(dict_out, dict_out, OVER_ROWS, HIGHEST)
    proj_two, gram_new = lax.psum((dot(acts, dict_out.astype(bf16)), gram_part), "hid")
    return refine(codes_mid, proj_two, gram_new), dict_out


def update(codes, sums, tokens, precision=HIGHEST):
    proj, gram = sums[:tokens], sums[tokens:]
    numer = jnp.maximum(proj, 0.0) + dot(codes, jnp.maximum(-gram, 0.0), precision=precision)
    denom = jnp.maximum(-proj, 0.0) + dot(codes, jnp.maximum(gram, 0.0), precision=precision)
    return codes * jnp.sqrt(numer / jnp.maximum(denom, floor_value))


def first_kernel(core_ref, codes_ref, mine_ref, theirs_ref, mid_ref, low_ref, gram_ref):
    mid = update(codes_ref[...], mine_ref[...] + theirs_ref[...], codes_ref.shape[0])
    low = mid.astype(bf16)
    mid_ref[...] = mid
    low_ref[...] = low
    half = low.shape[1] // 2
    side = jnp.where(core_ref[0] == 0, mid[:, :half], mid[:, half:]).astype(bf16)
    gram_ref[...] = dot(side.T, low)


def first_update(core, codes, mine, theirs):
    tokens, comp = codes.shape
    whole = pl.BlockSpec(memory_space=pltpu.VMEM)
    return pl.pallas_call(
        first_kernel,
        out_shape=[
            jax.ShapeDtypeStruct((tokens, comp), f32),
            jax.ShapeDtypeStruct((tokens, comp), bf16),
            jax.ShapeDtypeStruct((comp // 2, comp), f32),
        ],
        in_specs=[pl.BlockSpec(memory_space=pltpu.SMEM), whole, whole, whole],
        out_specs=[whole, whole, whole],
        compiler_params=LIMIT,
    )(core, codes, mine, theirs)


def second_kernel(codes_ref, mine_ref, theirs_ref, out_ref):
    out_ref[...] = update(codes_ref[...], mine_ref[...] + theirs_ref[...], codes_ref.shape[0])


def second_update(codes, mine, theirs):
    return pl.pallas_call(
        second_kernel,
        out_shape=jax.ShapeDtypeStruct(codes.shape, f32),
        compiler_params=LIMIT,
    )(codes, mine, theirs)


WHOLE = pl.BlockSpec(memory_space=pltpu.VMEM)
SCALARS = pl.BlockSpec(memory_space=pltpu.SMEM)
ANYWHERE = pl.BlockSpec(memory_space=pl.ANY)
TILE = 128


def call(kernel, out_shapes, table, values, after):
    return pl.pallas_call(
        kernel,
        out_shape=out_shapes,
        in_specs=[SCALARS] + [WHOLE] * len(values) + [ANYWHERE] * len(after),
        out_specs=[WHOLE] * len(out_shapes),
        compiler_params=LIMIT,
    )(table, *values, *after)


def shape(rows, comp):
    return jax.ShapeDtypeStruct((rows, comp), f32)


def first_fold_kernel(at, table_ref, mine_ref, theirs_ref, gram_ref, *refs):
    whole = mine_ref.shape[0]
    rows = whole // 2
    keep = pl.ds(pl.multiple_of(table_ref[at] * rows, rows), rows)
    give = pl.ds(pl.multiple_of((1 - table_ref[at]) * rows, rows), rows)
    gram = gram_ref[...] + theirs_ref[whole:, :]
    refs[-2][:rows, :] = mine_ref[give, :] + theirs_ref[give, :]
    refs[-2][rows:, :] = gram
    refs[-1][:rows, :] = mine_ref[keep, :] + theirs_ref[keep, :]
    refs[-1][rows:, :] = gram


def first_fold(table, at, mine, theirs, gram):
    half = shape(mine.shape[0] // 2 + gram.shape[0], mine.shape[1])
    return call(functools.partial(first_fold_kernel, at), [half, half], table, [mine, theirs, gram], [])


def mixed_fold_kernel(at, extra, table_ref, mine_ref, theirs_ref, give_ref, keep_ref):
    whole = mine_ref.shape[0] - extra
    rows = whole // 2
    keep = pl.ds(pl.multiple_of(table_ref[at] * rows, rows), rows)
    give = pl.ds(pl.multiple_of((1 - table_ref[at]) * rows, rows), rows)
    gram = mine_ref[whole:, :] + theirs_ref[whole:, :]
    give_ref[:rows, :] = mine_ref[give, :] + theirs_ref[give, :]
    give_ref[rows:, :] = gram
    keep_ref[:rows, :] = mine_ref[keep, :] + theirs_ref[keep, :]
    keep_ref[rows:, :] = gram


def mixed_fold(table, at, extra, mine, theirs):
    half = shape((mine.shape[0] - extra) // 2 + extra, mine.shape[1])
    return call(functools.partial(mixed_fold_kernel, at, extra), [half, half], table, [mine, theirs], [])


def part_kernel(table_ref, mine_ref, theirs_ref, rows_ref, rest_ref):
    rows = rows_ref.shape[0]
    rows_ref[...] = mine_ref[:rows, :] + theirs_ref[:rows, :]
    rest_ref[...] = mine_ref[rows:, :] + theirs_ref[rows:, :]


def part(table, rows, mine, theirs):
    shapes = [shape(rows, mine.shape[1]), shape(mine.shape[0] - rows, mine.shape[1])]
    return call(part_kernel, shapes, table, [mine, theirs], [])


def join_kernel(at, table_ref, mine_ref, theirs_ref, *refs):
    rows = mine_ref.shape[0]
    refs[-1][pl.ds(pl.multiple_of(table_ref[at] * rows, rows), rows), :] = mine_ref[...]
    refs[-1][pl.ds(pl.multiple_of((1 - table_ref[at]) * rows, rows), rows), :] = theirs_ref[...]


def join(table, at, mine, theirs, after):
    return call(functools.partial(join_kernel, at), [shape(2 * mine.shape[0], mine.shape[1])], table, [mine, theirs], after)[0]


def rows_kernel(theirs, table_ref, inverse_ref, mine_ref, *refs):
    inverse = inverse_ref[...]
    cross = mine_ref[...]
    if theirs:
        cross = cross + refs[0][...]
    refs[-1][...] = dot(dot(cross, inverse, OVER_COLS, HIGHEST), inverse, precision=HIGHEST)


def solve_sum(table, inverse, parts, after):
    kernel = functools.partial(rows_kernel, len(parts) > 1)
    return call(kernel, [shape(*parts[0].shape)], table, [inverse, *parts], after)[0]


def absorb_kernel(ats, fresh, table_ref, acts_ref, *refs):
    count = len(ats)
    values, refs = refs[:count], refs[count:]
    if not fresh:
        sums_ref, refs = refs[0], refs[2:]
    out_ref, dict_ref = refs[:2]
    buffers, in_sem, out_sem = refs[2 : 2 + count], refs[2 + count], refs[3 + count]
    tokens = acts_ref.shape[0]
    ins, outs = [], []
    for k, value in enumerate(values):
        row = pl.multiple_of(table_ref[ats[k]] * TILE, TILE)
        rows = value.shape[0]
        ins.append(pltpu.make_async_copy(acts_ref.at[:, pl.ds(row, rows)], buffers[k], in_sem.at[k]))
        outs.append(pltpu.make_async_copy(value, dict_ref.at[pl.ds(row, rows), :], out_sem.at[k]))
        ins[k].start()
        outs[k].start()
    proj, gram = (0.0, 0.0) if fresh else (sums_ref[:tokens, :], sums_ref[tokens:, :])
    for k, value in enumerate(values):
        high = value[...].astype(bf16)
        gram = gram + dot(high.T, high)
        ins[k].wait()
        proj = proj + dot(buffers[k][...], high)
    out_ref[:tokens, :] = proj
    out_ref[tokens:, :] = gram
    for copy in outs:
        copy.wait()


def absorb(table, state, acts, blocks):
    tokens, hidden = acts.shape
    comp = blocks[0][0].shape[1]
    count = len(blocks)
    values = [value for value, _ in blocks]
    held = [] if state is None else list(state)
    total = sum(value.shape[0] for value in values)
    return pl.pallas_call(
        functools.partial(absorb_kernel, [at for _, at in blocks], state is None),
        out_shape=[shape(tokens + comp, comp), shape(hidden, comp)],
        in_specs=[SCALARS, ANYWHERE] + [WHOLE] * count + ([WHOLE, ANYWHERE] if held else []),
        out_specs=[WHOLE, ANYWHERE],
        scratch_shapes=[pltpu.VMEM((tokens, value.shape[0]), bf16) for value in values]
        + [pltpu.SemaphoreType.DMA((count,)), pltpu.SemaphoreType.DMA((count,))],
        input_output_aliases={2 + count: 0, 3 + count: 1} if held else {},
        compiler_params=LIMIT,
        cost_estimate=pl.CostEstimate(
            flops=2 * total * comp * (tokens + comp), bytes_accessed=total * (2 * tokens + 8 * comp), transcendentals=0
        ),
    )(table, acts, *values, *held)


def flips(bits):
    return [(t * 2 + c, (t ^ bits[c]) * 2 + c) for t in range(16) for c in range(2)]


X, Y, ZL, ZH = 1, 2, 4, 8
ALONG = {"first": (X, Y), "second": (Y, X), "near": (ZL, ZL), "far": (ZH, ZH)}
ORDERS = {
    "A": ("first", "second", "near", "far"),
    "B": ("first", "near", "second", "far"),
    "N": ("near", "first", "second", "far"),
}
SHARES = {"A": 4, "B": 5, "N": 5}
FIELDS = ("c", "d", "mine", "theirs", "far_mine", "far_theirs")


def swap(value, along):
    return lax.ppermute(value, BOTH, flips(ALONG[along]))


def layout(hidden):
    unit = hidden // sum(SHARES.values())
    rows = {name: share * unit for name, share in SHARES.items()}
    table = np.zeros((32, 1 + len(FIELDS) * len(rows)), np.int32)
    where = {"core": 0}
    start, column = 0, 1
    for name, order in ORDERS.items():
        half, quarter = rows[name] // 2 // TILE, rows[name] // 4 // TILE
        for t in range(16):
            for core in range(2):
                a, b, c, d = (int(t & ALONG[along][core] != 0) for along in order)
                here, there = start + a * half, start + (1 - a) * half
                table[t * 2 + core, 0] = core
                table[t * 2 + core, column : column + len(FIELDS)] = (
                    c, d,
                    here + b * quarter, here + (1 - b) * quarter, there + b * quarter, there + (1 - b) * quarter,
                )
        for k, field in enumerate(FIELDS):
            where[name, field] = column + k
        start, column = start + 2 * half, column + len(FIELDS)
    return rows, table, where


def meshed(acts, dictionary, codes):
    hidden = acts.shape[1]
    tok, core = lax.axis_index("tok"), lax.axis_index("hid")
    rows, places, where = layout(hidden)
    table = lax.dynamic_slice_in_dim(jnp.asarray(places), tok * 2 + core, 1, 0).reshape(-1)

    def other_core(value):
        return lax.ppermute(value, "hid", [(0, 1), (1, 0)])

    sums = project(acts, dictionary)
    codes_mid, low, gram = first_update(table, codes, sums, other_core(sums))

    def bit(along):
        on_0, on_1 = ALONG[along]
        return jnp.where(core == 0, (tok & on_0) // on_0, (tok & on_1) // on_1)

    bits = {along: bit(along) for along in ALONG}
    starts, start = {}, 0
    for name in ORDERS:
        starts[name], start = start, start + rows[name]

    def cross_of(row, count):
        return dot(lax.dynamic_slice_in_dim(acts, row, count, 1), low, OVER_ROWS)

    def give_1(name):
        half = rows[name] // 2
        return cross_of(starts[name] + (1 - bits[ORDERS[name][0]]) * half, half)

    def stage_2(name, got, keep):
        half, quarter = rows[name] // 2, rows[name] // 4
        a, b = (bits[along] for along in ORDERS[name][:2])
        which = b if keep else 1 - b
        out = cross_of(starts[name] + a * half + which * quarter, quarter)
        return out + lax.dynamic_slice_in_dim(got, which * quarter, quarter, 0)

    def part_of(value, which):
        half = value.shape[0] // 2
        return lax.dynamic_slice_in_dim(value, which * half, half, 0)

    held = {}
    for name, order in ORDERS.items():
        give = give_1(name)
        if name == "A":
            give = jnp.concatenate([give, gram])
        got = swap(give, order[0])
        give = stage_2(name, got, False)
        if name == "A":
            gram = gram + got[rows[name] // 2 :]
            give = jnp.concatenate([give, gram])
        held[name] = stage_2(name, got, True), swap(give, order[1])
    for name, (keep, arrived) in held.items():
        along = ORDERS[name][2]
        if name == "A":
            give, keep = first_fold(table, where[name, "c"], keep, arrived, gram)
            held[name] = keep, swap(give, along)
        else:
            keep = keep + arrived
            held[name] = part_of(keep, bits[along]), swap(part_of(keep, 1 - bits[along]), along)
    for name, (keep, arrived) in held.items():
        along = ORDERS[name][3]
        if name == "A":
            give, keep = mixed_fold(table, where[name, "d"], gram.shape[0], keep, arrived)
            held[name] = keep, swap(give, along)
        else:
            keep = keep + arrived
            held[name] = part_of(keep, bits[along]), swap(part_of(keep, 1 - bits[along]), along)

    a_mine, gram = part(table, rows["A"] // 16, *held["A"])
    inverse = factor_inverse(table, gram, other_core(gram), [held["N"][0], held["B"][0]])
    held["A"] = (a_mine,)
    mine = {}
    for name in held:
        mine[name] = solve_sum(table, inverse, held[name], list(mine.values()))

    for k, field in ((3, "d"), (2, "c")):
        last = []
        for name, order in ORDERS.items():
            mine[name] = join(table, where[name, field], mine[name], swap(mine[name], order[k]), last)
            last = [mine[name]]
    near, far, last = [], [], []
    for name in mine:
        theirs = swap(mine[name], ORDERS[name][1])
        near += [(mine[name], where[name, "mine"]), (theirs, where[name, "theirs"])]
        far += [(swap(mine[name], ORDERS[name][0]), where[name, "far_mine"])]
        last += [(swap(theirs, ORDERS[name][0]), where[name, "far_theirs"])]
    state = None
    for blocks in (near, far, last[2:], last[:2]):
        state = absorb(table, state, acts, blocks)
    sums, dict_out = state
    return second_update(codes_mid, sums, other_core(sums)), dict_out


def solution(mesh):
    tok, hid = mesh.shape["tok"], mesh.shape["hid"]

    def per_device(acts, dictionary, codes):
        if tok == 16 and hid == 2 and acts.shape[1] % (14 * 512) == 0:
            return meshed(acts, dictionary, codes)
        return plain(acts, dictionary, codes, acts.shape[1] % tok == 0)

    return jax.shard_map(
        per_device,
        mesh=mesh,
        in_specs=(P("tok", "hid"), P("hid", None), P("tok", None)),
        out_specs=(P("tok", None), P("hid", None)),
        check_vma=False,
    )
```

```python
import functools

import jax
import jax.numpy as jnp
import numpy as np
from jax import lax
from jax.experimental import pallas as pl
from jax.experimental.pallas import tpu as pltpu
from jax.sharding import PartitionSpec as P

floor_value = 0.05
HIGHEST = lax.Precision.HIGHEST
f32, bf16 = jnp.float32, jnp.bfloat16
BOTH = ("tok", "hid")
OVER_ROWS = (((0,), (0,)), ((), ()))
OVER_COLS = (((1,), (1,)), ((), ()))
LIMIT = pltpu.CompilerParams(vmem_limit_bytes=48 * 2**20)


def dot(left, right, dims=(((1,), (0,)), ((), ())), precision=None):
    return lax.dot_general(left, right, dims, precision=precision, preferred_element_type=f32)


def refine(codes, proj, gram):
    gram_pos = jnp.maximum(gram, 0.0)
    gram_neg = jnp.maximum(-gram, 0.0)
    numer = jnp.maximum(proj, 0.0) + dot(codes, gram_neg, precision=HIGHEST)
    denom = jnp.maximum(jnp.maximum(-proj, 0.0) + dot(codes, gram_pos, precision=HIGHEST), floor_value)
    return codes * jnp.sqrt(numer / denom)


def project_kernel(acts_ref, dict_ref, out_ref, cross_ref):
    step = pl.program_id(0)
    tokens = acts_ref.shape[0]

    @pl.when(step == 0)
    def _():
        out_ref[...] = jnp.zeros_like(out_ref)
        cross_ref[...] = jnp.zeros_like(cross_ref)

    rows = dict_ref[...]
    high = rows.astype(bf16)
    low = (rows - high.astype(f32)).astype(bf16)
    out_ref[:tokens, :] += dot(acts_ref[...], high)
    turned = high.T
    out_ref[tokens:, :] += dot(turned, high)
    cross_ref[...] += dot(turned, low)

    @pl.when(step == pl.num_programs(0) - 1)
    def _():
        out_ref[tokens:, :] += cross_ref[...] + cross_ref[...].T


def project(acts, dictionary):
    tokens, hidden = acts.shape
    comp = dictionary.shape[1]
    tile = 1024 if hidden % 1024 == 0 else 512
    return pl.pallas_call(
        project_kernel,
        out_shape=jax.ShapeDtypeStruct((tokens + comp, comp), f32),
        grid=(hidden // tile,),
        in_specs=[
            pl.BlockSpec((tokens, tile), lambda i: (0, i)),
            pl.BlockSpec((tile, comp), lambda i: (i, 0)),
        ],
        out_specs=pl.BlockSpec((tokens + comp, comp), lambda i: (0, 0)),
        scratch_shapes=[pltpu.VMEM((comp, comp), f32)],
        compiler_params=LIMIT,
        cost_estimate=pl.CostEstimate(
            flops=2 * hidden * comp * (tokens + 2 * comp), bytes_accessed=hidden * (2 * tokens + 4 * comp), transcendentals=0
        ),
    )(acts, dictionary)


def unit_inverse(block):
    n = block.shape[0]
    done = []
    rest = block
    for start in range(0, n, 8):
        shape = rest.shape
        row = lax.broadcasted_iota(jnp.int32, shape, 0)
        lane = lax.broadcasted_iota(jnp.int32, shape, 1)
        lane_row = lax.broadcasted_iota(jnp.int32, (1, n), 1)
        cols = [jnp.broadcast_to(rest[:, start + j : start + j + 1], shape) for j in range(8)]
        for j in range(8):
            inverse = 1.0 / cols[j][j : j + 1, :]
            below = jnp.where(row > j, cols[j], 0.0)
            scaled = jnp.where(lane_row == start + j, inverse, rest[j : j + 1, :] * inverse)
            rest = jnp.where((lane == start + j) & (row > j), 0.0, rest) - below * scaled
            for k in range(j + 1, 8):
                cols[k] = cols[k] - below * (cols[k][j : j + 1, :] * inverse)
        done.append(rest[:8, :])
        rest = rest[8:, :]
    full = jnp.concatenate(done, axis=0)
    row = lax.broadcasted_iota(jnp.int32, (n, n), 0)
    lane = lax.broadcasted_iota(jnp.int32, (n, n), 1)
    pivots = jnp.sum(jnp.where(row == lane, full, 0.0), axis=1, keepdims=True)
    unit = jnp.where(row > lane, full, jnp.where(row == lane, 1.0, 0.0))
    return unit * (1.0 / jnp.sqrt(pivots))


def factor(gram_ref, out_ref):
    half = gram_ref.shape[0] // 2
    upper = unit_inverse(gram_ref[:half, :half])
    side = dot(gram_ref[half:, :half], upper, OVER_COLS, HIGHEST)
    lower = unit_inverse(gram_ref[half:, half:] - dot(side, side, OVER_COLS, HIGHEST))
    out_ref[:half, :half] = upper
    out_ref[:half, half:] = jnp.zeros((half, half), f32)
    out_ref[half:, :half] = -dot(dot(lower, side, precision=HIGHEST), upper, precision=HIGHEST)
    out_ref[half:, half:] = lower


def halves_kernel(table_ref, mine_ref, theirs_ref, *refs):
    half = mine_ref.shape[0]
    out_ref, gram_ref = refs[-2:]
    gram_ref[pl.ds(pl.multiple_of(table_ref[0] * half, half), half), :] = mine_ref[...]
    gram_ref[pl.ds(pl.multiple_of((1 - table_ref[0]) * half, half), half), :] = theirs_ref[...]
    factor(gram_ref, out_ref)


def factor_inverse(table, mine, theirs, after=()):
    comp = mine.shape[1]
    return pl.pallas_call(
        halves_kernel,
        out_shape=jax.ShapeDtypeStruct((comp, comp), f32),
        in_specs=[pl.BlockSpec(memory_space=pltpu.SMEM)]
        + [pl.BlockSpec(memory_space=pltpu.VMEM)] * 2
        + [pl.BlockSpec(memory_space=pl.ANY)] * len(after),
        scratch_shapes=[pltpu.VMEM((comp, comp), f32)],
        compiler_params=LIMIT,
        cost_estimate=pl.CostEstimate(flops=10**10, bytes_accessed=8 * comp * comp, transcendentals=0),
    )(table, mine, theirs, *after)


def solve_rows(cross, inverse):
    return dot(dot(cross, inverse, OVER_COLS, HIGHEST), inverse, precision=HIGHEST)


def plain(acts, dictionary, codes, split):
    tokens = acts.shape[0]
    sums = lax.psum(project(acts, dictionary), "hid")
    codes_mid = refine(codes, sums[:tokens], sums[tokens:])
    codes_low = codes_mid.astype(bf16)
    cross = dot(acts, codes_low, OVER_ROWS)
    gram_codes = lax.psum(dot(codes_low, codes_low, OVER_ROWS), "tok")
    half = gram_codes.shape[0] // 2
    if split:
        mine = solve_rows(lax.psum_scatter(cross, "tok", tiled=True), factor_inverse(jnp.zeros((1,), jnp.int32), gram_codes[:half], gram_codes[half:]))
        dict_out = lax.all_gather(mine, "tok", tiled=True)
    else:
        dict_out = solve_rows(lax.psum(cross, "tok"), factor_inverse(jnp.zeros((1,), jnp.int32), gram_codes[:half], gram_codes[half:]))
    gram_part = dot(dict_out, dict_out, OVER_ROWS, HIGHEST)
    proj_two, gram_new = lax.psum((dot(acts, dict_out.astype(bf16)), gram_part), "hid")
    return refine(codes_mid, proj_two, gram_new), dict_out


def update(codes, sums, tokens, precision=HIGHEST):
    proj, gram = sums[:tokens], sums[tokens:]
    numer = jnp.maximum(proj, 0.0) + dot(codes, jnp.maximum(-gram, 0.0), precision=precision)
    denom = jnp.maximum(-proj, 0.0) + dot(codes, jnp.maximum(gram, 0.0), precision=precision)
    return codes * jnp.sqrt(numer / jnp.maximum(denom, floor_value))


def first_kernel(core_ref, codes_ref, mine_ref, theirs_ref, mid_ref, low_ref, gram_ref):
    mid = update(codes_ref[...], mine_ref[...] + theirs_ref[...], codes_ref.shape[0])
    low = mid.astype(bf16)
    mid_ref[...] = mid
    low_ref[...] = low
    half = low.shape[1] // 2
    side = jnp.where(core_ref[0] == 0, mid[:, :half], mid[:, half:]).astype(bf16)
    gram_ref[...] = dot(side.T, low)


def first_update(core, codes, mine, theirs):
    tokens, comp = codes.shape
    whole = pl.BlockSpec(memory_space=pltpu.VMEM)
    return pl.pallas_call(
        first_kernel,
        out_shape=[
            jax.ShapeDtypeStruct((tokens, comp), f32),
            jax.ShapeDtypeStruct((tokens, comp), bf16),
            jax.ShapeDtypeStruct((comp // 2, comp), f32),
        ],
        in_specs=[pl.BlockSpec(memory_space=pltpu.SMEM), whole, whole, whole],
        out_specs=[whole, whole, whole],
        compiler_params=LIMIT,
    )(core, codes, mine, theirs)


def second_kernel(codes_ref, mine_ref, theirs_ref, out_ref):
    out_ref[...] = update(codes_ref[...], mine_ref[...] + theirs_ref[...], codes_ref.shape[0])


def second_update(codes, mine, theirs):
    return pl.pallas_call(
        second_kernel,
        out_shape=jax.ShapeDtypeStruct(codes.shape, f32),
        compiler_params=LIMIT,
    )(codes, mine, theirs)


WHOLE = pl.BlockSpec(memory_space=pltpu.VMEM)
SCALARS = pl.BlockSpec(memory_space=pltpu.SMEM)
ANYWHERE = pl.BlockSpec(memory_space=pl.ANY)
TILE = 128


def call(kernel, out_shapes, table, values, after):
    return pl.pallas_call(
        kernel,
        out_shape=out_shapes,
        in_specs=[SCALARS] + [WHOLE] * len(values) + [ANYWHERE] * len(after),
        out_specs=[WHOLE] * len(out_shapes),
        compiler_params=LIMIT,
    )(table, *values, *after)


def shape(rows, comp):
    return jax.ShapeDtypeStruct((rows, comp), f32)


def first_fold_kernel(at, table_ref, mine_ref, theirs_ref, gram_ref, *refs):
    whole = mine_ref.shape[0]
    rows = whole // 2
    keep = pl.ds(pl.multiple_of(table_ref[at] * rows, rows), rows)
    give = pl.ds(pl.multiple_of((1 - table_ref[at]) * rows, rows), rows)
    gram = gram_ref[...] + theirs_ref[whole:, :]
    refs[-2][:rows, :] = mine_ref[give, :] + theirs_ref[give, :]
    refs[-2][rows:, :] = gram
    refs[-1][:rows, :] = mine_ref[keep, :] + theirs_ref[keep, :]
    refs[-1][rows:, :] = gram


def first_fold(table, at, mine, theirs, gram):
    half = shape(mine.shape[0] // 2 + gram.shape[0], mine.shape[1])
    return call(functools.partial(first_fold_kernel, at), [half, half], table, [mine, theirs, gram], [])


def mixed_fold_kernel(at, extra, table_ref, mine_ref, theirs_ref, give_ref, keep_ref):
    whole = mine_ref.shape[0] - extra
    rows = whole // 2
    keep = pl.ds(pl.multiple_of(table_ref[at] * rows, rows), rows)
    give = pl.ds(pl.multiple_of((1 - table_ref[at]) * rows, rows), rows)
    gram = mine_ref[whole:, :] + theirs_ref[whole:, :]
    give_ref[:rows, :] = mine_ref[give, :] + theirs_ref[give, :]
    give_ref[rows:, :] = gram
    keep_ref[:rows, :] = mine_ref[keep, :] + theirs_ref[keep, :]
    keep_ref[rows:, :] = gram


def mixed_fold(table, at, extra, mine, theirs):
    half = shape((mine.shape[0] - extra) // 2 + extra, mine.shape[1])
    return call(functools.partial(mixed_fold_kernel, at, extra), [half, half], table, [mine, theirs], [])


def part_kernel(table_ref, mine_ref, theirs_ref, rows_ref, rest_ref):
    rows = rows_ref.shape[0]
    rows_ref[...] = mine_ref[:rows, :] + theirs_ref[:rows, :]
    rest_ref[...] = mine_ref[rows:, :] + theirs_ref[rows:, :]


def part(table, rows, mine, theirs):
    shapes = [shape(rows, mine.shape[1]), shape(mine.shape[0] - rows, mine.shape[1])]
    return call(part_kernel, shapes, table, [mine, theirs], [])


def take_kernel(at, count, table_ref, mine_ref, theirs_ref, *refs):
    which = 1 - table_ref[at]
    refs[-1][:count, :] = mine_ref[...] + theirs_ref[pl.ds(pl.multiple_of(which * count, count), count), :]
    if refs[-1].shape[0] > count:
        refs[-1][count:, :] = refs[0][...]


def take(table, at, mine, theirs, tail, after):
    count = mine.shape[0]
    rows = count + sum(value.shape[0] for value in tail)
    return call(functools.partial(take_kernel, at, count), [shape(rows, mine.shape[1])], table, [mine, theirs, *tail], after)[0]


def stack_kernel(table_ref, top_ref, rest_ref, *refs):
    count = top_ref.shape[0]
    refs[-1][:count, :] = top_ref[...]
    refs[-1][count:, :] = rest_ref[...]


def stack(table, top, rest, after):
    return call(stack_kernel, [shape(top.shape[0] + rest.shape[0], top.shape[1])], table, [top, rest], after)[0]


def rows_kernel(theirs, table_ref, inverse_ref, mine_ref, *refs):
    inverse = inverse_ref[...]
    cross = mine_ref[...]
    if theirs:
        cross = cross + refs[0][...]
    refs[-1][...] = dot(dot(cross, inverse, OVER_COLS, HIGHEST), inverse, precision=HIGHEST)


def solve_sum(table, inverse, parts, after):
    kernel = functools.partial(rows_kernel, len(parts) > 1)
    return call(kernel, [shape(*parts[0].shape)], table, [inverse, *parts], after)[0]


def absorb_kernel(ats, fresh, table_ref, acts_ref, *refs):
    count = len(ats)
    values, refs = refs[:count], refs[count:]
    if not fresh:
        sums_ref, refs = refs[0], refs[2:]
    out_ref, dict_ref = refs[:2]
    buffers, in_sem, out_sem = refs[2 : 2 + count], refs[2 + count], refs[3 + count]
    tokens = acts_ref.shape[0]
    ins, outs = [], []
    for k, value in enumerate(values):
        row = pl.multiple_of(table_ref[ats[k]] * TILE, TILE)
        rows = value.shape[0]
        ins.append(pltpu.make_async_copy(acts_ref.at[:, pl.ds(row, rows)], buffers[k], in_sem.at[k]))
        outs.append(pltpu.make_async_copy(value, dict_ref.at[pl.ds(row, rows), :], out_sem.at[k]))
        ins[k].start()
        outs[k].start()
    proj, gram = (0.0, 0.0) if fresh else (sums_ref[:tokens, :], sums_ref[tokens:, :])
    for k, value in enumerate(values):
        high = value[...].astype(bf16)
        gram = gram + dot(high.T, high)
        ins[k].wait()
        proj = proj + dot(buffers[k][...], high)
    out_ref[:tokens, :] = proj
    out_ref[tokens:, :] = gram
    for copy in outs:
        copy.wait()


def absorb(table, state, acts, blocks):
    tokens, hidden = acts.shape
    comp = blocks[0][0].shape[1]
    count = len(blocks)
    values = [value for value, _ in blocks]
    held = [] if state is None else list(state)
    total = sum(value.shape[0] for value in values)
    return pl.pallas_call(
        functools.partial(absorb_kernel, [at for _, at in blocks], state is None),
        out_shape=[shape(tokens + comp, comp), shape(hidden, comp)],
        in_specs=[SCALARS, ANYWHERE] + [WHOLE] * count + ([WHOLE, ANYWHERE] if held else []),
        out_specs=[WHOLE, ANYWHERE],
        scratch_shapes=[pltpu.VMEM((tokens, value.shape[0]), bf16) for value in values]
        + [pltpu.SemaphoreType.DMA((count,)), pltpu.SemaphoreType.DMA((count,))],
        input_output_aliases={2 + count: 0, 3 + count: 1} if held else {},
        compiler_params=LIMIT,
        cost_estimate=pl.CostEstimate(
            flops=2 * total * comp * (tokens + comp), bytes_accessed=total * (2 * tokens + 8 * comp), transcendentals=0
        ),
    )(table, acts, *values, *held)


def flips(bits):
    return [(t * 2 + c, (t ^ bits[c]) * 2 + c) for t in range(16) for c in range(2)]


X, Y, ZL, ZH = 1, 2, 4, 8
ALONG = {"first": (X, Y), "second": (Y, X), "near": (ZL, ZL), "far": (ZH, ZH)}
ORDERS = {
    "A": ("first", "second", "near", "far"),
    "N": ("near", "first", "second", "far"),
    "B": ("first", "near", "second", "far"),
}
SHARES = {"A": 4, "N": 5, "B": 5}
FIELDS = ("b", "c", "d", "mine", "theirs", "far_mine", "far_theirs")


def swap(value, along):
    return lax.ppermute(value, BOTH, flips(ALONG[along]))


def layout(hidden):
    unit = hidden // sum(SHARES.values())
    rows = {name: share * unit for name, share in SHARES.items()}
    table = np.zeros((32, 1 + len(FIELDS) * len(rows)), np.int32)
    where = {"core": 0}
    start, column = 0, 1
    for name, order in ORDERS.items():
        half, quarter = rows[name] // 2 // TILE, rows[name] // 4 // TILE
        for t in range(16):
            for core in range(2):
                a, b, c, d = (int(t & ALONG[along][core] != 0) for along in order)
                here, there = start + a * half, start + (1 - a) * half
                table[t * 2 + core, 0] = core
                table[t * 2 + core, column : column + len(FIELDS)] = (
                    b, c, d,
                    here + b * quarter, here + (1 - b) * quarter, there + b * quarter, there + (1 - b) * quarter,
                )
        for k, field in enumerate(FIELDS):
            where[name, field] = column + k
        start, column = start + 2 * half, column + len(FIELDS)
    return rows, table, where


def meshed(acts, dictionary, codes):
    hidden = acts.shape[1]
    tok, core = lax.axis_index("tok"), lax.axis_index("hid")
    rows, places, where = layout(hidden)
    table = lax.dynamic_slice_in_dim(jnp.asarray(places), tok * 2 + core, 1, 0).reshape(-1)

    def other_core(value):
        return lax.ppermute(value, "hid", [(0, 1), (1, 0)])

    sums = project(acts, dictionary)
    codes_mid, low, gram = first_update(table, codes, sums, other_core(sums))

    def bit(along):
        on_0, on_1 = ALONG[along]
        return jnp.where(core == 0, (tok & on_0) // on_0, (tok & on_1) // on_1)

    bits = {along: bit(along) for along in ALONG}
    starts, start = {}, 0
    for name in ORDERS:
        starts[name], start = start, start + rows[name]

    def cross_of(row, count):
        return dot(lax.dynamic_slice_in_dim(acts, row, count, 1), low, OVER_ROWS)

    def give_1(name):
        half = rows[name] // 2
        return cross_of(starts[name] + (1 - bits[ORDERS[name][0]]) * half, half)

    def own_2(name, keep):
        half, quarter = rows[name] // 2, rows[name] // 4
        a, b = (bits[along] for along in ORDERS[name][:2])
        return cross_of(starts[name] + a * half + (b if keep else 1 - b) * quarter, quarter)

    def part_of(value, which):
        half = value.shape[0] // 2
        return lax.dynamic_slice_in_dim(value, which * half, half, 0)

    def joined(one, other, which):
        return jnp.where(which == 0, jnp.concatenate([one, other]), jnp.concatenate([other, one]))

    held, last = {}, []
    first = {name: give_1(name) for name in ORDERS}
    first["A"] = stack(table, first["A"], gram, [first["N"]])
    for name, order in ORDERS.items():
        got = swap(first[name], order[0])
        tail = []
        if name == "A":
            gram = gram + got[rows[name] // 2 :]
            tail = [gram]
        give = take(table, where[name, "b"], own_2(name, False), got, tail, last)
        quarter = rows[name] // 4
        keep = own_2(name, True) + lax.dynamic_slice_in_dim(got, bits[order[1]] * quarter, quarter, 0)
        held[name], last = (keep, swap(give, order[1])), [give]
    for name, (keep, arrived) in held.items():
        along = ORDERS[name][2]
        if name == "A":
            give, keep = first_fold(table, where[name, "c"], keep, arrived, gram)
            held[name] = keep, swap(give, along)
        else:
            keep = keep + arrived
            held[name] = part_of(keep, bits[along]), swap(part_of(keep, 1 - bits[along]), along)
    for name, (keep, arrived) in held.items():
        along = ORDERS[name][3]
        if name == "A":
            give, keep = mixed_fold(table, where[name, "d"], gram.shape[0], keep, arrived)
            held[name] = keep, swap(give, along)
        else:
            keep = keep + arrived
            held[name] = part_of(keep, bits[along]), swap(part_of(keep, 1 - bits[along]), along)

    a_mine, gram = part(table, rows["A"] // 16, *held["A"])
    inverse = factor_inverse(table, gram, other_core(gram), [held["N"][0], held["B"][0]])
    held["A"] = (a_mine,)
    mine = {}
    for name in held:
        mine[name] = solve_sum(table, inverse, held[name], list(mine.values()))

    for k in (3, 2):
        for name in mine:
            along = ORDERS[name][k]
            mine[name] = joined(mine[name], swap(mine[name], along), bits[along])
    near, far, last = [], [], []
    for name in mine:
        theirs = swap(mine[name], ORDERS[name][1])
        near += [(mine[name], where[name, "mine"]), (theirs, where[name, "theirs"])]
        far += [(swap(mine[name], ORDERS[name][0]), where[name, "far_mine"])]
        last += [(swap(theirs, ORDERS[name][0]), where[name, "far_theirs"])]
    state = None
    for blocks in (near, far, last[::2], last[1:2]):
        state = absorb(table, state, acts, blocks)
    sums, dict_out = state
    return second_update(codes_mid, sums, other_core(sums)), dict_out


def solution(mesh):
    tok, hid = mesh.shape["tok"], mesh.shape["hid"]

    def per_device(acts, dictionary, codes):
        if tok == 16 and hid == 2 and acts.shape[1] % (14 * 512) == 0:
            return meshed(acts, dictionary, codes)
        return plain(acts, dictionary, codes, acts.shape[1] % tok == 0)

    return jax.shard_map(
        per_device,
        mesh=mesh,
        in_specs=(P("tok", "hid"), P("hid", None), P("tok", None)),
        out_specs=(P("tok", None), P("hid", None)),
        check_vma=False,
    )
```

```python
import functools

import jax
import jax.numpy as jnp
import numpy as np
from jax import lax
from jax.experimental import pallas as pl
from jax.experimental.pallas import tpu as pltpu
from jax.sharding import PartitionSpec as P

floor_value = 0.05
HIGHEST = lax.Precision.HIGHEST
f32, bf16 = jnp.float32, jnp.bfloat16
BOTH = ("tok", "hid")
OVER_ROWS = (((0,), (0,)), ((), ()))
OVER_COLS = (((1,), (1,)), ((), ()))
LIMIT = pltpu.CompilerParams(vmem_limit_bytes=48 * 2**20)


def dot(left, right, dims=(((1,), (0,)), ((), ())), precision=None):
    return lax.dot_general(left, right, dims, precision=precision, preferred_element_type=f32)


def refine(codes, proj, gram):
    gram_pos = jnp.maximum(gram, 0.0)
    gram_neg = jnp.maximum(-gram, 0.0)
    numer = jnp.maximum(proj, 0.0) + dot(codes, gram_neg, precision=HIGHEST)
    denom = jnp.maximum(jnp.maximum(-proj, 0.0) + dot(codes, gram_pos, precision=HIGHEST), floor_value)
    return codes * jnp.sqrt(numer / denom)


def project_kernel(acts_ref, dict_ref, out_ref, cross_ref):
    step = pl.program_id(0)
    tokens = acts_ref.shape[0]

    @pl.when(step == 0)
    def _():
        out_ref[...] = jnp.zeros_like(out_ref)
        cross_ref[...] = jnp.zeros_like(cross_ref)

    rows = dict_ref[...]
    high = rows.astype(bf16)
    low = (rows - high.astype(f32)).astype(bf16)
    out_ref[:tokens, :] += dot(acts_ref[...], high)
    turned = high.T
    out_ref[tokens:, :] += dot(turned, high)
    cross_ref[...] += dot(turned, low)

    @pl.when(step == pl.num_programs(0) - 1)
    def _():
        out_ref[tokens:, :] += cross_ref[...] + cross_ref[...].T


def project(acts, dictionary):
    tokens, hidden = acts.shape
    comp = dictionary.shape[1]
    tile = 1024 if hidden % 1024 == 0 else 512
    return pl.pallas_call(
        project_kernel,
        out_shape=jax.ShapeDtypeStruct((tokens + comp, comp), f32),
        grid=(hidden // tile,),
        in_specs=[
            pl.BlockSpec((tokens, tile), lambda i: (0, i)),
            pl.BlockSpec((tile, comp), lambda i: (i, 0)),
        ],
        out_specs=pl.BlockSpec((tokens + comp, comp), lambda i: (0, 0)),
        scratch_shapes=[pltpu.VMEM((comp, comp), f32)],
        compiler_params=LIMIT,
        cost_estimate=pl.CostEstimate(
            flops=2 * hidden * comp * (tokens + 2 * comp), bytes_accessed=hidden * (2 * tokens + 4 * comp), transcendentals=0
        ),
    )(acts, dictionary)


def unit_inverse(block):
    n = block.shape[0]
    done = []
    rest = block
    for start in range(0, n, 8):
        shape = rest.shape
        row = lax.broadcasted_iota(jnp.int32, shape, 0)
        lane = lax.broadcasted_iota(jnp.int32, shape, 1)
        lane_row = lax.broadcasted_iota(jnp.int32, (1, n), 1)
        cols = [jnp.broadcast_to(rest[:, start + j : start + j + 1], shape) for j in range(8)]
        for j in range(8):
            inverse = 1.0 / cols[j][j : j + 1, :]
            below = jnp.where(row > j, cols[j], 0.0)
            scaled = jnp.where(lane_row == start + j, inverse, rest[j : j + 1, :] * inverse)
            rest = jnp.where((lane == start + j) & (row > j), 0.0, rest) - below * scaled
            for k in range(j + 1, 8):
                cols[k] = cols[k] - below * (cols[k][j : j + 1, :] * inverse)
        done.append(rest[:8, :])
        rest = rest[8:, :]
    full = jnp.concatenate(done, axis=0)
    row = lax.broadcasted_iota(jnp.int32, (n, n), 0)
    lane = lax.broadcasted_iota(jnp.int32, (n, n), 1)
    pivots = jnp.sum(jnp.where(row == lane, full, 0.0), axis=1, keepdims=True)
    unit = jnp.where(row > lane, full, jnp.where(row == lane, 1.0, 0.0))
    return unit * (1.0 / jnp.sqrt(pivots))


def factor(gram_ref, out_ref):
    half = gram_ref.shape[0] // 2
    upper = unit_inverse(gram_ref[:half, :half])
    side = dot(gram_ref[half:, :half], upper, OVER_COLS, HIGHEST)
    lower = unit_inverse(gram_ref[half:, half:] - dot(side, side, OVER_COLS, HIGHEST))
    out_ref[:half, :half] = upper
    out_ref[:half, half:] = jnp.zeros((half, half), f32)
    out_ref[half:, :half] = -dot(dot(lower, side, precision=HIGHEST), upper, precision=HIGHEST)
    out_ref[half:, half:] = lower


def halves_kernel(table_ref, mine_ref, theirs_ref, *refs):
    half = mine_ref.shape[0]
    out_ref, gram_ref = refs[-2:]
    gram_ref[pl.ds(pl.multiple_of(table_ref[0] * half, half), half), :] = mine_ref[...]
    gram_ref[pl.ds(pl.multiple_of((1 - table_ref[0]) * half, half), half), :] = theirs_ref[...]
    factor(gram_ref, out_ref)


def factor_inverse(table, mine, theirs, after=()):
    comp = mine.shape[1]
    return pl.pallas_call(
        halves_kernel,
        out_shape=jax.ShapeDtypeStruct((comp, comp), f32),
        in_specs=[pl.BlockSpec(memory_space=pltpu.SMEM)]
        + [pl.BlockSpec(memory_space=pltpu.VMEM)] * 2
        + [pl.BlockSpec(memory_space=pl.ANY)] * len(after),
        scratch_shapes=[pltpu.VMEM((comp, comp), f32)],
        compiler_params=LIMIT,
        cost_estimate=pl.CostEstimate(flops=10**10, bytes_accessed=8 * comp * comp, transcendentals=0),
    )(table, mine, theirs, *after)


def solve_rows(cross, inverse):
    return dot(dot(cross, inverse, OVER_COLS, HIGHEST), inverse, precision=HIGHEST)


def plain(acts, dictionary, codes, split):
    tokens = acts.shape[0]
    sums = lax.psum(project(acts, dictionary), "hid")
    codes_mid = refine(codes, sums[:tokens], sums[tokens:])
    codes_low = codes_mid.astype(bf16)
    cross = dot(acts, codes_low, OVER_ROWS)
    gram_codes = lax.psum(dot(codes_low, codes_low, OVER_ROWS), "tok")
    half = gram_codes.shape[0] // 2
    if split:
        mine = solve_rows(lax.psum_scatter(cross, "tok", tiled=True), factor_inverse(jnp.zeros((1,), jnp.int32), gram_codes[:half], gram_codes[half:]))
        dict_out = lax.all_gather(mine, "tok", tiled=True)
    else:
        dict_out = solve_rows(lax.psum(cross, "tok"), factor_inverse(jnp.zeros((1,), jnp.int32), gram_codes[:half], gram_codes[half:]))
    gram_part = dot(dict_out, dict_out, OVER_ROWS, HIGHEST)
    proj_two, gram_new = lax.psum((dot(acts, dict_out.astype(bf16)), gram_part), "hid")
    return refine(codes_mid, proj_two, gram_new), dict_out


def update(codes, sums, tokens, precision=HIGHEST):
    proj, gram = sums[:tokens], sums[tokens:]
    numer = jnp.maximum(proj, 0.0) + dot(codes, jnp.maximum(-gram, 0.0), precision=precision)
    denom = jnp.maximum(-proj, 0.0) + dot(codes, jnp.maximum(gram, 0.0), precision=precision)
    return codes * jnp.sqrt(numer / jnp.maximum(denom, floor_value))


def first_kernel(core_ref, codes_ref, mine_ref, theirs_ref, mid_ref, low_ref, gram_ref):
    mid = update(codes_ref[...], mine_ref[...] + theirs_ref[...], codes_ref.shape[0])
    low = mid.astype(bf16)
    mid_ref[...] = mid
    low_ref[...] = low
    half = low.shape[1] // 2
    side = jnp.where(core_ref[0] == 0, mid[:, :half], mid[:, half:]).astype(bf16)
    gram_ref[...] = dot(side.T, low)


def first_update(core, codes, mine, theirs):
    tokens, comp = codes.shape
    whole = pl.BlockSpec(memory_space=pltpu.VMEM)
    return pl.pallas_call(
        first_kernel,
        out_shape=[
            jax.ShapeDtypeStruct((tokens, comp), f32),
            jax.ShapeDtypeStruct((tokens, comp), bf16),
            jax.ShapeDtypeStruct((comp // 2, comp), f32),
        ],
        in_specs=[pl.BlockSpec(memory_space=pltpu.SMEM), whole, whole, whole],
        out_specs=[whole, whole, whole],
        compiler_params=LIMIT,
    )(core, codes, mine, theirs)


def second_kernel(codes_ref, mine_ref, theirs_ref, out_ref):
    out_ref[...] = update(codes_ref[...], mine_ref[...] + theirs_ref[...], codes_ref.shape[0])


def second_update(codes, mine, theirs):
    return pl.pallas_call(
        second_kernel,
        out_shape=jax.ShapeDtypeStruct(codes.shape, f32),
        compiler_params=LIMIT,
    )(codes, mine, theirs)


WHOLE = pl.BlockSpec(memory_space=pltpu.VMEM)
SCALARS = pl.BlockSpec(memory_space=pltpu.SMEM)
ANYWHERE = pl.BlockSpec(memory_space=pl.ANY)
TILE = 128


def call(kernel, out_shapes, table, values, after):
    return pl.pallas_call(
        kernel,
        out_shape=out_shapes,
        in_specs=[SCALARS] + [WHOLE] * len(values) + [ANYWHERE] * len(after),
        out_specs=[WHOLE] * len(out_shapes),
        compiler_params=LIMIT,
    )(table, *values, *after)


def shape(rows, comp):
    return jax.ShapeDtypeStruct((rows, comp), f32)


def first_fold_kernel(at, table_ref, mine_ref, theirs_ref, gram_ref, *refs):
    whole = mine_ref.shape[0]
    rows = whole // 2
    keep = pl.ds(pl.multiple_of(table_ref[at] * rows, rows), rows)
    give = pl.ds(pl.multiple_of((1 - table_ref[at]) * rows, rows), rows)
    gram = gram_ref[...] + theirs_ref[whole:, :]
    refs[-2][:rows, :] = mine_ref[give, :] + theirs_ref[give, :]
    refs[-2][rows:, :] = gram
    refs[-1][:rows, :] = mine_ref[keep, :] + theirs_ref[keep, :]
    refs[-1][rows:, :] = gram


def first_fold(table, at, mine, theirs, gram):
    half = shape(mine.shape[0] // 2 + gram.shape[0], mine.shape[1])
    return call(functools.partial(first_fold_kernel, at), [half, half], table, [mine, theirs, gram], [])


def mixed_fold_kernel(at, extra, table_ref, mine_ref, theirs_ref, give_ref, keep_ref):
    whole = mine_ref.shape[0] - extra
    rows = whole // 2
    keep = pl.ds(pl.multiple_of(table_ref[at] * rows, rows), rows)
    give = pl.ds(pl.multiple_of((1 - table_ref[at]) * rows, rows), rows)
    gram = mine_ref[whole:, :] + theirs_ref[whole:, :]
    give_ref[:rows, :] = mine_ref[give, :] + theirs_ref[give, :]
    give_ref[rows:, :] = gram
    keep_ref[:rows, :] = mine_ref[keep, :] + theirs_ref[keep, :]
    keep_ref[rows:, :] = gram


def mixed_fold(table, at, extra, mine, theirs):
    half = shape((mine.shape[0] - extra) // 2 + extra, mine.shape[1])
    return call(functools.partial(mixed_fold_kernel, at, extra), [half, half], table, [mine, theirs], [])


def part_kernel(table_ref, mine_ref, theirs_ref, rows_ref, rest_ref):
    rows = rows_ref.shape[0]
    rows_ref[...] = mine_ref[:rows, :] + theirs_ref[:rows, :]
    rest_ref[...] = mine_ref[rows:, :] + theirs_ref[rows:, :]


def part(table, rows, mine, theirs):
    shapes = [shape(rows, mine.shape[1]), shape(mine.shape[0] - rows, mine.shape[1])]
    return call(part_kernel, shapes, table, [mine, theirs], [])


def take_kernel(at, count, table_ref, mine_ref, theirs_ref, *refs):
    which = 1 - table_ref[at]
    refs[-1][:count, :] = mine_ref[...] + theirs_ref[pl.ds(pl.multiple_of(which * count, count), count), :]
    if refs[-1].shape[0] > count:
        refs[-1][count:, :] = refs[0][...]


def take(table, at, mine, theirs, tail, after):
    count = mine.shape[0]
    rows = count + sum(value.shape[0] for value in tail)
    return call(functools.partial(take_kernel, at, count), [shape(rows, mine.shape[1])], table, [mine, theirs, *tail], after)[0]


def stack_kernel(table_ref, top_ref, rest_ref, *refs):
    count = top_ref.shape[0]
    refs[-1][:count, :] = top_ref[...]
    refs[-1][count:, :] = rest_ref[...]


def stack(table, top, rest, after):
    return call(stack_kernel, [shape(top.shape[0] + rest.shape[0], top.shape[1])], table, [top, rest], after)[0]


def rows_kernel(theirs, table_ref, inverse_ref, mine_ref, *refs):
    inverse = inverse_ref[...]
    cross = mine_ref[...]
    if theirs:
        cross = cross + refs[0][...]
    refs[-1][...] = dot(dot(cross, inverse, OVER_COLS, HIGHEST), inverse, precision=HIGHEST)


def solve_sum(table, inverse, parts, after):
    kernel = functools.partial(rows_kernel, len(parts) > 1)
    return call(kernel, [shape(*parts[0].shape)], table, [inverse, *parts], after)[0]


def absorb_kernel(ats, fresh, table_ref, acts_ref, *refs):
    count = len(ats)
    values, refs = refs[:count], refs[count:]
    if not fresh:
        sums_ref, refs = refs[0], refs[2:]
    out_ref, dict_ref = refs[:2]
    buffers, in_sem, out_sem = refs[2 : 2 + count], refs[2 + count], refs[3 + count]
    tokens = acts_ref.shape[0]
    ins, outs = [], []
    for k, value in enumerate(values):
        row = pl.multiple_of(table_ref[ats[k]] * TILE, TILE)
        rows = value.shape[0]
        ins.append(pltpu.make_async_copy(acts_ref.at[:, pl.ds(row, rows)], buffers[k], in_sem.at[k]))
        outs.append(pltpu.make_async_copy(value, dict_ref.at[pl.ds(row, rows), :], out_sem.at[k]))
        ins[k].start()
        outs[k].start()
    proj, gram = (0.0, 0.0) if fresh else (sums_ref[:tokens, :], sums_ref[tokens:, :])
    for k, value in enumerate(values):
        high = value[...].astype(bf16)
        gram = gram + dot(high.T, high)
        ins[k].wait()
        proj = proj + dot(buffers[k][...], high)
    out_ref[:tokens, :] = proj
    out_ref[tokens:, :] = gram
    for copy in outs:
        copy.wait()


def absorb(table, state, acts, blocks):
    tokens, hidden = acts.shape
    comp = blocks[0][0].shape[1]
    count = len(blocks)
    values = [value for value, _ in blocks]
    held = [] if state is None else list(state)
    total = sum(value.shape[0] for value in values)
    return pl.pallas_call(
        functools.partial(absorb_kernel, [at for _, at in blocks], state is None),
        out_shape=[shape(tokens + comp, comp), shape(hidden, comp)],
        in_specs=[SCALARS, ANYWHERE] + [WHOLE] * count + ([WHOLE, ANYWHERE] if held else []),
        out_specs=[WHOLE, ANYWHERE],
        scratch_shapes=[pltpu.VMEM((tokens, value.shape[0]), bf16) for value in values]
        + [pltpu.SemaphoreType.DMA((count,)), pltpu.SemaphoreType.DMA((count,))],
        input_output_aliases={2 + count: 0, 3 + count: 1} if held else {},
        compiler_params=LIMIT,
        cost_estimate=pl.CostEstimate(
            flops=2 * total * comp * (tokens + comp), bytes_accessed=total * (2 * tokens + 8 * comp), transcendentals=0
        ),
    )(table, acts, *values, *held)


def flips(bits):
    return [(t * 2 + c, (t ^ bits[c]) * 2 + c) for t in range(16) for c in range(2)]


X, Y, ZL, ZH = 1, 2, 4, 8
ALONG = {"first": (X, Y), "second": (Y, X), "near": (ZL, ZL), "far": (ZH, ZH)}
ORDERS = {
    "N": ("near", "first", "second", "far"),
    "B": ("first", "near", "second", "far"),
    "A": ("first", "second", "near", "far"),
}
SHARES = {"N": 5, "B": 5, "A": 4}
FIELDS = ("b", "c", "d", "mine", "theirs", "far_mine", "far_theirs")


def swap(value, along):
    return lax.ppermute(value, BOTH, flips(ALONG[along]))


def layout(hidden):
    unit = hidden // sum(SHARES.values())
    rows = {name: share * unit for name, share in SHARES.items()}
    table = np.zeros((32, 1 + len(FIELDS) * len(rows)), np.int32)
    where = {"core": 0}
    start, column = 0, 1
    for name, order in ORDERS.items():
        half, quarter = rows[name] // 2 // TILE, rows[name] // 4 // TILE
        for t in range(16):
            for core in range(2):
                a, b, c, d = (int(t & ALONG[along][core] != 0) for along in order)
                here, there = start + a * half, start + (1 - a) * half
                table[t * 2 + core, 0] = core
                table[t * 2 + core, column : column + len(FIELDS)] = (
                    b, c, d,
                    here + b * quarter, here + (1 - b) * quarter, there + b * quarter, there + (1 - b) * quarter,
                )
        for k, field in enumerate(FIELDS):
            where[name, field] = column + k
        start, column = start + 2 * half, column + len(FIELDS)
    return rows, table, where


def meshed(acts, dictionary, codes):
    hidden = acts.shape[1]
    tok, core = lax.axis_index("tok"), lax.axis_index("hid")
    rows, places, where = layout(hidden)
    table = lax.dynamic_slice_in_dim(jnp.asarray(places), tok * 2 + core, 1, 0).reshape(-1)

    def other_core(value):
        return lax.ppermute(value, "hid", [(0, 1), (1, 0)])

    sums = project(acts, dictionary)
    codes_mid, low, gram = first_update(table, codes, sums, other_core(sums))

    def bit(along):
        on_0, on_1 = ALONG[along]
        return jnp.where(core == 0, (tok & on_0) // on_0, (tok & on_1) // on_1)

    bits = {along: bit(along) for along in ALONG}
    starts, start = {}, 0
    for name in ORDERS:
        starts[name], start = start, start + rows[name]

    def cross_of(row, count):
        return dot(lax.dynamic_slice_in_dim(acts, row, count, 1), low, OVER_ROWS)

    def give_1(name):
        half = rows[name] // 2
        return cross_of(starts[name] + (1 - bits[ORDERS[name][0]]) * half, half)

    def own_2(name, keep):
        half, quarter = rows[name] // 2, rows[name] // 4
        a, b = (bits[along] for along in ORDERS[name][:2])
        return cross_of(starts[name] + a * half + (b if keep else 1 - b) * quarter, quarter)

    def part_of(value, which):
        half = value.shape[0] // 2
        return lax.dynamic_slice_in_dim(value, which * half, half, 0)

    def joined(one, other, which):
        return jnp.where(which == 0, jnp.concatenate([one, other]), jnp.concatenate([other, one]))

    held, last = {}, []
    first = {name: give_1(name) for name in ORDERS}
    first["A"] = stack(table, first["A"], gram, [first["N"]])
    for name, order in ORDERS.items():
        got = swap(first[name], order[0])
        tail = []
        if name == "A":
            gram = gram + got[rows[name] // 2 :]
            tail = [gram]
        give = take(table, where[name, "b"], own_2(name, False), got, tail, last)
        quarter = rows[name] // 4
        keep = own_2(name, True) + lax.dynamic_slice_in_dim(got, bits[order[1]] * quarter, quarter, 0)
        held[name], last = (keep, swap(give, order[1])), [give]
    for name, (keep, arrived) in held.items():
        along = ORDERS[name][2]
        if name == "A":
            give, keep = first_fold(table, where[name, "c"], keep, arrived, gram)
            held[name] = keep, swap(give, along)
        else:
            keep = keep + arrived
            held[name] = part_of(keep, bits[along]), swap(part_of(keep, 1 - bits[along]), along)
    for name, (keep, arrived) in held.items():
        along = ORDERS[name][3]
        if name == "A":
            give, keep = mixed_fold(table, where[name, "d"], gram.shape[0], keep, arrived)
            held[name] = keep, swap(give, along)
        else:
            keep = keep + arrived
            held[name] = part_of(keep, bits[along]), swap(part_of(keep, 1 - bits[along]), along)

    a_mine, gram = part(table, rows["A"] // 16, *held["A"])
    inverse = factor_inverse(table, gram, other_core(gram), [held["N"][0], held["B"][0]])
    held["A"] = (a_mine,)
    mine = {}
    for name in held:
        mine[name] = solve_sum(table, inverse, held[name], list(mine.values()))

    for k in (3, 2):
        for name in mine:
            along = ORDERS[name][k]
            mine[name] = joined(mine[name], swap(mine[name], along), bits[along])
    near, far, last = [], [], []
    for name in mine:
        theirs = swap(mine[name], ORDERS[name][1])
        near += [(mine[name], where[name, "mine"]), (theirs, where[name, "theirs"])]
        far += [(swap(mine[name], ORDERS[name][0]), where[name, "far_mine"])]
        last += [(swap(theirs, ORDERS[name][0]), where[name, "far_theirs"])]
    state = None
    for blocks in (near, far, [last[1], last[2]], [last[0]]):
        state = absorb(table, state, acts, blocks)
    sums, dict_out = state
    return second_update(codes_mid, sums, other_core(sums)), dict_out


def solution(mesh):
    tok, hid = mesh.shape["tok"], mesh.shape["hid"]

    def per_device(acts, dictionary, codes):
        if tok == 16 and hid == 2 and acts.shape[1] % (14 * 512) == 0:
            return meshed(acts, dictionary, codes)
        return plain(acts, dictionary, codes, acts.shape[1] % tok == 0)

    return jax.shard_map(
        per_device,
        mesh=mesh,
        in_specs=(P("tok", "hid"), P("hid", None), P("tok", None)),
        out_specs=(P("tok", None), P("hid", None)),
        check_vma=False,
    )
```

```python
import functools

import jax
import jax.numpy as jnp
import numpy as np
from jax import lax
from jax.experimental import pallas as pl
from jax.experimental.pallas import tpu as pltpu
from jax.sharding import PartitionSpec as P

floor_value = 0.05
HIGHEST = lax.Precision.HIGHEST
f32, bf16 = jnp.float32, jnp.bfloat16
BOTH = ("tok", "hid")
OVER_ROWS = (((0,), (0,)), ((), ()))
OVER_COLS = (((1,), (1,)), ((), ()))
LIMIT = pltpu.CompilerParams(vmem_limit_bytes=48 * 2**20)


def dot(left, right, dims=(((1,), (0,)), ((), ())), precision=None):
    return lax.dot_general(left, right, dims, precision=precision, preferred_element_type=f32)


def refine(codes, proj, gram):
    gram_pos = jnp.maximum(gram, 0.0)
    gram_neg = jnp.maximum(-gram, 0.0)
    numer = jnp.maximum(proj, 0.0) + dot(codes, gram_neg, precision=HIGHEST)
    denom = jnp.maximum(jnp.maximum(-proj, 0.0) + dot(codes, gram_pos, precision=HIGHEST), floor_value)
    return codes * jnp.sqrt(numer / denom)


def project_kernel(acts_ref, dict_ref, out_ref, cross_ref):
    step = pl.program_id(0)
    tokens = acts_ref.shape[0]

    @pl.when(step == 0)
    def _():
        out_ref[...] = jnp.zeros_like(out_ref)
        cross_ref[...] = jnp.zeros_like(cross_ref)

    rows = dict_ref[...]
    high = rows.astype(bf16)
    low = (rows - high.astype(f32)).astype(bf16)
    out_ref[:tokens, :] += dot(acts_ref[...], high)
    turned = high.T
    out_ref[tokens:, :] += dot(turned, high)
    cross_ref[...] += dot(turned, low)

    @pl.when(step == pl.num_programs(0) - 1)
    def _():
        out_ref[tokens:, :] += cross_ref[...] + cross_ref[...].T


def project(acts, dictionary):
    tokens, hidden = acts.shape
    comp = dictionary.shape[1]
    tile = 1024 if hidden % 1024 == 0 else 512
    return pl.pallas_call(
        project_kernel,
        out_shape=jax.ShapeDtypeStruct((tokens + comp, comp), f32),
        grid=(hidden // tile,),
        in_specs=[
            pl.BlockSpec((tokens, tile), lambda i: (0, i)),
            pl.BlockSpec((tile, comp), lambda i: (i, 0)),
        ],
        out_specs=pl.BlockSpec((tokens + comp, comp), lambda i: (0, 0)),
        scratch_shapes=[pltpu.VMEM((comp, comp), f32)],
        compiler_params=LIMIT,
        cost_estimate=pl.CostEstimate(
            flops=2 * hidden * comp * (tokens + 2 * comp), bytes_accessed=hidden * (2 * tokens + 4 * comp), transcendentals=0
        ),
    )(acts, dictionary)


def unit_inverse(block):
    n = block.shape[0]
    done = []
    rest = block
    for start in range(0, n, 8):
        shape = rest.shape
        row = lax.broadcasted_iota(jnp.int32, shape, 0)
        lane = lax.broadcasted_iota(jnp.int32, shape, 1)
        lane_row = lax.broadcasted_iota(jnp.int32, (1, n), 1)
        cols = [jnp.broadcast_to(rest[:, start + j : start + j + 1], shape) for j in range(8)]
        for j in range(8):
            inverse = 1.0 / cols[j][j : j + 1, :]
            below = jnp.where(row > j, cols[j], 0.0)
            scaled = jnp.where(lane_row == start + j, inverse, rest[j : j + 1, :] * inverse)
            rest = jnp.where((lane == start + j) & (row > j), 0.0, rest) - below * scaled
            for k in range(j + 1, 8):
                cols[k] = cols[k] - below * (cols[k][j : j + 1, :] * inverse)
        done.append(rest[:8, :])
        rest = rest[8:, :]
    full = jnp.concatenate(done, axis=0)
    row = lax.broadcasted_iota(jnp.int32, (n, n), 0)
    lane = lax.broadcasted_iota(jnp.int32, (n, n), 1)
    pivots = jnp.sum(jnp.where(row == lane, full, 0.0), axis=1, keepdims=True)
    unit = jnp.where(row > lane, full, jnp.where(row == lane, 1.0, 0.0))
    return unit * (1.0 / jnp.sqrt(pivots))


def factor(gram_ref, out_ref):
    half = gram_ref.shape[0] // 2
    upper = unit_inverse(gram_ref[:half, :half])
    side = dot(gram_ref[half:, :half], upper, OVER_COLS, HIGHEST)
    lower = unit_inverse(gram_ref[half:, half:] - dot(side, side, OVER_COLS, HIGHEST))
    out_ref[:half, :half] = upper
    out_ref[:half, half:] = jnp.zeros((half, half), f32)
    out_ref[half:, :half] = -dot(dot(lower, side, precision=HIGHEST), upper, precision=HIGHEST)
    out_ref[half:, half:] = lower


def halves_kernel(table_ref, mine_ref, theirs_ref, *refs):
    half = mine_ref.shape[0]
    out_ref, gram_ref = refs[-2:]
    gram_ref[pl.ds(pl.multiple_of(table_ref[0] * half, half), half), :] = mine_ref[...]
    gram_ref[pl.ds(pl.multiple_of((1 - table_ref[0]) * half, half), half), :] = theirs_ref[...]
    factor(gram_ref, out_ref)


def factor_inverse(table, mine, theirs, after=()):
    comp = mine.shape[1]
    return pl.pallas_call(
        halves_kernel,
        out_shape=jax.ShapeDtypeStruct((comp, comp), f32),
        in_specs=[pl.BlockSpec(memory_space=pltpu.SMEM)]
        + [pl.BlockSpec(memory_space=pltpu.VMEM)] * 2
        + [pl.BlockSpec(memory_space=pl.ANY)] * len(after),
        scratch_shapes=[pltpu.VMEM((comp, comp), f32)],
        compiler_params=LIMIT,
        cost_estimate=pl.CostEstimate(flops=10**10, bytes_accessed=8 * comp * comp, transcendentals=0),
    )(table, mine, theirs, *after)


def solve_rows(cross, inverse):
    return dot(dot(cross, inverse, OVER_COLS, HIGHEST), inverse, precision=HIGHEST)


def plain(acts, dictionary, codes, split):
    tokens = acts.shape[0]
    sums = lax.psum(project(acts, dictionary), "hid")
    codes_mid = refine(codes, sums[:tokens], sums[tokens:])
    codes_low = codes_mid.astype(bf16)
    cross = dot(acts, codes_low, OVER_ROWS)
    gram_codes = lax.psum(dot(codes_low, codes_low, OVER_ROWS), "tok")
    half = gram_codes.shape[0] // 2
    if split:
        mine = solve_rows(lax.psum_scatter(cross, "tok", tiled=True), factor_inverse(jnp.zeros((1,), jnp.int32), gram_codes[:half], gram_codes[half:]))
        dict_out = lax.all_gather(mine, "tok", tiled=True)
    else:
        dict_out = solve_rows(lax.psum(cross, "tok"), factor_inverse(jnp.zeros((1,), jnp.int32), gram_codes[:half], gram_codes[half:]))
    gram_part = dot(dict_out, dict_out, OVER_ROWS, HIGHEST)
    proj_two, gram_new = lax.psum((dot(acts, dict_out.astype(bf16)), gram_part), "hid")
    return refine(codes_mid, proj_two, gram_new), dict_out


def update(codes, sums, tokens, precision=HIGHEST):
    proj, gram = sums[:tokens], sums[tokens:]
    numer = jnp.maximum(proj, 0.0) + dot(codes, jnp.maximum(-gram, 0.0), precision=precision)
    denom = jnp.maximum(-proj, 0.0) + dot(codes, jnp.maximum(gram, 0.0), precision=precision)
    return codes * jnp.sqrt(numer / jnp.maximum(denom, floor_value))


def first_kernel(core_ref, codes_ref, mine_ref, theirs_ref, mid_ref, low_ref, gram_ref):
    mid = update(codes_ref[...], mine_ref[...] + theirs_ref[...], codes_ref.shape[0])
    low = mid.astype(bf16)
    mid_ref[...] = mid
    low_ref[...] = low
    half = low.shape[1] // 2
    side = jnp.where(core_ref[0] == 0, mid[:, :half], mid[:, half:]).astype(bf16)
    gram_ref[...] = dot(side.T, low)


def first_update(core, codes, mine, theirs):
    tokens, comp = codes.shape
    whole = pl.BlockSpec(memory_space=pltpu.VMEM)
    return pl.pallas_call(
        first_kernel,
        out_shape=[
            jax.ShapeDtypeStruct((tokens, comp), f32),
            jax.ShapeDtypeStruct((tokens, comp), bf16),
            jax.ShapeDtypeStruct((comp // 2, comp), f32),
        ],
        in_specs=[pl.BlockSpec(memory_space=pltpu.SMEM), whole, whole, whole],
        out_specs=[whole, whole, whole],
        compiler_params=LIMIT,
    )(core, codes, mine, theirs)


def second_kernel(codes_ref, mine_ref, theirs_ref, out_ref):
    out_ref[...] = update(codes_ref[...], mine_ref[...] + theirs_ref[...], codes_ref.shape[0])


def second_update(codes, mine, theirs):
    return pl.pallas_call(
        second_kernel,
        out_shape=jax.ShapeDtypeStruct(codes.shape, f32),
        compiler_params=LIMIT,
    )(codes, mine, theirs)


WHOLE = pl.BlockSpec(memory_space=pltpu.VMEM)
SCALARS = pl.BlockSpec(memory_space=pltpu.SMEM)
ANYWHERE = pl.BlockSpec(memory_space=pl.ANY)
TILE = 128


def call(kernel, out_shapes, table, values, after):
    return pl.pallas_call(
        kernel,
        out_shape=out_shapes,
        in_specs=[SCALARS] + [WHOLE] * len(values) + [ANYWHERE] * len(after),
        out_specs=[WHOLE] * len(out_shapes),
        compiler_params=LIMIT,
    )(table, *values, *after)


def shape(rows, comp):
    return jax.ShapeDtypeStruct((rows, comp), f32)


def first_fold_kernel(at, table_ref, mine_ref, theirs_ref, gram_ref, *refs):
    whole = mine_ref.shape[0]
    rows = whole // 2
    keep = pl.ds(pl.multiple_of(table_ref[at] * rows, rows), rows)
    give = pl.ds(pl.multiple_of((1 - table_ref[at]) * rows, rows), rows)
    gram = gram_ref[...] + theirs_ref[whole:, :]
    refs[-2][:rows, :] = mine_ref[give, :] + theirs_ref[give, :]
    refs[-2][rows:, :] = gram
    refs[-1][:rows, :] = mine_ref[keep, :] + theirs_ref[keep, :]
    refs[-1][rows:, :] = gram


def first_fold(table, at, mine, theirs, gram):
    half = shape(mine.shape[0] // 2 + gram.shape[0], mine.shape[1])
    return call(functools.partial(first_fold_kernel, at), [half, half], table, [mine, theirs, gram], [])


def split_fold_kernel(at, table_ref, mine_ref, theirs_ref, give_ref, keep_ref, gram_ref):
    rows = give_ref.shape[0]
    keep = pl.ds(pl.multiple_of(table_ref[at] * rows, rows), rows)
    give = pl.ds(pl.multiple_of((1 - table_ref[at]) * rows, rows), rows)
    give_ref[...] = mine_ref[give, :] + theirs_ref[give, :]
    keep_ref[...] = mine_ref[keep, :] + theirs_ref[keep, :]
    gram_ref[...] = mine_ref[2 * rows :, :] + theirs_ref[2 * rows :, :]


def split_fold(table, at, extra, mine, theirs):
    comp = mine.shape[1]
    half = shape((mine.shape[0] - extra) // 2, comp)
    return call(functools.partial(split_fold_kernel, at), [half, half, shape(extra, comp)], table, [mine, theirs], [])


def take_kernel(at, count, table_ref, mine_ref, theirs_ref, *refs):
    which = 1 - table_ref[at]
    refs[-1][:count, :] = mine_ref[...] + theirs_ref[pl.ds(pl.multiple_of(which * count, count), count), :]
    if refs[-1].shape[0] > count:
        refs[-1][count:, :] = refs[0][...]


def take(table, at, mine, theirs, tail, after):
    count = mine.shape[0]
    rows = count + sum(value.shape[0] for value in tail)
    return call(functools.partial(take_kernel, at, count), [shape(rows, mine.shape[1])], table, [mine, theirs, *tail], after)[0]


def stack_kernel(table_ref, top_ref, rest_ref, *refs):
    count = top_ref.shape[0]
    refs[-1][:count, :] = top_ref[...]
    refs[-1][count:, :] = rest_ref[...]


def stack(table, top, rest, after):
    return call(stack_kernel, [shape(top.shape[0] + rest.shape[0], top.shape[1])], table, [top, rest], after)[0]


def rows_kernel(table_ref, inverse_ref, mine_ref, *refs):
    inverse = inverse_ref[...]
    cross = mine_ref[...] + refs[0][...]
    refs[-1][...] = dot(dot(cross, inverse, OVER_COLS, HIGHEST), inverse, precision=HIGHEST)


def solve_sum(table, inverse, parts, after):
    return call(rows_kernel, [shape(*parts[0].shape)], table, [inverse, *parts], after)[0]


def absorb_kernel(ats, fresh, table_ref, acts_ref, *refs):
    count = len(ats)
    values, refs = refs[:count], refs[count:]
    if not fresh:
        sums_ref, refs = refs[0], refs[2:]
    out_ref, dict_ref = refs[:2]
    buffers, in_sem, out_sem = refs[2 : 2 + count], refs[2 + count], refs[3 + count]
    tokens = acts_ref.shape[0]
    ins, outs = [], []
    for k, value in enumerate(values):
        row = pl.multiple_of(table_ref[ats[k]] * TILE, TILE)
        rows = value.shape[0]
        ins.append(pltpu.make_async_copy(acts_ref.at[:, pl.ds(row, rows)], buffers[k], in_sem.at[k]))
        outs.append(pltpu.make_async_copy(value, dict_ref.at[pl.ds(row, rows), :], out_sem.at[k]))
        ins[k].start()
        outs[k].start()
    proj, gram = (0.0, 0.0) if fresh else (sums_ref[:tokens, :], sums_ref[tokens:, :])
    for k, value in enumerate(values):
        block = value[...]
        high = block.astype(bf16)
        low = (block - high.astype(f32)).astype(bf16)
        turned = high.T
        cross = dot(turned, low)
        gram = gram + (dot(turned, high) + (cross + cross.T))
        ins[k].wait()
        proj = proj + dot(buffers[k][...], high)
    out_ref[:tokens, :] = proj
    out_ref[tokens:, :] = gram
    for copy in outs:
        copy.wait()


def absorb(table, state, acts, blocks):
    tokens, hidden = acts.shape
    comp = blocks[0][0].shape[1]
    count = len(blocks)
    values = [value for value, _ in blocks]
    held = [] if state is None else list(state)
    total = sum(value.shape[0] for value in values)
    return pl.pallas_call(
        functools.partial(absorb_kernel, [at for _, at in blocks], state is None),
        out_shape=[shape(tokens + comp, comp), shape(hidden, comp)],
        in_specs=[SCALARS, ANYWHERE] + [WHOLE] * count + ([WHOLE, ANYWHERE] if held else []),
        out_specs=[WHOLE, ANYWHERE],
        scratch_shapes=[pltpu.VMEM((tokens, value.shape[0]), bf16) for value in values]
        + [pltpu.SemaphoreType.DMA((count,)), pltpu.SemaphoreType.DMA((count,))],
        input_output_aliases={2 + count: 0, 3 + count: 1} if held else {},
        compiler_params=LIMIT,
        cost_estimate=pl.CostEstimate(
            flops=2 * total * comp * (tokens + comp), bytes_accessed=total * (2 * tokens + 8 * comp), transcendentals=0
        ),
    )(table, acts, *values, *held)


def flips(bits):
    return [(t * 2 + c, (t ^ bits[c]) * 2 + c) for t in range(16) for c in range(2)]


X, Y, ZL, ZH = 1, 2, 4, 8
ALONG = {"first": (X, Y), "second": (Y, X), "near": (ZL, ZL), "far": (ZH, ZH)}
ORDERS = {
    "N": ("near", "first", "second", "far"),
    "B": ("first", "near", "second", "far"),
    "A": ("first", "second", "near", "far"),
}
SHARES = {"N": 5, "B": 5, "A": 4}
FIELDS = ("b", "c", "d", "mine", "theirs", "far_mine", "far_theirs")


def swap(value, along):
    return lax.ppermute(value, BOTH, flips(ALONG[along]))


def layout(hidden):
    unit = hidden // sum(SHARES.values())
    rows = {name: share * unit for name, share in SHARES.items()}
    table = np.zeros((32, 1 + len(FIELDS) * len(rows)), np.int32)
    where = {"core": 0}
    start, column = 0, 1
    for name, order in ORDERS.items():
        half, quarter = rows[name] // 2 // TILE, rows[name] // 4 // TILE
        for t in range(16):
            for core in range(2):
                a, b, c, d = (int(t & ALONG[along][core] != 0) for along in order)
                here, there = start + a * half, start + (1 - a) * half
                table[t * 2 + core, 0] = core
                table[t * 2 + core, column : column + len(FIELDS)] = (
                    b, c, d,
                    here + b * quarter, here + (1 - b) * quarter, there + b * quarter, there + (1 - b) * quarter,
                )
        for k, field in enumerate(FIELDS):
            where[name, field] = column + k
        start, column = start + 2 * half, column + len(FIELDS)
    return rows, table, where


def meshed(acts, dictionary, codes):
    hidden = acts.shape[1]
    tok, core = lax.axis_index("tok"), lax.axis_index("hid")
    rows, places, where = layout(hidden)
    table = lax.dynamic_slice_in_dim(jnp.asarray(places), tok * 2 + core, 1, 0).reshape(-1)

    def other_core(value):
        return lax.ppermute(value, "hid", [(0, 1), (1, 0)])

    sums = project(acts, dictionary)
    codes_mid, low, gram = first_update(table, codes, sums, other_core(sums))

    def bit(along):
        on_0, on_1 = ALONG[along]
        return jnp.where(core == 0, (tok & on_0) // on_0, (tok & on_1) // on_1)

    bits = {along: bit(along) for along in ALONG}
    starts, start = {}, 0
    for name in ORDERS:
        starts[name], start = start, start + rows[name]

    def cross_of(row, count):
        return dot(lax.dynamic_slice_in_dim(acts, row, count, 1), low, OVER_ROWS)

    def give_1(name):
        half = rows[name] // 2
        return cross_of(starts[name] + (1 - bits[ORDERS[name][0]]) * half, half)

    def own_2(name, keep):
        half, quarter = rows[name] // 2, rows[name] // 4
        a, b = (bits[along] for along in ORDERS[name][:2])
        return cross_of(starts[name] + a * half + (b if keep else 1 - b) * quarter, quarter)

    def part_of(value, which):
        half = value.shape[0] // 2
        return lax.dynamic_slice_in_dim(value, which * half, half, 0)

    def joined(one, other, which):
        return jnp.where(which == 0, jnp.concatenate([one, other]), jnp.concatenate([other, one]))

    held, last = {}, []
    first = {name: give_1(name) for name in ORDERS}
    first["A"] = stack(table, first["A"], gram, [first["N"]])
    for name, order in ORDERS.items():
        got = swap(first[name], order[0])
        tail = []
        if name == "A":
            gram = gram + got[rows[name] // 2 :]
            tail = [gram]
        give = take(table, where[name, "b"], own_2(name, False), got, tail, last)
        quarter = rows[name] // 4
        keep = own_2(name, True) + lax.dynamic_slice_in_dim(got, bits[order[1]] * quarter, quarter, 0)
        held[name], last = (keep, swap(give, order[1])), [give]
    for name, (keep, arrived) in held.items():
        along = ORDERS[name][2]
        if name == "A":
            give, keep = first_fold(table, where[name, "c"], keep, arrived, gram)
            held[name] = keep, swap(give, along)
        else:
            keep = keep + arrived
            held[name] = part_of(keep, bits[along]), swap(part_of(keep, 1 - bits[along]), along)
    for name, (keep, arrived) in held.items():
        along = ORDERS[name][3]
        if name == "A":
            give, keep, gram = split_fold(table, where[name, "d"], gram.shape[0], keep, arrived)
            gram = gram + swap(gram, along)
            held[name] = keep, swap(give, along)
        else:
            keep = keep + arrived
            held[name] = part_of(keep, bits[along]), swap(part_of(keep, 1 - bits[along]), along)

    inverse = factor_inverse(table, gram, other_core(gram), [held["N"][0], held["B"][0]])
    mine = {}
    for name in held:
        mine[name] = solve_sum(table, inverse, held[name], list(mine.values()))

    for k in (3, 2):
        for name in mine:
            along = ORDERS[name][k]
            mine[name] = joined(mine[name], swap(mine[name], along), bits[along])
    near, far, last = [], [], []
    for name in mine:
        theirs = swap(mine[name], ORDERS[name][1])
        near += [(mine[name], where[name, "mine"]), (theirs, where[name, "theirs"])]
        far += [(swap(mine[name], ORDERS[name][0]), where[name, "far_mine"])]
        last += [(swap(theirs, ORDERS[name][0]), where[name, "far_theirs"])]
    state = None
    for blocks in (near, far, [last[1], last[2]], [last[0]]):
        state = absorb(table, state, acts, blocks)
    sums, dict_out = state
    return second_update(codes_mid, sums, other_core(sums)), dict_out


def solution(mesh):
    tok, hid = mesh.shape["tok"], mesh.shape["hid"]

    def per_device(acts, dictionary, codes):
        if tok == 16 and hid == 2 and acts.shape[1] % (14 * 512) == 0:
            return meshed(acts, dictionary, codes)
        return plain(acts, dictionary, codes, acts.shape[1] % tok == 0)

    return jax.shard_map(
        per_device,
        mesh=mesh,
        in_specs=(P("tok", "hid"), P("hid", None), P("tok", None)),
        out_specs=(P("tok", None), P("hid", None)),
        check_vma=False,
    )
```

```python
import functools

import jax
import jax.numpy as jnp
import numpy as np
from jax import lax
from jax.experimental import pallas as pl
from jax.experimental.pallas import tpu as pltpu
from jax.sharding import PartitionSpec as P

floor_value = 0.05
HIGHEST = lax.Precision.HIGHEST
f32, bf16 = jnp.float32, jnp.bfloat16
BOTH = ("tok", "hid")
OVER_ROWS = (((0,), (0,)), ((), ()))
OVER_COLS = (((1,), (1,)), ((), ()))
LIMIT = pltpu.CompilerParams(vmem_limit_bytes=48 * 2**20)


def dot(left, right, dims=(((1,), (0,)), ((), ())), precision=None):
    return lax.dot_general(left, right, dims, precision=precision, preferred_element_type=f32)


def refine(codes, proj, gram):
    gram_pos = jnp.maximum(gram, 0.0)
    gram_neg = jnp.maximum(-gram, 0.0)
    numer = jnp.maximum(proj, 0.0) + dot(codes, gram_neg, precision=HIGHEST)
    denom = jnp.maximum(jnp.maximum(-proj, 0.0) + dot(codes, gram_pos, precision=HIGHEST), floor_value)
    return codes * jnp.sqrt(numer / denom)


def project_kernel(acts_ref, dict_ref, out_ref, cross_ref):
    step = pl.program_id(0)
    tokens = acts_ref.shape[0]

    @pl.when(step == 0)
    def _():
        out_ref[...] = jnp.zeros_like(out_ref)
        cross_ref[...] = jnp.zeros_like(cross_ref)

    rows = dict_ref[...]
    high = rows.astype(bf16)
    low = (rows - high.astype(f32)).astype(bf16)
    out_ref[:tokens, :] += dot(acts_ref[...], high)
    turned = high.T
    out_ref[tokens:, :] += dot(turned, high)
    cross_ref[...] += dot(turned, low)

    @pl.when(step == pl.num_programs(0) - 1)
    def _():
        out_ref[tokens:, :] += cross_ref[...] + cross_ref[...].T


def project(acts, dictionary):
    tokens, hidden = acts.shape
    comp = dictionary.shape[1]
    tile = 1024 if hidden % 1024 == 0 else 512
    return pl.pallas_call(
        project_kernel,
        out_shape=jax.ShapeDtypeStruct((tokens + comp, comp), f32),
        grid=(hidden // tile,),
        in_specs=[
            pl.BlockSpec((tokens, tile), lambda i: (0, i)),
            pl.BlockSpec((tile, comp), lambda i: (i, 0)),
        ],
        out_specs=pl.BlockSpec((tokens + comp, comp), lambda i: (0, 0)),
        scratch_shapes=[pltpu.VMEM((comp, comp), f32)],
        compiler_params=LIMIT,
        cost_estimate=pl.CostEstimate(
            flops=2 * hidden * comp * (tokens + 2 * comp), bytes_accessed=hidden * (2 * tokens + 4 * comp), transcendentals=0
        ),
    )(acts, dictionary)


def unit_inverse(block):
    n = block.shape[0]
    done = []
    rest = block
    for start in range(0, n, 8):
        shape = rest.shape
        row = lax.broadcasted_iota(jnp.int32, shape, 0)
        lane = lax.broadcasted_iota(jnp.int32, shape, 1)
        lane_row = lax.broadcasted_iota(jnp.int32, (1, n), 1)
        cols = [jnp.broadcast_to(rest[:, start + j : start + j + 1], shape) for j in range(8)]
        for j in range(8):
            inverse = 1.0 / cols[j][j : j + 1, :]
            below = jnp.where(row > j, cols[j], 0.0)
            scaled = jnp.where(lane_row == start + j, inverse, rest[j : j + 1, :] * inverse)
            rest = jnp.where((lane == start + j) & (row > j), 0.0, rest) - below * scaled
            for k in range(j + 1, 8):
                cols[k] = cols[k] - below * (cols[k][j : j + 1, :] * inverse)
        done.append(rest[:8, :])
        rest = rest[8:, :]
    full = jnp.concatenate(done, axis=0)
    row = lax.broadcasted_iota(jnp.int32, (n, n), 0)
    lane = lax.broadcasted_iota(jnp.int32, (n, n), 1)
    pivots = jnp.sum(jnp.where(row == lane, full, 0.0), axis=1, keepdims=True)
    unit = jnp.where(row > lane, full, jnp.where(row == lane, 1.0, 0.0))
    return unit * (1.0 / jnp.sqrt(pivots))


def factor(gram_ref, out_ref):
    half = gram_ref.shape[0] // 2
    upper = unit_inverse(gram_ref[:half, :half])
    side = dot(gram_ref[half:, :half], upper, OVER_COLS, HIGHEST)
    lower = unit_inverse(gram_ref[half:, half:] - dot(side, side, OVER_COLS, HIGHEST))
    out_ref[:half, :half] = upper
    out_ref[:half, half:] = jnp.zeros((half, half), f32)
    out_ref[half:, :half] = -dot(dot(lower, side, precision=HIGHEST), upper, precision=HIGHEST)
    out_ref[half:, half:] = lower


def halves_kernel(table_ref, mine_ref, theirs_ref, *refs):
    half = mine_ref.shape[0]
    out_ref, gram_ref = refs[-2:]
    gram_ref[pl.ds(pl.multiple_of(table_ref[0] * half, half), half), :] = mine_ref[...]
    gram_ref[pl.ds(pl.multiple_of((1 - table_ref[0]) * half, half), half), :] = theirs_ref[...]
    factor(gram_ref, out_ref)


def factor_inverse(table, mine, theirs, after=()):
    comp = mine.shape[1]
    return pl.pallas_call(
        halves_kernel,
        out_shape=jax.ShapeDtypeStruct((comp, comp), f32),
        in_specs=[pl.BlockSpec(memory_space=pltpu.SMEM)]
        + [pl.BlockSpec(memory_space=pltpu.VMEM)] * 2
        + [pl.BlockSpec(memory_space=pl.ANY)] * len(after),
        scratch_shapes=[pltpu.VMEM((comp, comp), f32)],
        compiler_params=LIMIT,
        cost_estimate=pl.CostEstimate(flops=10**10, bytes_accessed=8 * comp * comp, transcendentals=0),
    )(table, mine, theirs, *after)


def solve_rows(cross, inverse):
    return dot(dot(cross, inverse, OVER_COLS, HIGHEST), inverse, precision=HIGHEST)


def plain(acts, dictionary, codes, split):
    tokens = acts.shape[0]
    sums = lax.psum(project(acts, dictionary), "hid")
    codes_mid = refine(codes, sums[:tokens], sums[tokens:])
    codes_low = codes_mid.astype(bf16)
    cross = dot(acts, codes_low, OVER_ROWS)
    gram_codes = lax.psum(dot(codes_low, codes_low, OVER_ROWS), "tok")
    half = gram_codes.shape[0] // 2
    if split:
        mine = solve_rows(lax.psum_scatter(cross, "tok", tiled=True), factor_inverse(jnp.zeros((1,), jnp.int32), gram_codes[:half], gram_codes[half:]))
        dict_out = lax.all_gather(mine, "tok", tiled=True)
    else:
        dict_out = solve_rows(lax.psum(cross, "tok"), factor_inverse(jnp.zeros((1,), jnp.int32), gram_codes[:half], gram_codes[half:]))
    gram_part = dot(dict_out, dict_out, OVER_ROWS, HIGHEST)
    proj_two, gram_new = lax.psum((dot(acts, dict_out.astype(bf16)), gram_part), "hid")
    return refine(codes_mid, proj_two, gram_new), dict_out


def halves(value):
    high = value.astype(bf16)
    return high, (value - high.astype(f32)).astype(bf16)


def update(codes, sums, tokens):
    proj, gram = sums[:tokens], sums[tokens:]
    comp = gram.shape[1]
    high, low = halves(codes)
    gram_high, gram_low = halves(jnp.concatenate([jnp.maximum(-gram, 0.0), jnp.maximum(gram, 0.0)], axis=1))
    both = dot(high, gram_high) + (dot(high, gram_low) + dot(low, gram_high))
    numer = jnp.maximum(proj, 0.0) + both[:, :comp]
    denom = jnp.maximum(-proj, 0.0) + both[:, comp:]
    return codes * jnp.sqrt(numer / jnp.maximum(denom, floor_value))


def first_kernel(core_ref, codes_ref, mine_ref, theirs_ref, mid_ref, low_ref, gram_ref):
    mid = update(codes_ref[...], mine_ref[...] + theirs_ref[...], codes_ref.shape[0])
    low = mid.astype(bf16)
    mid_ref[...] = mid
    low_ref[...] = low
    half = low.shape[1] // 2
    side = jnp.where(core_ref[0] == 0, mid[:, :half], mid[:, half:]).astype(bf16)
    gram_ref[...] = dot(side.T, low)


def first_update(core, codes, mine, theirs):
    tokens, comp = codes.shape
    whole = pl.BlockSpec(memory_space=pltpu.VMEM)
    return pl.pallas_call(
        first_kernel,
        out_shape=[
            jax.ShapeDtypeStruct((tokens, comp), f32),
            jax.ShapeDtypeStruct((tokens, comp), bf16),
            jax.ShapeDtypeStruct((comp // 2, comp), f32),
        ],
        in_specs=[pl.BlockSpec(memory_space=pltpu.SMEM), whole, whole, whole],
        out_specs=[whole, whole, whole],
        compiler_params=LIMIT,
    )(core, codes, mine, theirs)


def second_kernel(codes_ref, mine_ref, theirs_ref, out_ref):
    out_ref[...] = update(codes_ref[...], mine_ref[...] + theirs_ref[...], codes_ref.shape[0])


def second_update(codes, mine, theirs):
    return pl.pallas_call(
        second_kernel,
        out_shape=jax.ShapeDtypeStruct(codes.shape, f32),
        compiler_params=LIMIT,
    )(codes, mine, theirs)


WHOLE = pl.BlockSpec(memory_space=pltpu.VMEM)
SCALARS = pl.BlockSpec(memory_space=pltpu.SMEM)
ANYWHERE = pl.BlockSpec(memory_space=pl.ANY)
TILE = 128


def call(kernel, out_shapes, table, values, after):
    return pl.pallas_call(
        kernel,
        out_shape=out_shapes,
        in_specs=[SCALARS] + [WHOLE] * len(values) + [ANYWHERE] * len(after),
        out_specs=[WHOLE] * len(out_shapes),
        compiler_params=LIMIT,
    )(table, *values, *after)


def shape(rows, comp):
    return jax.ShapeDtypeStruct((rows, comp), f32)


def first_fold_kernel(at, table_ref, mine_ref, theirs_ref, gram_ref, *refs):
    whole = mine_ref.shape[0]
    rows = whole // 2
    keep = pl.ds(pl.multiple_of(table_ref[at] * rows, rows), rows)
    give = pl.ds(pl.multiple_of((1 - table_ref[at]) * rows, rows), rows)
    gram = gram_ref[...] + theirs_ref[whole:, :]
    refs[-2][:rows, :] = mine_ref[give, :] + theirs_ref[give, :]
    refs[-2][rows:, :] = gram
    refs[-1][:rows, :] = mine_ref[keep, :] + theirs_ref[keep, :]
    refs[-1][rows:, :] = gram


def first_fold(table, at, mine, theirs, gram):
    half = shape(mine.shape[0] // 2 + gram.shape[0], mine.shape[1])
    return call(functools.partial(first_fold_kernel, at), [half, half], table, [mine, theirs, gram], [])


def split_fold_kernel(at, table_ref, mine_ref, theirs_ref, give_ref, keep_ref, gram_ref):
    rows = give_ref.shape[0]
    keep = pl.ds(pl.multiple_of(table_ref[at] * rows, rows), rows)
    give = pl.ds(pl.multiple_of((1 - table_ref[at]) * rows, rows), rows)
    give_ref[...] = mine_ref[give, :] + theirs_ref[give, :]
    keep_ref[...] = mine_ref[keep, :] + theirs_ref[keep, :]
    gram_ref[...] = mine_ref[2 * rows :, :] + theirs_ref[2 * rows :, :]


def split_fold(table, at, extra, mine, theirs):
    comp = mine.shape[1]
    half = shape((mine.shape[0] - extra) // 2, comp)
    return call(functools.partial(split_fold_kernel, at), [half, half, shape(extra, comp)], table, [mine, theirs], [])


def take_kernel(at, count, table_ref, mine_ref, theirs_ref, *refs):
    which = 1 - table_ref[at]
    refs[-1][:count, :] = mine_ref[...] + theirs_ref[pl.ds(pl.multiple_of(which * count, count), count), :]
    if refs[-1].shape[0] > count:
        refs[-1][count:, :] = refs[0][...]


def take(table, at, mine, theirs, tail, after):
    count = mine.shape[0]
    rows = count + sum(value.shape[0] for value in tail)
    return call(functools.partial(take_kernel, at, count), [shape(rows, mine.shape[1])], table, [mine, theirs, *tail], after)[0]


def stack_kernel(table_ref, top_ref, rest_ref, *refs):
    count = top_ref.shape[0]
    refs[-1][:count, :] = top_ref[...]
    refs[-1][count:, :] = rest_ref[...]


def stack(table, top, rest, after):
    return call(stack_kernel, [shape(top.shape[0] + rest.shape[0], top.shape[1])], table, [top, rest], after)[0]


def rows_kernel(table_ref, inverse_ref, mine_ref, *refs):
    inverse = inverse_ref[...]
    cross = mine_ref[...] + refs[0][...]
    refs[-1][...] = dot(dot(cross, inverse, OVER_COLS, HIGHEST), inverse, precision=HIGHEST)


def solve_sum(table, inverse, parts, after):
    return call(rows_kernel, [shape(*parts[0].shape)], table, [inverse, *parts], after)[0]


def absorb_kernel(ats, fresh, table_ref, acts_ref, *refs):
    count = len(ats)
    values, refs = refs[:count], refs[count:]
    if not fresh:
        sums_ref, refs = refs[0], refs[2:]
    out_ref, dict_ref = refs[:2]
    buffers, in_sem, out_sem = refs[2 : 2 + count], refs[2 + count], refs[3 + count]
    tokens = acts_ref.shape[0]
    ins, outs = [], []
    for k, value in enumerate(values):
        row = pl.multiple_of(table_ref[ats[k]] * TILE, TILE)
        rows = value.shape[0]
        ins.append(pltpu.make_async_copy(acts_ref.at[:, pl.ds(row, rows)], buffers[k], in_sem.at[k]))
        outs.append(pltpu.make_async_copy(value, dict_ref.at[pl.ds(row, rows), :], out_sem.at[k]))
        ins[k].start()
        outs[k].start()
    proj, gram = (0.0, 0.0) if fresh else (sums_ref[:tokens, :], sums_ref[tokens:, :])
    for k, value in enumerate(values):
        block = value[...]
        high = block.astype(bf16)
        low = (block - high.astype(f32)).astype(bf16)
        turned = high.T
        cross = dot(turned, low)
        gram = gram + (dot(turned, high) + (cross + cross.T))
        ins[k].wait()
        proj = proj + dot(buffers[k][...], high)
    out_ref[:tokens, :] = proj
    out_ref[tokens:, :] = gram
    for copy in outs:
        copy.wait()


def absorb(table, state, acts, blocks):
    tokens, hidden = acts.shape
    comp = blocks[0][0].shape[1]
    count = len(blocks)
    values = [value for value, _ in blocks]
    held = [] if state is None else list(state)
    total = sum(value.shape[0] for value in values)
    return pl.pallas_call(
        functools.partial(absorb_kernel, [at for _, at in blocks], state is None),
        out_shape=[shape(tokens + comp, comp), shape(hidden, comp)],
        in_specs=[SCALARS, ANYWHERE] + [WHOLE] * count + ([WHOLE, ANYWHERE] if held else []),
        out_specs=[WHOLE, ANYWHERE],
        scratch_shapes=[pltpu.VMEM((tokens, value.shape[0]), bf16) for value in values]
        + [pltpu.SemaphoreType.DMA((count,)), pltpu.SemaphoreType.DMA((count,))],
        input_output_aliases={2 + count: 0, 3 + count: 1} if held else {},
        compiler_params=LIMIT,
        cost_estimate=pl.CostEstimate(
            flops=2 * total * comp * (tokens + comp), bytes_accessed=total * (2 * tokens + 8 * comp), transcendentals=0
        ),
    )(table, acts, *values, *held)


def flips(bits):
    return [(t * 2 + c, (t ^ bits[c]) * 2 + c) for t in range(16) for c in range(2)]


X, Y, ZL, ZH = 1, 2, 4, 8
ALONG = {"first": (X, Y), "second": (Y, X), "near": (ZL, ZL), "far": (ZH, ZH)}
ORDERS = {
    "N": ("near", "first", "second", "far"),
    "B": ("first", "near", "second", "far"),
    "A": ("first", "second", "near", "far"),
}
SHARES = {"N": 5, "B": 5, "A": 4}
FIELDS = ("b", "c", "d", "mine", "theirs", "far_mine", "far_theirs")


def swap(value, along):
    return lax.ppermute(value, BOTH, flips(ALONG[along]))


def layout(hidden):
    unit = hidden // sum(SHARES.values())
    rows = {name: share * unit for name, share in SHARES.items()}
    table = np.zeros((32, 1 + len(FIELDS) * len(rows)), np.int32)
    where = {"core": 0}
    start, column = 0, 1
    for name, order in ORDERS.items():
        half, quarter = rows[name] // 2 // TILE, rows[name] // 4 // TILE
        for t in range(16):
            for core in range(2):
                a, b, c, d = (int(t & ALONG[along][core] != 0) for along in order)
                here, there = start + a * half, start + (1 - a) * half
                table[t * 2 + core, 0] = core
                table[t * 2 + core, column : column + len(FIELDS)] = (
                    b, c, d,
                    here + b * quarter, here + (1 - b) * quarter, there + b * quarter, there + (1 - b) * quarter,
                )
        for k, field in enumerate(FIELDS):
            where[name, field] = column + k
        start, column = start + 2 * half, column + len(FIELDS)
    return rows, table, where


def meshed(acts, dictionary, codes):
    hidden = acts.shape[1]
    tok, core = lax.axis_index("tok"), lax.axis_index("hid")
    rows, places, where = layout(hidden)
    table = lax.dynamic_slice_in_dim(jnp.asarray(places), tok * 2 + core, 1, 0).reshape(-1)

    def other_core(value):
        return lax.ppermute(value, "hid", [(0, 1), (1, 0)])

    sums = project(acts, dictionary)
    codes_mid, low, gram = first_update(table, codes, sums, other_core(sums))

    def bit(along):
        on_0, on_1 = ALONG[along]
        return jnp.where(core == 0, (tok & on_0) // on_0, (tok & on_1) // on_1)

    bits = {along: bit(along) for along in ALONG}
    starts, start = {}, 0
    for name in ORDERS:
        starts[name], start = start, start + rows[name]

    def cross_of(row, count):
        return dot(lax.dynamic_slice_in_dim(acts, row, count, 1), low, OVER_ROWS)

    def give_1(name):
        half = rows[name] // 2
        return cross_of(starts[name] + (1 - bits[ORDERS[name][0]]) * half, half)

    def own_2(name, keep):
        half, quarter = rows[name] // 2, rows[name] // 4
        a, b = (bits[along] for along in ORDERS[name][:2])
        return cross_of(starts[name] + a * half + (b if keep else 1 - b) * quarter, quarter)

    def part_of(value, which):
        half = value.shape[0] // 2
        return lax.dynamic_slice_in_dim(value, which * half, half, 0)

    def joined(one, other, which):
        return jnp.where(which == 0, jnp.concatenate([one, other]), jnp.concatenate([other, one]))

    held, last = {}, []
    first = {name: give_1(name) for name in ORDERS}
    first["A"] = stack(table, first["A"], gram, [first["N"]])
    for name, order in ORDERS.items():
        got = swap(first[name], order[0])
        tail = []
        if name == "A":
            gram = gram + got[rows[name] // 2 :]
            tail = [gram]
        give = take(table, where[name, "b"], own_2(name, False), got, tail, last)
        quarter = rows[name] // 4
        keep = own_2(name, True) + lax.dynamic_slice_in_dim(got, bits[order[1]] * quarter, quarter, 0)
        held[name], last = (keep, swap(give, order[1])), [give]
    for name, (keep, arrived) in held.items():
        along = ORDERS[name][2]
        if name == "A":
            give, keep = first_fold(table, where[name, "c"], keep, arrived, gram)
            held[name] = keep, swap(give, along)
        else:
            keep = keep + arrived
            held[name] = part_of(keep, bits[along]), swap(part_of(keep, 1 - bits[along]), along)
    for name, (keep, arrived) in held.items():
        along = ORDERS[name][3]
        if name == "A":
            give, keep, gram = split_fold(table, where[name, "d"], gram.shape[0], keep, arrived)
            gram = gram + swap(gram, along)
            held[name] = keep, swap(give, along)
        else:
            keep = keep + arrived
            held[name] = part_of(keep, bits[along]), swap(part_of(keep, 1 - bits[along]), along)

    inverse = factor_inverse(table, gram, other_core(gram), [held["N"][0], held["B"][0]])
    mine = {}
    for name in held:
        mine[name] = solve_sum(table, inverse, held[name], list(mine.values()))

    for k in (3, 2):
        for name in mine:
            along = ORDERS[name][k]
            mine[name] = joined(mine[name], swap(mine[name], along), bits[along])
    near, far, last = [], [], []
    for name in mine:
        theirs = swap(mine[name], ORDERS[name][1])
        near += [(mine[name], where[name, "mine"]), (theirs, where[name, "theirs"])]
        far += [(swap(mine[name], ORDERS[name][0]), where[name, "far_mine"])]
        last += [(swap(theirs, ORDERS[name][0]), where[name, "far_theirs"])]
    state = None
    for blocks in (near, far, [last[1], last[2]], [last[0]]):
        state = absorb(table, state, acts, blocks)
    sums, dict_out = state
    return second_update(codes_mid, sums, other_core(sums)), dict_out


def solution(mesh):
    tok, hid = mesh.shape["tok"], mesh.shape["hid"]

    def per_device(acts, dictionary, codes):
        if tok == 16 and hid == 2 and acts.shape[1] % (14 * 512) == 0:
            return meshed(acts, dictionary, codes)
        return plain(acts, dictionary, codes, acts.shape[1] % tok == 0)

    return jax.shard_map(
        per_device,
        mesh=mesh,
        in_specs=(P("tok", "hid"), P("hid", None), P("tok", None)),
        out_specs=(P("tok", None), P("hid", None)),
        check_vma=False,
    )
```
